32 devices in a mesh: dp: 16 (over z, y, core), vocab: 2 (over x).
Axes of the slice: x: 2, y: 2, z: 4, core: 2. Of those that a mesh axis runs over, the one named last changes fastest.
Arguments:
- src_tokens: int32 [32, 256], P('dp'), may hold values from 0 to 31999
- tgt_tokens: int32 [32, 256], P('dp'), may hold values from 0 to 31999
- src_segments: int32 [32, 256], P('dp'), may hold values from 0 to 7, never falling along the last dimension, each value on 1 to 96 neighbouring positions
- tgt_lengths: int32 [32, 8], P('dp'), may hold values from 1 to 96, 256 in all within a row
- mask_order: int32 [32, 256], P('dp'), may hold values from 0 to 255, each once within a row
- attn_project: float32 [3, 512, 1536], P(None, 'dp'), may hold values from -0.1875 to 0.1875
- attn_output: float32 [3, 512, 512], P(None, 'dp'), may hold values from -0.5 to 0.5
- ffn_expand: float32 [2, 512, 2048], P(None, 'dp'), may hold values from -0.25 to 0.25
- ffn_reduce: float32 [2, 2048, 512], P(None, 'dp'), may hold values from -0.125 to 0.125
- norm_gains: float32 [7, 512], P(None, 'dp')
- length_table: float32 [256, 512], P(None, 'dp'), may hold values from -1.5 to 1.5
- embedding: float32 [32000, 512], P(('vocab', 'dp'))
- momentum_attn_project: float32 [3, 512, 1536], P(None, 'dp'), may hold values from -2.2888184e-05 to 2.2888184e-05
- momentum_attn_output: float32 [3, 512, 512], P(None, 'dp'), may hold values from -2.2888184e-05 to 2.2888184e-05
- momentum_ffn_expand: float32 [2, 512, 2048], P(None, 'dp'), may hold values from -2.2888184e-05 to 2.2888184e-05
- momentum_ffn_reduce: float32 [2, 2048, 512], P(None, 'dp'), may hold values from -2.2888184e-05 to 2.2888184e-05
- momentum_norm_gains: float32 [7, 512], P(None, 'dp'), may hold values from -0.00024414062 to 0.00024414062
- momentum_length_table: float32 [256, 512], P(None, 'dp'), may hold values from -3.8146973e-06 to 3.8146973e-06
- momentum_embedding: float32 [32000, 512], P(('vocab', 'dp')), may hold values from -2.3841858e-06 to 2.3841858e-06
- average_attn_project: float32 [3, 512, 1536], P(None, 'dp'), may hold values from -0.1875 to 0.1875
- average_attn_output: float32 [3, 512, 512], P(None, 'dp'), may hold values from -0.5 to 0.5
- average_ffn_expand: float32 [2, 512, 2048], P(None, 'dp'), may hold values from -0.25 to 0.25
- average_ffn_reduce: float32 [2, 2048, 512], P(None, 'dp'), may hold values from -0.125 to 0.125
- average_norm_gains: float32 [7, 512], P(None, 'dp'), may hold values from 0.5 to 1.5
- average_length_table: float32 [256, 512], P(None, 'dp'), may hold values from -1.5 to 1.5
- average_embedding: float32 [32000, 512], P(('vocab', 'dp')), may hold values from -0.25 to 0.25
Outputs:
- loss_sum: float32 [], replicated
- grad_norm: float32 [], replicated
- new_attn_project: float32 [3, 512, 1536], P(None, 'dp')
- new_attn_output: float32 [3, 512, 512], P(None, 'dp')
- new_ffn_expand: float32 [2, 512, 2048], P(None, 'dp')
- new_ffn_reduce: float32 [2, 2048, 512], P(None, 'dp')
- new_norm_gains: float32 [7, 512], P(None, 'dp')
- new_length_table: float32 [256, 512], P(None, 'dp')
- new_embedding: float32 [32000, 512], P(('vocab', 'dp'))
- new_momentum_attn_project: float32 [3, 512, 1536], P(None, 'dp')
- new_momentum_attn_output: float32 [3, 512, 512], P(None, 'dp')
- new_momentum_ffn_expand: float32 [2, 512, 2048], P(None, 'dp')
- new_momentum_ffn_reduce: float32 [2, 2048, 512], P(None, 'dp')
- new_momentum_norm_gains: float32 [7, 512], P(None, 'dp')
- new_momentum_length_table: float32 [256, 512], P(None, 'dp')
- new_momentum_embedding: float32 [32000, 512], P(('vocab', 'dp'))
- new_average_attn_project: float32 [3, 512, 1536], P(None, 'dp')
- new_average_attn_output: float32 [3, 512, 512], P(None, 'dp')
- new_average_ffn_expand: float32 [2, 512, 2048], P(None, 'dp')
- new_average_ffn_reduce: float32 [2, 2048, 512], P(None, 'dp')
- new_average_norm_gains: float32 [7, 512], P(None, 'dp')
- new_average_length_table: float32 [256, 512], P(None, 'dp')
- new_average_embedding: float32 [32000, 512], P(('vocab', 'dp'))
- copy_attn_project: bfloat16 [3, 512, 1536], P(None, 'dp')
- copy_attn_output: bfloat16 [3, 512, 512], P(None, 'dp')
- copy_ffn_expand: bfloat16 [2, 512, 2048], P(None, 'dp')
- copy_ffn_reduce: bfloat16 [2, 2048, 512], P(None, 'dp')
- copy_norm_gains: bfloat16 [7, 512], P(None, 'dp')
- copy_length_table: bfloat16 [256, 512], P(None, 'dp')
- copy_embedding: bfloat16 [32000, 512], P(('vocab', 'dp'))
The draws below stay inside these ranges and needn't reach their ends.
Inputs may be any that keep to these rules, and one draw needn't show every extreme that they name: `src_segments`: segment numbers never fall along a row; each of the 8 sentences has 1 to 96 source tokens, one exactly 96. `tgt_lengths`: A row's 8 lengths sum to 256; the largest is 96. `mask_order`: each row is a permutation of the 256 target positions.
All inputs are finite; a program needn't handle non-finite values.
Results may differ from the reference program's by a relative error of at most 0.012.
The reference program's roundings to bfloat16 on the way count: a program that leaves them out, or rounds other values in their place, can miss the bound.
Values may be sent and summed in bfloat16 or wider, within the bound.
No kernel may reach another device: no remote copies, remote signals or barrier semaphores. Data moves between devices by JAX's collectives and lax.ppermute only.
A program may use at most 384 MiB of HBM per device.

```python
import math
import jax
import jax.numpy as jnp
import numpy as np
from jax import lax

D = 512
HEADS = 8
HDIM = 64
FF = 2048
V = 32000
LCLS = 256
NORMS = 7
ATTNS = 3
FFNS = 2
ROW = 256
SENTS = 8
MOST = 96
MASKED = 96
BATCH = 32
COUNT = 256
NPARAM = 23858688


def draw_norm_gains(key, part):
    key = jax.random.fold_in(key, 11)
    ramp = 1.0 + 2.0 * jnp.arange(D, dtype=jnp.float32)[None, :] / D
    noise = jnp.exp(0.15 * jax.random.normal(key, (NORMS, D), jnp.float32))
    return ramp * noise


def draw_embedding(key, part):
    key = jax.random.fold_in(key, 23)
    place = jnp.arange(V, dtype=jnp.float32)[:, None] / V
    base = jax.random.normal(key, (V, D), jnp.float32)
    ramp = 1.0 + 2.0 * place
    return ramp * base / (2.5 * D ** 0.5)


def set_ends(array, key, least, high):
    dims = array.shape
    spot = [jax.random.randint(jax.random.fold_in(key, axis), (), 0, dims[axis]) for axis in range(len(dims))]
    array = array.at[tuple(spot)].set(least)
    longest = dims.index(max(dims))
    spot[longest] = (spot[longest] + 1) % dims[longest]
    return array.at[tuple(spot)].set(high)


def levels(key, dims, split, smallest, high):
    def one(axis_at, shards_of):
        heights = jax.random.uniform(jax.random.fold_in(jax.random.fold_in(key, 6), axis_at), (shards_of,), jnp.float32, smallest / len(split), high / len(split))
        return jnp.repeat(jnp.exp(heights), dims[axis_at] // shards_of).reshape((-1,) + (1,) * (len(dims) - axis_at - 1))

    factor_of = one(*split[0])
    for cut in split[1:]:
        factor_of = factor_of * one(*cut)
    return factor_of


def cumulative_ranks(count, skew):
    weights = [(1 << 20) // math.isqrt(standing ** skew) + 1 for standing in range(1, count + 1)]
    scale = 1 + sum(weights) // (1 << 30)
    return np.cumsum(np.array([max(1, weight // scale) for weight in weights]))


def ranked(own_key, extent, count, skew):
    grid = cumulative_ranks(count, skew)
    pick = jax.random.randint(jax.random.fold_in(own_key, 1), extent, 0, int(grid[count - 1]))
    standing = jnp.searchsorted(jnp.asarray(grid, jnp.int32), pick, side="right")
    return jax.random.permutation(jax.random.fold_in(own_key, 2), count)[standing].astype(jnp.int32)


def split_up(number_of, total, bound, slope):
    loads = [(1 << 20) // math.isqrt(grade ** slope) + 1 for grade in range(2, number_of + 1)]
    surplus, holding = total - bound - (number_of - 1), [1] * (number_of - 1)
    while surplus > 0:
        movable = [i for i in range(number_of - 1) if holding[i] < bound]
        whole, budget = sum([loads[i] for i in movable]), surplus
        for i in movable:
            extra = min(bound - holding[i], max(1, budget * loads[i] // whole), surplus)
            holding[i] = holding[i] + extra
            surplus = surplus - extra
    return np.array([bound] + holding)


def uneven(key, count, total, reach, skew):
    if count == 2:
        one = jax.random.randint(key, (), max(1, total - reach), min(reach, total - 1) + 1)
        return jnp.stack([one, total - one])
    sizes = jnp.asarray(split_up(count, total, reach, skew), jnp.int32)
    twos = (count - 1) // 2
    giver, sink = sizes[1:1 + 2 * twos:2], sizes[2:2 + 2 * twos:2]
    margin = jnp.minimum(giver - 1, reach - sink)
    passed = jax.random.randint(jax.random.fold_in(key, 1), (twos,), 0, 1 << 20) % (margin + 1)
    sizes = sizes.at[1:1 + 2 * twos:2].set(giver - passed).at[2:2 + 2 * twos:2].set(sink + passed)
    return sizes[jax.random.permutation(jax.random.fold_in(key, 2), count)]


def bell_draw(stream_key, dims, scale, limit, shards=(), held_as=jnp.bfloat16):
    level = levels(stream_key, dims, shards, -0.22, 0.18) if shards else 1.0
    array = jax.random.normal(stream_key, dims, jnp.float32) * scale * level
    return jnp.minimum(jnp.maximum(array, -limit), limit).astype(held_as)


def setup_inputs(seed: int = 0) -> dict:
    key_list = jax.random.split(jax.random.key(seed), 27)
    return {
        "src_tokens": set_ends(ranked(key_list[0], (BATCH, ROW), V, 2), jax.random.fold_in(key_list[0], 3), 0, V - 1).astype(jnp.int32),
        "tgt_tokens": set_ends(ranked(key_list[1], (BATCH, ROW), V, 2), jax.random.fold_in(key_list[1], 3), 0, V - 1).astype(jnp.int32),
        "src_segments": jax.vmap(lambda own: jnp.searchsorted(jnp.cumsum(uneven(own, SENTS, ROW, MOST, 2)), jnp.arange(ROW), side="right"))(jax.random.split(key_list[2], BATCH)).reshape((BATCH, ROW)).astype(jnp.int32),
        "tgt_lengths": jax.vmap(lambda own: uneven(own, SENTS, ROW, MOST, 2))(jax.random.split(key_list[3], BATCH)).reshape((BATCH, SENTS)).astype(jnp.int32),
        "mask_order": jax.vmap(lambda own: jax.random.permutation(own, ROW))(jax.random.split(key_list[4], BATCH)).reshape((BATCH, ROW)).astype(jnp.int32),
        "attn_project": bell_draw(key_list[5], (ATTNS, D, 3 * D), (2 * D) ** -0.5, 0.1875, ((1, 16),), jnp.float32),
        "attn_output": bell_draw(key_list[6], (ATTNS, D, D), (D // 4) ** -0.5, 0.5, ((1, 16),), jnp.float32),
        "ffn_expand": bell_draw(key_list[7], (FFNS, D, FF), D ** -0.5, 0.25, ((1, 16),), jnp.float32),
        "ffn_reduce": bell_draw(key_list[8], (FFNS, FF, D), FF ** -0.5, 0.125, ((1, 16),), jnp.float32),
        "norm_gains": draw_norm_gains(jax.random.fold_in(key_list[26], 71), 0),
        "length_table": bell_draw(key_list[10], (LCLS, D), (D // 32) ** -0.5, 1.5, ((1, 16),), jnp.float32),
        "embedding": draw_embedding(jax.random.fold_in(key_list[26], 71), 0),
        "momentum_attn_project": bell_draw(key_list[12], (ATTNS, D, 3 * D), (0.02 / NPARAM ** 0.5), 2.288818359375e-05, ((1, 16),), jnp.float32),
        "momentum_attn_output": bell_draw(key_list[13], (ATTNS, D, D), (0.02 / NPARAM ** 0.5), 2.288818359375e-05, ((1, 16),), jnp.float32),
        "momentum_ffn_expand": bell_draw(key_list[14], (FFNS, D, FF), (0.02 / NPARAM ** 0.5), 2.288818359375e-05, ((1, 16),), jnp.float32),
        "momentum_ffn_reduce": bell_draw(key_list[15], (FFNS, FF, D), (0.02 / NPARAM ** 0.5), 2.288818359375e-05, ((1, 16),), jnp.float32),
        "momentum_norm_gains": bell_draw(key_list[16], (NORMS, D), (0.2 / NPARAM ** 0.5), 0.00024414062, ((1, 16),), jnp.float32),
        "momentum_length_table": bell_draw(key_list[17], (LCLS, D), (0.003 / NPARAM ** 0.5), 3.814697265625e-06, ((1, 16),), jnp.float32),
        "momentum_embedding": bell_draw(key_list[18], (V, D), (0.002 / NPARAM ** 0.5), 2.384185791015625e-06, ((0, 32),), jnp.float32),
        "average_attn_project": bell_draw(key_list[19], (ATTNS, D, 3 * D), (2 * D) ** -0.5, 0.1875, ((1, 16),), jnp.float32),
        "average_attn_output": bell_draw(key_list[20], (ATTNS, D, D), (D // 4) ** -0.5, 0.5, ((1, 16),), jnp.float32),
        "average_ffn_expand": bell_draw(key_list[21], (FFNS, D, FF), D ** -0.5, 0.25, ((1, 16),), jnp.float32),
        "average_ffn_reduce": bell_draw(key_list[22], (FFNS, FF, D), FF ** -0.5, 0.125, ((1, 16),), jnp.float32),
        "average_norm_gains": jnp.clip(1.0 + 0.1 * jax.random.normal(key_list[23], (NORMS, D), jnp.float32), 0.5, 1.5),
        "average_length_table": bell_draw(key_list[24], (LCLS, D), (D // 32) ** -0.5, 1.5, ((1, 16),), jnp.float32),
        "average_embedding": bell_draw(key_list[25], (V, D), D ** -0.5, 0.25, ((0, 32),), jnp.float32),
    }


HIGHEST = lax.Precision.HIGHEST
EPSILON = 1e-05
MASK_TOKEN = 3
MOMENTUM = 0.9
KEEP = 0.9
CLIP = 0.02
LENGTH_WEIGHT = 0.1
NEGATIVE = -1e+30
RATE_SCALE = 0.25
RATE_FACTORS = (1.0, 1.0, 1.0, 1.0, 6.0, 24.0, 1.0)

@jax.custom_vjp
def low(v):
    return lax.optimization_barrier(v.astype(jnp.bfloat16)).astype(jnp.float32)

@jax.custom_vjp
def low_back(v):
    return v

def low_keep(v):
    return (low(v), None)

def low_pass(kept, grad):
    return (grad,)

def back_keep(v):
    return (v, None)

def back_low(kept, grad):
    return (low(grad),)
low.defvjp(low_keep, low_pass)
low_back.defvjp(back_keep, back_low)

def matmul(left, right):
    return jnp.dot(left, right, precision=HIGHEST)

def layer_norm(stream, gain):
    centred = stream - lax.optimization_barrier(jnp.mean(stream, axis=-1, keepdims=True))
    spread = lax.optimization_barrier(jnp.mean(centred * centred, axis=-1, keepdims=True))
    return centred * lax.rsqrt(spread + EPSILON) * gain

def sinusoid(count, width):
    place = jnp.arange(count, dtype=jnp.float32)[:, None]
    index = jnp.arange(width // 2, dtype=jnp.float32)[None, :]
    angle = place * jnp.exp(-math.log(10000.0) * 2.0 * index / width)
    return jnp.concatenate([jnp.sin(angle), jnp.cos(angle)], axis=1)

def attend(a_query, a_memory, w_in, w_out, allowed):
    count = a_query.shape[0]
    query = low(low_back(matmul(low(a_query), w_in[:, :D]))).reshape(count, HEADS, HDIM)
    memory = low(low_back(matmul(low(a_memory), w_in[:, D:])))
    keys = memory[:, :D].reshape(-1, HEADS, HDIM)
    values = memory[:, D:].reshape(-1, HEADS, HDIM)
    scores = low_back(jnp.einsum('qhd,khd->hqk', query, keys, precision=HIGHEST) * HDIM ** (-0.5))
    scores = jnp.where(allowed[None], scores, NEGATIVE)
    probs = jax.nn.softmax(scores, axis=-1)
    mixed = jnp.einsum('hqk,khd->qhd', low(probs), values, precision=HIGHEST).reshape(count, D)
    return low_back(matmul(low(low_back(mixed)), w_out))

def feed_forward(normed, w_up, w_down):
    hidden = low_back(matmul(low(normed), w_up))
    return low_back(matmul(low(jax.nn.gelu(hidden)), w_down))

def row_loss(weights, row):
    w_in, w_out, w_up, w_down, gain, table, embed = weights
    source, target, segments, lengths, order = row
    position = sinusoid(ROW, D)
    places = jnp.arange(ROW, dtype=jnp.int32)
    masked = order[:MASKED].astype(jnp.int32)
    flag = jnp.any(places[:, None] == masked[None, :], axis=1)
    dec_in = jnp.where(flag, MASK_TOKEN, target).astype(jnp.int32)
    bounds = jnp.cumsum(lengths).astype(jnp.int32)
    tsegs = lax.optimization_barrier(jnp.sum((places[:, None] >= bounds[None, :]).astype(jnp.int32), axis=1)).astype(jnp.int32)
    src_allowed = segments[:, None] == segments[None, :]
    tgt_allowed = tsegs[:, None] == tsegs[None, :]
    cross_allowed = tsegs[:, None] == segments[None, :]
    stream = math.sqrt(D) * low_back(embed[source]) + position
    normed = layer_norm(stream, gain[0])
    stream = stream + attend(normed, normed, w_in[0], w_out[0], src_allowed)
    stream = stream + feed_forward(layer_norm(stream, gain[1]), w_up[0], w_down[0])
    enc = layer_norm(stream, gain[2])
    decoded = math.sqrt(D) * low_back(embed[dec_in]) + position
    normed = layer_norm(decoded, gain[3])
    decoded = decoded + attend(normed, normed, w_in[1], w_out[1], tgt_allowed)
    decoded = decoded + attend(layer_norm(decoded, gain[4]), enc, w_in[2], w_out[2], cross_allowed)
    decoded = decoded + feed_forward(layer_norm(decoded, gain[5]), w_up[1], w_down[1])
    top = layer_norm(decoded, gain[6])[masked]
    logits = low_back(matmul(low(top), embed.T))
    picked = jnp.take_along_axis(logits, target[masked][:, None], axis=1)[:, 0]
    token_loss = jax.nn.logsumexp(logits, axis=1) - picked
    member = (segments[None, :] == jnp.arange(SENTS, dtype=jnp.int32)[:, None]).astype(jnp.float32)
    pooled = matmul(member, enc) / lax.optimization_barrier(jnp.sum(member, axis=1, keepdims=True))
    length_logits = low_back(matmul(low(pooled), table.T))
    classes = (lengths - 1).astype(jnp.int32)
    length_pick = jnp.take_along_axis(length_logits, classes[:, None], axis=1)[:, 0]
    length_loss = jax.nn.logsumexp(length_logits, axis=1) - length_pick
    return jnp.sum(token_loss) + LENGTH_WEIGHT * jnp.sum(length_loss)

def reference(src_tokens, tgt_tokens, src_segments, tgt_lengths, mask_order, attn_project, attn_output, ffn_expand, ffn_reduce, norm_gains, length_table, embedding, momentum_attn_project, momentum_attn_output, momentum_ffn_expand, momentum_ffn_reduce, momentum_norm_gains, momentum_length_table, momentum_embedding, average_attn_project, average_attn_output, average_ffn_expand, average_ffn_reduce, average_norm_gains, average_length_table, average_embedding):
    params = (attn_project, attn_output, ffn_expand, ffn_reduce, norm_gains, length_table, embedding)
    moments = (momentum_attn_project, momentum_attn_output, momentum_ffn_expand, momentum_ffn_reduce, momentum_norm_gains, momentum_length_table, momentum_embedding)
    averages = (average_attn_project, average_attn_output, average_ffn_expand, average_ffn_reduce, average_norm_gains, average_length_table, average_embedding)
    rows = (src_tokens, tgt_tokens, src_segments, tgt_lengths, mask_order)
    step = jax.checkpoint(row_loss)

    def total(weights_in):
        weights = tuple((low(w) for w in weights_in))

        def accumulate(carry, row):
            return (carry + step(weights, row), None)
        summed, _ = lax.scan(accumulate, jnp.zeros((), jnp.float32), rows)
        return summed
    loss_sum, back = jax.vjp(total, params)
    grads, = back(jnp.ones_like(loss_sum) / COUNT)
    squares = jnp.zeros((), jnp.float32)
    for grad in grads:
        squares = squares + jnp.sum(grad * grad)
    grad_norm = jnp.sqrt(squares)
    factor = jnp.minimum(1.0, CLIP / grad_norm)
    rate = RATE_SCALE * math.sqrt(NPARAM / D) / CLIP
    fresh, moved, smooth, copies = ([], [], [], [])
    for weight, grad, moment, average, boost in zip(params, grads, moments, averages, RATE_FACTORS):
        clipped = grad * factor
        moment = MOMENTUM * moment + clipped
        weight = weight - boost * rate * (clipped + MOMENTUM * moment)
        average = KEEP * average + (1.0 - KEEP) * weight
        fresh.append(weight)
        moved.append(moment)
        smooth.append(average)
        copies.append(weight.astype(jnp.bfloat16))
    return (loss_sum, grad_norm, fresh[0], fresh[1], fresh[2], fresh[3], fresh[4], fresh[5], fresh[6], moved[0], moved[1], moved[2], moved[3], moved[4], moved[5], moved[6], smooth[0], smooth[1], smooth[2], smooth[3], smooth[4], smooth[5], smooth[6], copies[0], copies[1], copies[2], copies[3], copies[4], copies[5], copies[6])
```

```python
import math

import jax
import jax.numpy as jnp
from jax import lax
from jax.sharding import Mesh
from jax.sharding import PartitionSpec as P

D = 512
HDIM = 64
LCLS = 256
ROW = 256
SENTS = 8
MASKED = 96
NPARAM = 23858688


HIGHEST = lax.Precision.HIGHEST
EPSILON = 1e-05
MASK_TOKEN = 3
MOMENTUM = 0.9
KEEP = 0.9
CLIP = 0.02
LENGTH_WEIGHT = 0.1
NEGATIVE = -1e30
RATE_SCALE = 0.25
RATE_FACTORS = (1.0, 1.0, 1.0, 1.0, 6.0, 24.0, 1.0)


def layer_norm(stream, gain):
    centred = stream - jnp.mean(stream, axis=-1, keepdims=True)
    spread = jnp.mean(centred * centred, axis=-1, keepdims=True)
    return centred * lax.rsqrt(spread + EPSILON) * gain


def sinusoid(count, width):
    place = jnp.arange(count, dtype=jnp.float32)[:, None]
    index = jnp.arange(width // 2, dtype=jnp.float32)[None, :]
    angle = place * jnp.exp(-math.log(10000.0) * 2.0 * index / width)
    return jnp.concatenate([jnp.sin(angle), jnp.cos(angle)], axis=1)


SWAP = [(0, 1), (1, 0)]


def swap(value, axis):
    return lax.ppermute(value, axis, SWAP)


def shift(value, by):
    count = lax.axis_size("z")
    return lax.ppermute(value, "z", [(i, (i + by) % count) for i in range(count)])


def low(value):
    return value.astype(jnp.bfloat16)


def wide(value):
    return value.astype(jnp.float32)


def ring_gather(value):
    count = lax.axis_size("z")
    if count != 4:
        whole = lax.all_gather(value, "z", axis=0)
        here = lax.axis_index("z")
        return [
            lax.dynamic_index_in_dim(whole, (here - k) % count, 0, False) for k in range(count)
        ]
    half = value.shape[0] // 2
    below = shift(value, 1)
    above = shift(value, -1)
    far = jnp.concatenate([shift(below[:half], 1), shift(above[half:], -1)], axis=0)
    return [value, below, far, above]


def ring_scatter(blocks):
    count = lax.axis_size("z")
    if count != 4:
        here = lax.axis_index("z")
        order = (here - jnp.arange(count)) % count
        stacked = jnp.stack([low(block) for block in blocks])
        whole = jnp.zeros_like(stacked).at[order].set(stacked)
        return wide(lax.psum_scatter(whole, "z", scatter_dimension=0))
    half = blocks[0].shape[0] // 2
    from_above = shift(low(blocks[2][:half]), -1)
    from_below = shift(low(blocks[2][half:]), 1)
    down = jnp.concatenate([wide(blocks[1][:half]) + wide(from_above), wide(blocks[1][half:])])
    up = jnp.concatenate([wide(blocks[3][:half]), wide(blocks[3][half:]) + wide(from_below)])
    from_above = shift(low(down), -1)
    from_below = shift(low(up), 1)
    return wide(blocks[0]) + wide(from_above) + wide(from_below)


def gather_weight(value):
    blocks, rows, columns = value.shape
    count = lax.axis_size("z")
    here, side, core = (lax.axis_index("z"), lax.axis_index("y"), lax.axis_index("core"))
    mine = jnp.stack(ring_gather(value))
    both = jnp.stack([mine, swap(mine, "y")])
    rest = swap(both, "core")
    whole = jnp.zeros((blocks, count, 2, 2, rows, columns), value.dtype)
    for held, at_core in ((both, core), (rest, 1 - core)):
        for j, at_side in ((0, side), (1, 1 - side)):
            for k in range(count):
                whole = lax.dynamic_update_slice(
                    whole,
                    held[j, k][:, None, None, None],
                    (0, (here - k) % count, at_side, at_core, 0, 0),
                )
    return whole.reshape(blocks, count * 4 * rows, columns)


def scatter_weight(grad):
    count = lax.axis_size("z")
    here, side, core = (lax.axis_index("z"), lax.axis_index("y"), lax.axis_index("core"))
    blocks, height, columns = grad.shape
    rows = height // (count * 4)
    parts = grad.reshape(blocks, count, 2, 2, rows, columns)
    mine = lax.dynamic_index_in_dim(parts, core, 3, False)
    theirs = lax.dynamic_index_in_dim(parts, 1 - core, 3, False)
    chip = wide(mine) + wide(swap(low(theirs), "core"))
    mine = lax.dynamic_index_in_dim(chip, side, 2, False)
    theirs = lax.dynamic_index_in_dim(chip, 1 - side, 2, False)
    pair = low(mine + wide(swap(low(theirs), "y")))
    line = ring_scatter(
        [lax.dynamic_index_in_dim(pair, (here - k) % count, 1, False) for k in range(count)]
    )
    half = low(line)
    return wide(half) + wide(swap(half, "vocab"))


def gather_group(value):
    pair = jnp.stack([value, swap(value, "vocab")])
    return jnp.stack(ring_gather(pair))


def scatter_group(parts):
    held = parts[:, 0] + swap(low(parts[:, 1]), "vocab")
    return ring_scatter([held[k] for k in range(parts.shape[0])])


def butterfly(value, join, axes):
    for axis in axes:
        count = lax.axis_size(axis)
        step = 1
        while step < count:
            pairs = [(i, i ^ step) for i in range(count)]
            value = join(value, lax.ppermute(value, axis, pairs))
            step *= 2
    return value


def join_totals(left, right):
    peak = jnp.maximum(left[0], right[0])
    return jnp.stack(
        [peak, left[1] * jnp.exp(left[0] - peak) + right[1] * jnp.exp(right[0] - peak)]
    )


def turn(value):
    count = lax.axis_size("z")
    here, half = (lax.axis_index("z"), lax.axis_index("vocab"))
    value = jnp.where(half == 0, value, value[:, ::-1])
    backward = value[::-1]
    twice = jnp.concatenate([backward, backward])
    return lax.dynamic_slice_in_dim(twice, count - 1 - here, count, 0)


def heads_of(value):
    return value.reshape(value.shape[0], -1, HDIM)


def dot(left, right):
    return jnp.dot(left, right, preferred_element_type=jnp.float32)


def dot_left(left, right):
    return jnp.einsum("rd,re->de", left, right, preferred_element_type=jnp.float32)


def dot_right(left, right):
    return jnp.einsum("re,de->rd", left, right, preferred_element_type=jnp.float32)


def attend_fwd(a_query, a_memory, w, allowed):
    count, width = a_query.shape
    low_query = low(a_query)
    low_memory = low(a_memory)
    query = heads_of(low(dot(low_query, w[0])))
    keys = heads_of(low(dot(low_memory, w[1])))
    values = heads_of(low(dot(low_memory, w[2])))
    scores = jnp.einsum("qhd,khd->hqk", query, keys, preferred_element_type=jnp.float32) * HDIM ** (
        -0.5
    )
    scores = jnp.where(allowed[None], scores, NEGATIVE)
    expo = jnp.exp(scores - jnp.max(scores, axis=-1, keepdims=True))
    probs = expo / jnp.sum(expo, axis=-1, keepdims=True)
    low_probs = low(probs)
    mixed = low(
        jnp.einsum("hqk,khd->qhd", low_probs, values, preferred_element_type=jnp.float32)
    ).reshape(count, width)
    branch = dot(mixed, w[3])
    return (branch, (low_query, low_memory, query, keys, values, probs, low_probs, mixed))


def attend_bwd(grad_out, cache, w):
    low_query, low_memory, query, keys, values, probs, low_probs, mixed = cache
    count, width = mixed.shape
    scale = HDIM ** (-0.5)
    grad_low = low(grad_out)
    grad_wout = dot_left(mixed, grad_low)
    grad_mixed = heads_of(low(dot_right(grad_low, w[3])))
    grad_probs = jnp.einsum("qhd,khd->hqk", grad_mixed, values, preferred_element_type=jnp.float32)
    grad_scores = low(probs * (grad_probs - jnp.sum(probs * grad_probs, axis=-1, keepdims=True)))
    grad_query = low(
        jnp.einsum("hqk,khd->qhd", grad_scores, keys, preferred_element_type=jnp.float32) * scale
    ).reshape(count, width)
    grad_keys = low(
        jnp.einsum("hqk,qhd->khd", grad_scores, query, preferred_element_type=jnp.float32) * scale
    ).reshape(-1, width)
    grad_values = low(
        jnp.einsum("hqk,qhd->khd", low_probs, grad_mixed, preferred_element_type=jnp.float32)
    ).reshape(-1, width)
    grads = jnp.stack(
        [
            dot_left(low_query, grad_query),
            dot_left(low_memory, grad_keys),
            dot_left(low_memory, grad_values),
            grad_wout,
        ]
    )
    grad_aq = dot_right(grad_query, w[0])
    grad_am = dot_right(grad_keys, w[1]) + dot_right(grad_values, w[2])
    return (grad_aq, grad_am, grads)


def ffn_fwd(normed, w):
    low_normed = low(normed)
    hidden = [dot(low_normed, w[j]) for j in range(4)]
    active = [low(jax.nn.gelu(part)) for part in hidden]
    branch = sum(dot(active[j], w[4 + j]) for j in range(4))
    return (branch, (low_normed, hidden, active))


def ffn_bwd(grad_out, cache, w):
    low_normed, hidden, active = cache
    grad_low = low(grad_out)
    grad_down = [dot_left(part, grad_low) for part in active]
    grad_hidden = []
    for j in range(4):
        _, gelu_back = jax.vjp(jax.nn.gelu, hidden[j])
        grad_hidden.append(low(gelu_back(dot_right(grad_low, w[4 + j]))[0]))
    grad_up = [dot_left(low_normed, part) for part in grad_hidden]
    grad_normed = sum(dot_right(grad_hidden[j], w[j]) for j in range(4))
    return (grad_normed, jnp.stack(grad_up + grad_down))


def layer_fwd(stream, weights, depth, allowed, memory, cross_allowed):
    w_attn, w_ffn, gain = weights
    base = 3 * depth
    records = []
    normed, norm_back = jax.vjp(layer_norm, stream, gain[base])
    branch, cache = attend_fwd(normed, normed, w_attn[depth], allowed)
    records.append((norm_back, cache))
    stream = stream + branch
    if memory is not None:
        base = base + 1
        normed, norm_back = jax.vjp(layer_norm, stream, gain[base])
        branch, cache = attend_fwd(normed, memory, w_attn[2], cross_allowed)
        records.append((norm_back, cache))
        stream = stream + branch
    normed, norm_back = jax.vjp(layer_norm, stream, gain[base + 1])
    branch, cache = ffn_fwd(normed, w_ffn[depth])
    records.append((norm_back, cache))
    stream = stream + branch
    top, final_back = jax.vjp(layer_norm, stream, gain[base + 2])
    return (top, (records, final_back))


def layer_bwd(grad_top, kept, weights, depth):
    w_attn, w_ffn, gain = weights
    records, final_back = kept
    grad_stream, final_gain = final_back(grad_top)
    ffn_back, ffn_cache = records[-1]
    grad_normed, ffn_grads = ffn_bwd(grad_stream, ffn_cache, w_ffn[depth])
    extra, ffn_gain = ffn_back(grad_normed)
    grad_stream = grad_stream + extra
    gain_grads = [ffn_gain, final_gain]
    attn_grads = {}
    memory_grad = None
    for place in range(len(records) - 2, -1, -1):
        attn_back, attn_cache = records[place]
        index = depth if place == 0 else 2
        grad_aq, grad_am, attn_grads[index] = attend_bwd(grad_stream, attn_cache, w_attn[index])
        if place == 0:
            grad_aq = grad_aq + grad_am
        else:
            memory_grad = grad_am
        extra, attn_gain = attn_back(grad_aq)
        grad_stream = grad_stream + extra
        gain_grads.insert(0, attn_gain)
    return (grad_stream, memory_grad, gain_grads, attn_grads, ffn_grads)


def pack_attn(project, output):
    width = output.shape[1]
    return jnp.stack([project[:, j * width : (j + 1) * width] for j in range(3)] + [output])


def pack_ffn(expand, reduce):
    rows, width = (expand.shape[0], reduce.shape[1])
    up = expand.reshape(rows, width // rows, 4, rows).transpose(2, 0, 1, 3)
    return jnp.concatenate([up.reshape(4, rows, width), reduce.reshape(4, rows, width)])


def unpack_attn(pack):
    return (jnp.concatenate([pack[0], pack[1], pack[2]], axis=1), pack[3])


def unpack_ffn(pack):
    rows, width = pack.shape[1:]
    up = pack[:4].reshape(4, rows, width // rows, rows).transpose(1, 2, 0, 3)
    return (up.reshape(rows, 4 * width), pack[4:].reshape(4 * rows, width))


def shards(
    src_tokens,
    tgt_tokens,
    src_segments,
    tgt_lengths,
    mask_order,
    attn_project,
    attn_output,
    ffn_expand,
    ffn_reduce,
    norm_gains,
    length_table,
    embedding,
    momentum_attn_project,
    momentum_attn_output,
    momentum_ffn_expand,
    momentum_ffn_reduce,
    momentum_norm_gains,
    momentum_length_table,
    momentum_embedding,
    average_attn_project,
    average_attn_output,
    average_ffn_expand,
    average_ffn_reduce,
    average_norm_gains,
    average_length_table,
    average_embedding,
):
    masters = (
        attn_project,
        attn_output,
        ffn_expand,
        ffn_reduce,
        norm_gains,
        length_table,
        embedding,
    )
    moments = (
        momentum_attn_project,
        momentum_attn_output,
        momentum_ffn_expand,
        momentum_ffn_reduce,
        momentum_norm_gains,
        momentum_length_table,
        momentum_embedding,
    )
    averages = (
        average_attn_project,
        average_attn_output,
        average_ffn_expand,
        average_ffn_reduce,
        average_norm_gains,
        average_length_table,
        average_embedding,
    )
    count_z = lax.axis_size("z")
    here, side, core, half = (
        lax.axis_index("z"),
        lax.axis_index("y"),
        lax.axis_index("core"),
        lax.axis_index("vocab"),
    )
    rows_here = src_tokens.shape[0]
    count_dp = count_z * 4
    inverse = 1.0 / (SENTS * rows_here * count_dp)
    source, target, segments, lengths, order = (
        lax.dynamic_index_in_dim(array, half, 0, False)
        for array in (src_tokens, tgt_tokens, src_segments, tgt_lengths, mask_order)
    )
    shuffled = target[order]
    bounds = jnp.cumsum(lengths)
    tsegs = jnp.sum((order[:, None] >= bounds[None, :]).astype(jnp.int32), axis=1)
    src_allowed = segments[:, None] == segments[None, :]
    tgt_allowed = tsegs[:, None] == tsegs[None, :]
    cross_allowed = tsegs[:, None] == segments[None, :]
    position = sinusoid(ROW, D)
    dec_position = position[order]

    own_rows = low(embedding)
    shard = own_rows.shape[0]
    far_rows = swap(own_rows, "y")
    near = jnp.concatenate([own_rows, swap(own_rows, "core")])
    away = jnp.concatenate([far_rows, swap(far_rows, "core")])
    first = half * count_dp + here * 4
    ids = jnp.arange(shard, dtype=jnp.int32)
    block_ids = jnp.concatenate(
        [
            ids + (first + at_side * 2 + at_core) * shard
            for at_side in (side, 1 - side)
            for at_core in (core, 1 - core)
        ]
    )
    near_ids, away_ids = (block_ids[: 2 * shard], block_ids[2 * shard :])
    block_rows = jnp.concatenate([near, away])

    few = ROW - MASKED + 16
    extra = jnp.where(jnp.arange(16) == 0, MASK_TOKEN, -1).astype(jnp.int32)
    numbers = gather_group(jnp.concatenate([source, shuffled, extra]))
    numbers = numbers.reshape(count_z * 2, 2 * ROW + 16)
    src_ids = numbers[:, :ROW].reshape(-1)
    goal_ids = numbers[:, ROW : ROW + MASKED].reshape(-1)
    dec_ids = numbers[:, ROW + MASKED :].reshape(-1)

    def look_up(tokens):
        near_hot = low(tokens[:, None] == near_ids[None, :])
        away_hot = low(tokens[:, None] == away_ids[None, :])
        rows = low(dot(near_hot, near) + dot(away_hot, away))
        return scatter_group(rows.reshape(count_z, 2, -1, D))

    blanks = jnp.zeros((1, length_table.shape[1], D - LCLS - 7), jnp.bfloat16)
    misc = jnp.concatenate([low(length_table).T[None], low(norm_gains).T[None], blanks], axis=2)
    enc_pack = gather_weight(
        jnp.concatenate(
            [
                low(pack_attn(attn_project[0], attn_output[0])),
                misc,
                low(pack_ffn(ffn_expand[0], ffn_reduce[0])),
            ]
        )
    )
    dec_pack = gather_weight(
        jnp.concatenate(
            [
                low(pack_attn(attn_project[1], attn_output[1])),
                low(pack_attn(attn_project[2], attn_output[2])),
            ]
        )
    )
    dec_wide = gather_weight(low(pack_ffn(ffn_expand[1], ffn_reduce[1])))
    table = enc_pack[4, :, :LCLS].T
    gain = enc_pack[4, :, LCLS : LCLS + 7].T.astype(jnp.float32)
    weights = ((enc_pack[:4], dec_pack[:4], dec_pack[4:]), (enc_pack[5:], dec_wide), gain)
    scale_in = math.sqrt(D)
    class_ids = jnp.arange(LCLS, dtype=jnp.int32)
    sentence_ids = jnp.arange(SENTS, dtype=jnp.int32)

    src_emb = look_up(src_ids)
    dec_rows = look_up(dec_ids)
    dec_emb = jnp.concatenate(
        [
            jnp.broadcast_to(dec_rows[ROW - MASKED][None], (MASKED, D)),
            dec_rows[: ROW - MASKED],
        ]
    )
    enc_top, enc_kept = layer_fwd(
        scale_in * src_emb + position, weights, 0, src_allowed, None, None
    )
    dec_top, dec_kept = layer_fwd(
        scale_in * dec_emb + dec_position, weights, 1, tgt_allowed, enc_top, cross_allowed
    )

    tops = gather_group(low(dec_top[:MASKED])).reshape(-1, D)
    logits = dot_right(tops, block_rows)
    goal_hot = goal_ids[:, None] == block_ids[None, :]
    picked = jnp.sum(jnp.where(goal_hot, logits, 0.0))
    peak = jnp.max(logits, axis=1)
    total = jnp.sum(jnp.exp(logits - peak[:, None]), axis=1)
    totals = jnp.stack([turn(part.reshape(count_z, 2, MASKED)) for part in (peak, total)])
    totals = butterfly(totals, join_totals, ("vocab", "z"))
    log_total = turn(totals[0] + jnp.log(totals[1])).reshape(-1)
    grad_logits = low(
        (jnp.exp(logits - log_total[:, None]) - goal_hot.astype(jnp.float32)) * inverse
    )
    grad_rows = scatter_group(low(dot(grad_logits, block_rows)).reshape(count_z, 2, MASKED, D))
    grad_top = jnp.concatenate([grad_rows, jnp.zeros((ROW - MASKED, D), jnp.float32)])
    grad_block = dot_left(grad_logits, tops)

    member = (segments[None, :] == sentence_ids[:, None]).astype(jnp.float32)
    members = jnp.sum(member, axis=1, keepdims=True)
    pooled_low = low(jnp.dot(member, enc_top, precision=HIGHEST) / members)
    length_logits = jnp.einsum("sd,cd->sc", pooled_low, table, preferred_element_type=jnp.float32)
    length_total = jax.nn.logsumexp(length_logits, axis=1)
    class_hot = (lengths[:, None] - 1 == class_ids[None, :]).astype(jnp.float32)
    length_loss = length_total - jnp.sum(length_logits * class_hot, axis=1)
    loss_local = jnp.sum(log_total[:MASKED]) - picked + LENGTH_WEIGHT * jnp.sum(length_loss)
    grad_length = low(
        (jnp.exp(length_logits - length_total[:, None]) - class_hot) * (LENGTH_WEIGHT * inverse)
    )
    grad_table = jnp.einsum("sc,sd->dc", grad_length, pooled_low, preferred_element_type=jnp.float32)
    grad_pooled = jnp.einsum("sc,cd->sd", grad_length, table, preferred_element_type=jnp.float32)
    grad_enc = jnp.dot(member.T, grad_pooled / members, precision=HIGHEST)

    dec_stream, memory_grad, dec_gains, dec_attn, dec_ffn = layer_bwd(
        grad_top, dec_kept, weights, 1
    )
    sent = wide(low(scale_in * dec_stream))
    blank_sum = jnp.sum(sent[:MASKED], axis=0, keepdims=True)
    blank_high = low(blank_sum)
    blank_rest = low(blank_sum - wide(blank_high))
    sent = jnp.concatenate(
        [low(sent[MASKED:]), blank_high, blank_rest, jnp.zeros((14, D), jnp.bfloat16)]
    )
    again = jnp.where(jnp.arange(few) == ROW - MASKED + 1, MASK_TOKEN, 0).astype(jnp.int32)
    dec_sent = gather_group(sent).reshape(-1, D)
    back_ids = jnp.where(again[None] > 0, again[None], dec_ids.reshape(-1, few)).reshape(-1)
    dec_hot = low(back_ids[:, None] == block_ids[None, :])
    grad_block = grad_block + dot_left(dec_hot, dec_sent)
    enc_stream, _, enc_gains, enc_attn, enc_ffn = layer_bwd(
        grad_enc + memory_grad, enc_kept, weights, 0
    )
    src_sent = gather_group(low(scale_in * enc_stream)).reshape(-1, D)
    src_hot = low(src_ids[:, None] == block_ids[None, :])
    grad_block = grad_block + dot_left(src_hot, src_sent)
    blocks = grad_block.reshape(2, 2, shard, D)
    chip = blocks[:, 0] + wide(swap(low(blocks[:, 1]), "core"))
    grad_embed = chip[0] + wide(swap(low(chip[1]), "y"))

    grad_gain = jnp.stack(enc_gains + dec_gains).T
    grad_misc = jnp.concatenate(
        [grad_table, grad_gain, jnp.zeros((D, D - LCLS - 7), jnp.float32)], axis=1
    )
    sum_dec_ffn = scatter_weight(dec_ffn)
    sum_dec_attn = scatter_weight(jnp.concatenate([dec_attn[1], dec_attn[2]]))
    sum_enc_ffn = scatter_weight(enc_ffn)
    sum_enc_attn = scatter_weight(jnp.concatenate([enc_attn[0], grad_misc[None]]))
    attn = [unpack_attn(part) for part in (sum_enc_attn[:4], sum_dec_attn[:4], sum_dec_attn[4:])]
    ffn = [unpack_ffn(part) for part in (sum_enc_ffn, sum_dec_ffn)]
    reduced = (
        jnp.stack([part[0] for part in attn]),
        jnp.stack([part[1] for part in attn]),
        jnp.stack([part[0] for part in ffn]),
        jnp.stack([part[1] for part in ffn]),
        sum_enc_attn[4, :, LCLS : LCLS + 7].T,
        sum_enc_attn[4, :, :LCLS].T,
        grad_embed,
    )
    layer_squares = jnp.zeros((), jnp.float32)
    for grad in reduced[:6]:
        layer_squares = layer_squares + jnp.sum(grad * grad)
    table_squares = jnp.sum(reduced[6] * reduced[6])
    vocab_count = lax.axis_size("vocab")
    totals = butterfly(
        jnp.stack([layer_squares / vocab_count + table_squares, loss_local]),
        jnp.add,
        ("core", "vocab", "y", "z"),
    )
    squares, loss_sum = (totals[0], totals[1])
    grad_norm = jnp.sqrt(squares)
    factor = jnp.minimum(1.0, CLIP / grad_norm)
    rate = RATE_SCALE * math.sqrt(NPARAM / D) / CLIP
    fresh, moved, smooth, copies = ([], [], [], [])
    for weight, grad, moment, average, boost in zip(
        masters, reduced, moments, averages, RATE_FACTORS
    ):
        clipped = grad * factor
        moment = MOMENTUM * moment + clipped
        weight = weight - boost * rate * (clipped + MOMENTUM * moment)
        average = KEEP * average + (1.0 - KEEP) * weight
        fresh.append(weight)
        moved.append(moment)
        smooth.append(average)
        copies.append(weight.astype(jnp.bfloat16))
    return (loss_sum, grad_norm) + tuple(fresh) + tuple(moved) + tuple(smooth) + tuple(copies)


def solution(mesh):
    vocab = mesh.shape["vocab"]
    grid = Mesh(mesh.devices.reshape(-1, 2, 2, vocab), ("z", "y", "core", "vocab"))
    dp = ("z", "y", "core")
    return jax.shard_map(
        shards,
        mesh=grid,
        in_specs=(
            P(dp, None),
            P(dp, None),
            P(dp, None),
            P(dp, None),
            P(dp, None),
            P(None, dp, None),
            P(None, dp, None),
            P(None, dp, None),
            P(None, dp, None),
            P(None, dp),
            P(None, dp),
            P(("vocab",) + dp, None),
            P(None, dp, None),
            P(None, dp, None),
            P(None, dp, None),
            P(None, dp, None),
            P(None, dp),
            P(None, dp),
            P(("vocab",) + dp, None),
            P(None, dp, None),
            P(None, dp, None),
            P(None, dp, None),
            P(None, dp, None),
            P(None, dp),
            P(None, dp),
            P(("vocab",) + dp, None),
        ),
        out_specs=(
            P(),
            P(),
            P(None, dp, None),
            P(None, dp, None),
            P(None, dp, None),
            P(None, dp, None),
            P(None, dp),
            P(None, dp),
            P(("vocab",) + dp, None),
            P(None, dp, None),
            P(None, dp, None),
            P(None, dp, None),
            P(None, dp, None),
            P(None, dp),
            P(None, dp),
            P(("vocab",) + dp, None),
            P(None, dp, None),
            P(None, dp, None),
            P(None, dp, None),
            P(None, dp, None),
            P(None, dp),
            P(None, dp),
            P(("vocab",) + dp, None),
            P(None, dp, None),
            P(None, dp, None),
            P(None, dp, None),
            P(None, dp, None),
            P(None, dp),
            P(None, dp),
            P(("vocab",) + dp, None),
        ),
        check_vma=False,
    )
```

```python
import functools
import math

import jax
import jax.numpy as jnp
from jax import lax
from jax.experimental import pallas as pl
from jax.experimental.pallas import tpu as pltpu
from jax.sharding import Mesh
from jax.sharding import PartitionSpec as P

D = 512
HDIM = 64
LCLS = 256
ROW = 256
SENTS = 8
MASKED = 96
NPARAM = 23858688


HIGHEST = lax.Precision.HIGHEST
EPSILON = 1e-05
MASK_TOKEN = 3
MOMENTUM = 0.9
KEEP = 0.9
CLIP = 0.02
LENGTH_WEIGHT = 0.1
NEGATIVE = -1e30
RATE_SCALE = 0.25
RATE_FACTORS = (1.0, 1.0, 1.0, 1.0, 6.0, 24.0, 1.0)


def sinusoid(count, width):
    place = jnp.arange(count, dtype=jnp.float32)[:, None]
    index = jnp.arange(width // 2, dtype=jnp.float32)[None, :]
    angle = place * jnp.exp(-math.log(10000.0) * 2.0 * index / width)
    return jnp.concatenate([jnp.sin(angle), jnp.cos(angle)], axis=1)


SWAP = [(0, 1), (1, 0)]


def swap(value, axis):
    return lax.ppermute(value, axis, SWAP)


def shift(value, by):
    count = lax.axis_size("z")
    return lax.ppermute(value, "z", [(i, (i + by) % count) for i in range(count)])


def low(value):
    return value.astype(jnp.bfloat16)


def wide(value):
    return value.astype(jnp.float32)


def ring_first(value):
    if lax.axis_size("z") != 4:
        return value, value
    return shift(value, 1), shift(value, -1)


def ring_second(value, below, above):
    count = lax.axis_size("z")
    if count != 4:
        whole = lax.all_gather(value, "z", axis=0)
        here = lax.axis_index("z")
        return [lax.dynamic_index_in_dim(whole, (here - k) % count, 0, False) for k in range(count)]
    half = value.shape[0] // 2
    return [value, below, shift(below[:half], 1), shift(above[half:], -1), above]


def ring_gather(value):
    return ring_second(value, *ring_first(value))


def ring_scatter(blocks):
    count = lax.axis_size("z")
    if count != 4:
        here = lax.axis_index("z")
        order = (here - jnp.arange(count)) % count
        stacked = jnp.stack([low(block) for block in blocks])
        whole = jnp.zeros_like(stacked).at[order].set(stacked)
        return wide(lax.psum_scatter(whole, "z", scatter_dimension=0))
    half = blocks[0].shape[0] // 2
    from_above = shift(low(blocks[2][:half]), -1)
    from_below = shift(low(blocks[2][half:]), 1)
    down = jnp.concatenate([wide(blocks[1][:half]) + wide(from_above), wide(blocks[1][half:])])
    up = jnp.concatenate([wide(blocks[3][:half]), wide(blocks[3][half:]) + wide(from_below)])
    from_above = shift(low(down), -1)
    from_below = shift(low(up), 1)
    return wide(blocks[0]) + wide(from_above) + wide(from_below)


def gather_weight(value):
    return lax.all_gather(value, ("z", "y", "core"), axis=1, tiled=True)


def take(value, index, axis):
    return lax.dynamic_index_in_dim(value, index, axis, False)


def add_swap(value):
    mine = low(value)
    return wide(mine) + wide(swap(mine, "vocab"))


def by_core(grads):
    core = lax.axis_index("core")
    count = lax.axis_size("z")
    parts = grads.reshape(grads.shape[0], count, 2, 2, -1, grads.shape[2])
    parts = parts.transpose(0, 3, 2, 1, 4, 5).reshape(grads.shape[0], 2, -1, grads.shape[2])
    return take(parts, core, 1), take(parts, 1 - core, 1)


def swap_core(mine, theirs):
    if lax.axis_size("z") != 4:
        mine, theirs = by_core(jnp.concatenate([mine, theirs], axis=1))
    return mine, swap(theirs, "core")


def low_sum(*refs):
    return low(sum(wide(ref[...]) for ref in refs))


def sums_kernel(at_ref, *refs):
    count = len(refs) // 3
    for k in range(count):
        refs[2 * count + k][...] = low_sum(refs[2 * k], refs[2 * k + 1])


def line_kernel(at_ref, *refs):
    own, down, far, up = (low_sum(refs[2 * k], refs[2 * k + 1]) for k in range(4))
    own_ref, down_ref, far_down_ref, far_up_ref, up_ref = refs[8:]
    own_ref[...] = own
    down_ref[...] = down
    up_ref[...] = up
    half = far.shape[2] // 2
    far_down_ref[...] = far[:, :, :half]
    far_up_ref[...] = far[:, :, half:]


def pass_kernel(down_ref, up_ref, above_ref, below_ref, down_out, up_out):
    half = above_ref.shape[2]
    down_out[:, :, :half] = low(wide(down_ref[:, :, :half]) + wide(above_ref[...]))
    down_out[:, :, half:] = down_ref[:, :, half:]
    up_out[:, :, :half] = up_ref[:, :, :half]
    up_out[:, :, half:] = low(wide(up_ref[:, :, half:]) + wide(below_ref[...]))


def three_kernel(one_ref, two_ref, three_ref, out_ref):
    out_ref[...] = low_sum(one_ref, two_ref, three_ref)


def two_kernel(one_ref, two_ref, out_ref, square_ref):
    total = wide(one_ref[...]) + wide(two_ref[...])
    out_ref[...] = total
    square_ref[0, 0] = jnp.sum(total * total)


def both_kernel(at_ref, mine_ref, theirs_ref, out_ref, square_ref):
    size = mine_ref.shape[0]
    mine, theirs = (wide(mine_ref[...]), wide(theirs_ref[...]))
    out_ref[pl.ds(at_ref[0] * size, size)] = mine
    out_ref[pl.ds((1 - at_ref[0]) * size, size)] = theirs
    square_ref[0, 0] = jnp.sum(mine * mine) + jnp.sum(theirs * theirs)


def staged(kernel, at, steps, block, mine, theirs, places, outs, out_place):
    def spec(place):
        return pl.BlockSpec(block, lambda i, at: place(i, at[0]))

    def out_spec(shape):
        return pl.BlockSpec(block[:2] + shape[2:], lambda i, at: out_place(i))

    return pl.pallas_call(
        kernel,
        grid_spec=pltpu.PrefetchScalarGridSpec(
            num_scalar_prefetch=1,
            grid=(steps,),
            in_specs=[spec(place) for place in places for _ in (0, 1)],
            out_specs=[out_spec(shape) for shape in outs],
        ),
        out_shape=[jax.ShapeDtypeStruct(shape, jnp.bfloat16) for shape in outs],
        compiler_params=pltpu.CompilerParams(vmem_limit_bytes=VMEM_BYTES),
    )(at[None].astype(jnp.int32), *([mine, theirs] * len(places)))


def add_vocab_parts(mine, theirs):
    blocks, rows, columns = mine.shape
    kept = (blocks // 2, rows, columns)
    steps = 2
    return staged(
        sums_kernel, lax.axis_index("vocab"), steps, (blocks // 2 // steps, rows, columns),
        mine, theirs,
        (lambda i, at: (at * steps + i, 0, 0), lambda i, at: ((1 - at) * steps + i, 0, 0)),
        (kept, kept), lambda i: (i, 0, 0),
    )


def add_side_parts(mine, theirs):
    blocks, rows, columns = mine.shape
    kept = (blocks, rows // 2, columns)
    steps = 2
    return staged(
        sums_kernel, lax.axis_index("y"), steps, (blocks, rows // 2 // steps, columns),
        mine, theirs,
        (lambda i, at: (0, at * steps + i, 0), lambda i, at: (0, (1 - at) * steps + i, 0)),
        (kept, kept), lambda i: (0, i, 0),
    )


def line_parts(mine, theirs):
    here, count = (lax.axis_index("z"), lax.axis_size("z"))
    blocks, rows, columns = mine.shape
    if count != 4:
        return low(wide(mine) + wide(theirs)).reshape(blocks, count, -1, columns)
    part = (blocks, rows // 4, columns)
    half = (blocks, rows // 4, columns // 2)
    places = [lambda i, at, k=k: (0, lax.rem(at - k + 4, 4), 0) for k in range(4)]
    return staged(
        line_kernel, here, 1, part, mine, theirs, places, (part, part, half, half, part),
        lambda i: (0, 0, 0),
    )


def line_first(parts):
    if lax.axis_size("z") != 4:
        return parts
    return shift(parts[2], -1), shift(parts[3], 1)


def line_second(parts, near):
    if lax.axis_size("z") != 4:
        return low(lax.psum_scatter(near, "z", scatter_dimension=1))
    own, down, _, _, up = parts
    down, up = run(pass_kernel, (down, up), down, up, *near)
    return run(three_kernel, (own,), own, shift(down, -1), shift(up, 1))[0]


SQUARE = jax.ShapeDtypeStruct((1, 1), jnp.float32)


def add_vocab_last(part):
    out = jax.ShapeDtypeStruct(part.shape, jnp.float32)
    total, square = run(two_kernel, (out, SQUARE), part, swap(part, "vocab"))
    return total, square[0, 0]


def join_vocab(part):
    out = jax.ShapeDtypeStruct((2 * part.shape[0],) + part.shape[1:], jnp.float32)
    half = lax.axis_index("vocab")[None].astype(jnp.int32)
    total, square = run(both_kernel, (out, SQUARE), half, part, swap(part, "vocab"))
    return total, square[0, 0]


def after(value, *others):
    return lax.optimization_barrier((value,) + others)[0]


def pair_vocab(value):
    return jnp.stack([value, swap(value, "vocab")])


def gather_group(value):
    pieces = ring_gather(pair_vocab(value))
    return jnp.concatenate([piece.reshape(-1, value.shape[-1]) for piece in pieces])


def add_vocab(parts):
    return parts[..., 0, :, :] + swap(low(parts[..., 1, :, :]), "vocab")


def scatter_line(parts):
    return ring_scatter([parts[k] for k in range(parts.shape[0])])


def scatter_group(parts):
    return scatter_line(add_vocab(parts))


def butterfly(value, join, axes):
    for axis in axes:
        count = lax.axis_size(axis)
        step = 1
        while step < count:
            pairs = [(i, i ^ step) for i in range(count)]
            value = join(value, lax.ppermute(value, axis, pairs))
            step *= 2
    return value


def join_totals(left, right):
    peak = jnp.maximum(left[0], right[0])
    return jnp.stack(
        [peak, left[1] * jnp.exp(left[0] - peak) + right[1] * jnp.exp(right[0] - peak)]
    )


def turn(value):
    count = lax.axis_size("z")
    here, half = (lax.axis_index("z"), lax.axis_index("vocab"))
    value = jnp.where(half == 0, value, value[:, ::-1])
    backward = value[::-1]
    twice = jnp.concatenate([backward, backward])
    return lax.dynamic_slice_in_dim(twice, count - 1 - here, count, 0)


SCALE = HDIM ** (-0.5)
GELU_A = math.sqrt(2.0 / math.pi)
GELU_B = 0.044715


def dot(left, right):
    return jnp.dot(left, right, preferred_element_type=jnp.float32)


def dot_left(left, right):
    return lax.dot_general(left, right, (((0,), (0,)), ((), ())), preferred_element_type=jnp.float32)


def dot_right(left, right):
    return lax.dot_general(left, right, (((1,), (1,)), ((), ())), preferred_element_type=jnp.float32)


def norm_parts(stream):
    centred = stream - jnp.mean(stream, axis=-1, keepdims=True)
    inverse = lax.rsqrt(jnp.mean(centred * centred, axis=-1, keepdims=True) + EPSILON)
    return centred * inverse, inverse


def norm_back(grad, stream, gain):
    normed, inverse = norm_parts(stream)
    scaled = grad * gain
    through = scaled - jnp.mean(scaled, axis=-1, keepdims=True)
    through = through - normed * jnp.mean(scaled * normed, axis=-1, keepdims=True)
    return through * inverse, jnp.sum(grad * normed, axis=0, keepdims=True)


def gelu_parts(hidden):
    bend = jnp.tanh(GELU_A * (hidden + GELU_B * hidden * hidden * hidden))
    return bend, 0.5 * (1.0 + bend)


def lane_halves(kind):
    first = lax.broadcasted_iota(jnp.int32, (1, 2 * HDIM), 1) < HDIM
    ones = first.astype(jnp.float32)
    return first, (ones.astype(kind), (1.0 - ones).astype(kind))


def softmax_of(query, keys, allowed):
    scores = jnp.where(allowed, dot_right(query, keys) * SCALE, NEGATIVE)
    expo = jnp.exp(scores - jnp.max(scores, axis=-1, keepdims=True))
    return expo / jnp.sum(expo, axis=-1, keepdims=True)


def attend_inside(low_query, low_memory, w, allowed, q_ref, k_ref, v_ref, o_ref):
    q_ref[...] = low(dot(low_query, w[0]))
    k_ref[...] = low(dot(low_memory, w[1]))
    v_ref[...] = low(dot(low_memory, w[2]))
    first, keeps = lane_halves(jnp.bfloat16)
    for tile in range(0, D, 2 * HDIM):
        lanes = slice(tile, tile + 2 * HDIM)
        query, keys, values = (q_ref[:, lanes], k_ref[:, lanes], v_ref[:, lanes])
        outs = [
            dot(low(softmax_of(query * keep, keys, allowed)), values) for keep in keeps
        ]
        o_ref[:, lanes] = low(jnp.where(first, outs[0], outs[1]))
    return dot(o_ref[...], w[3])


def down_blocks(w, plain, wd_ref):
    if plain:
        return [w[4 + j] for j in range(4)]
    rows = D // 16
    for place in range(16):
        for j in range(4):
            start = (place % 4) * 4 * rows + j * rows
            wd_ref[place // 4, start : start + rows] = w[4 + j, place * rows : (place + 1) * rows]
    return [wd_ref[j] for j in range(4)]


def ffn_inside(normed, w, plain, h_ref, wd_ref):
    branch = None
    down = down_blocks(w, plain, wd_ref)
    for j in range(4):
        hidden = dot(normed, w[j])
        h_ref[j] = hidden
        part = dot(low(hidden * gelu_parts(hidden)[1]), down[j])
        branch = part if branch is None else branch + part
    return branch


def store_split(core_ref, mine_ref, theirs_ref, j, value):
    value = low(value)
    count = core_ref.shape[0]
    step = D // (4 * count)
    if count != 4:
        mine_ref[j] = value[: D // 2]
        theirs_ref[j] = value[D // 2 :]
        return
    upper, lower = (
        jnp.concatenate(
            [
                value[((z * 2 + y) * 2 + c) * step : ((z * 2 + y) * 2 + c + 1) * step]
                for y in (0, 1)
                for z in range(count)
            ]
        )
        for c in (0, 1)
    )
    first = core_ref[0] == 0
    mine_ref[j] = jnp.where(first, upper, lower)
    theirs_ref[j] = jnp.where(first, lower, upper)


def enc_fwd_kernel(plain, x_ref, gain_ref, wa_ref, wf_ref, sc_ref, sr_ref, x1_ref, x2_ref, top_ref, q_ref, k_ref, v_ref, o_ref, h_ref, *wd):
    allowed = sc_ref[...] == sr_ref[...]
    stream = x_ref[...]
    normed = low(norm_parts(stream)[0] * gain_ref[0:1])
    stream = stream + attend_inside(normed, normed, wa_ref, allowed, q_ref, k_ref, v_ref, o_ref)
    x1_ref[...] = stream
    normed = low(norm_parts(stream)[0] * gain_ref[1:2])
    stream = stream + ffn_inside(normed, wf_ref, plain, h_ref, *wd)
    x2_ref[...] = stream
    top_ref[...] = norm_parts(stream)[0] * gain_ref[2:3]


def dec_self_kernel(x_ref, gain_ref, w_ref, tc_ref, tr_ref, y1_ref, q_ref, k_ref, v_ref, o_ref):
    stream = x_ref[...]
    normed = low(norm_parts(stream)[0] * gain_ref[3:4])
    branch = attend_inside(
        normed, normed, w_ref, tc_ref[...] == tr_ref[...], q_ref, k_ref, v_ref, o_ref
    )
    y1_ref[...] = stream + branch


def dec_rest_kernel(plain, y1_ref, mem_ref, gain_ref, wa_ref, wf_ref, tc_ref, sr_ref, y2_ref, y3_ref, top_ref, q_ref, k_ref, v_ref, o_ref, h_ref, *wd):
    stream = y1_ref[...]
    normed = low(norm_parts(stream)[0] * gain_ref[4:5])
    memory = low(mem_ref[...])
    stream = stream + attend_inside(
        normed, memory, wa_ref, tc_ref[...] == sr_ref[...], q_ref, k_ref, v_ref, o_ref
    )
    y2_ref[...] = stream
    normed = low(norm_parts(stream)[0] * gain_ref[5:6])
    stream = stream + ffn_inside(normed, wf_ref, plain, h_ref, *wd)
    y3_ref[...] = stream
    top_ref[...] = norm_parts(stream)[0] * gain_ref[6:7]


def store_down(core_ref, mine_ref, theirs_ref, j, value):
    if core_ref.shape[0] != 4:
        store_split(core_ref, mine_ref, theirs_ref, 4 + j, value)
        return
    value = low(value)
    first = core_ref[0] == 0
    rows = D // 16
    for y in (0, 1):
        for part in range(4):
            upper, lower = (
                value[start : start + rows]
                for start in ((y * 2 + c) * 4 * rows + part * rows for c in (0, 1))
            )
            to = slice((y * 4 + j) * rows, (y * 4 + j + 1) * rows)
            mine_ref[4 + part, to] = jnp.where(first, upper, lower)
            theirs_ref[4 + part, to] = jnp.where(first, lower, upper)


def ffn_back_kernel(place, plain, grad_ref, end_ref, mid_ref, h_ref, gain_ref, w_ref, core_ref, out_ref, mine_ref, theirs_ref, dg_ref, *wd):
    grad_stream, end_gain = norm_back(grad_ref[...], end_ref[...], gain_ref[place + 1 : place + 2])
    grad_low = low(grad_stream)
    gain = gain_ref[place : place + 1]
    normed = low(norm_parts(mid_ref[...])[0] * gain)
    total = None
    down = down_blocks(w_ref, plain, *(wd or (None,)))
    for j in range(4):
        hidden = h_ref[j]
        bend, half = gelu_parts(hidden)
        store_down(core_ref, mine_ref, theirs_ref, j, dot_left(low(hidden * half), grad_low))
        slope = half + 0.5 * hidden * (1.0 - bend * bend) * GELU_A * (
            1.0 + 3.0 * GELU_B * hidden * hidden
        )
        grad_hidden = low(dot_right(grad_low, down[j]) * slope)
        store_split(core_ref, mine_ref, theirs_ref, j, dot_left(normed, grad_hidden))
        part = dot_right(grad_hidden, w_ref[j])
        total = part if total is None else total + part
    extra, mid_gain = norm_back(total, mid_ref[...], gain)
    out_ref[...] = grad_stream + extra
    dg_ref[...] = jnp.concatenate([mid_gain, end_gain], axis=0)


def attn_back_inside(grad_low, normed, memory, refs, w, allowed, dw_refs, scratch):
    q_ref, k_ref, v_ref, o_ref = refs
    do_ref, dq_ref, dk_ref, dv_ref = scratch
    store_split(*dw_refs, 3, dot_left(o_ref[...], grad_low))
    do_ref[...] = low(dot_right(grad_low, w[3]))
    first, keeps = lane_halves(jnp.bfloat16)
    for tile in range(0, D, 2 * HDIM):
        lanes = slice(tile, tile + 2 * HDIM)
        query, keys, values, grad_mixed = (
            ref[:, lanes] for ref in (q_ref, k_ref, v_ref, do_ref)
        )
        found = []
        for keep in keeps:
            probs = softmax_of(query * keep, keys, allowed)
            grad_probs = dot_right(grad_mixed * keep, values)
            inner = jnp.sum(probs * grad_probs, axis=-1, keepdims=True)
            grad_scores = low(probs * (grad_probs - inner))
            found.append(
                (
                    dot(grad_scores, keys),
                    dot_left(grad_scores, query),
                    dot_left(low(probs), grad_mixed),
                )
            )
        dq_ref[:, lanes] = low(jnp.where(first, found[0][0], found[1][0]) * SCALE)
        dk_ref[:, lanes] = low(jnp.where(first, found[0][1], found[1][1]) * SCALE)
        dv_ref[:, lanes] = low(jnp.where(first, found[0][2], found[1][2]))
    store_split(*dw_refs, 0, dot_left(normed, dq_ref[...]))
    store_split(*dw_refs, 1, dot_left(memory, dk_ref[...]))
    store_split(*dw_refs, 2, dot_left(memory, dv_ref[...]))
    grad_query = dot_right(dq_ref[...], w[0])
    grad_memory = dot_right(dk_ref[...], w[1]) + dot_right(dv_ref[...], w[2])
    return grad_query, grad_memory


def self_back_kernel(place, grad_ref, x_ref, q_ref, k_ref, v_ref, o_ref, gain_ref, w_ref, sc_ref, sr_ref, core_ref, held_ref, kept_ref, out_ref, mine_ref, theirs_ref, dg_ref, *scratch):
    gain = gain_ref[place : place + 1]
    normed = low(norm_parts(x_ref[...])[0] * gain)
    grad_query, grad_memory = attn_back_inside(
        low(grad_ref[...]), normed, normed, (q_ref, k_ref, v_ref, o_ref), w_ref,
        sc_ref[...] == sr_ref[...], (core_ref, mine_ref, theirs_ref), scratch,
    )
    extra, dg_ref[...] = norm_back(grad_query + grad_memory, x_ref[...], gain)
    out_ref[...] = grad_ref[...] + extra


def cross_back_kernel(place, grad_ref, x_ref, mem_ref, q_ref, k_ref, v_ref, o_ref, gain_ref, w_ref, sc_ref, sr_ref, core_ref, held_ref, kept_ref, out_ref, dmem_ref, mine_ref, theirs_ref, dg_ref, *scratch):
    gain = gain_ref[place : place + 1]
    normed = low(norm_parts(x_ref[...])[0] * gain)
    grad_query, dmem_ref[...] = attn_back_inside(
        low(grad_ref[...]), normed, low(mem_ref[...]), (q_ref, k_ref, v_ref, o_ref), w_ref,
        sc_ref[...] == sr_ref[...], (core_ref, mine_ref, theirs_ref), scratch,
    )
    extra, dg_ref[...] = norm_back(grad_query, x_ref[...], gain)
    out_ref[...] = grad_ref[...] + extra


def ids_along(first_ref, j, count, dim):
    shape = (1, count) if dim else (count, 1)
    return first_ref[j] + lax.broadcasted_iota(jnp.int32, shape, dim)


def head_fwd_kernel(top_ref, goal_ref, first_ref, *refs):
    blocks, (peak_ref, total_ref, pick_ref) = (refs[:4], refs[4:])
    peak_ref[...] = jnp.full(peak_ref.shape, NEGATIVE, jnp.float32)
    total_ref[...] = jnp.zeros(total_ref.shape, jnp.float32)
    pick_ref[...] = jnp.zeros(pick_ref.shape, jnp.float32)
    for j, block_ref in enumerate(blocks):
        logits = dot_right(top_ref[...], block_ref[...])
        hot = goal_ref[...] == ids_along(first_ref, j, block_ref.shape[0], 1)
        pick_ref[...] += jnp.sum(jnp.where(hot, logits, 0.0), axis=1, keepdims=True)
        peak = peak_ref[...]
        higher = jnp.maximum(peak, jnp.max(logits, axis=1, keepdims=True))
        total_ref[...] = total_ref[...] * jnp.exp(peak - higher) + jnp.sum(
            jnp.exp(logits - higher), axis=1, keepdims=True
        )
        peak_ref[...] = higher


def head_back_kernel(inverse, top_ref, goal_ref, log_ref, first_ref, *refs):
    blocks, (rows_ref, *grads_out, sum_ref) = (refs[:4], refs[4:])
    for j, block_ref in enumerate(blocks):
        logits = dot_right(top_ref[...], block_ref[...])
        hot = goal_ref[...] == ids_along(first_ref, j, block_ref.shape[0], 1)
        grads = low((jnp.exp(logits - log_ref[...]) - hot.astype(jnp.float32)) * inverse)
        rows = dot(grads, block_ref[...])
        sum_ref[...] = rows if j == 0 else sum_ref[...] + rows
        grads_out[j][...] = dot_left(grads, top_ref[...])
    rows_ref[...] = low(sum_ref[...])


def spread_kernel(picks, pieces, first_ref, ids_ref, *refs):
    count = len(picks)
    rows_refs, refs = (refs[:pieces], refs[pieces:])
    for j, base_ref, out_ref in zip(picks, refs[:count], refs[count:]):
        total = base_ref[...]
        start = 0
        for rows_ref in rows_refs:
            stop = start + rows_ref.shape[0]
            hot = ids_along(first_ref, j, base_ref.shape[0], 0) == ids_ref[:, start:stop]
            total = total + dot(hot.astype(jnp.bfloat16), rows_ref[...])
            start = stop
        out_ref[...] = total.astype(out_ref.dtype)


VMEM_BYTES = 48 * 2**20
FULL = jax.ShapeDtypeStruct((ROW, D), jnp.float32)
HALF = jax.ShapeDtypeStruct((ROW, D), jnp.bfloat16)
HIDDEN = jax.ShapeDtypeStruct((4, ROW, D), jnp.float32)


def halves_of(count):
    return jax.ShapeDtypeStruct((count, D // 2, D), jnp.bfloat16)


def gains_of(count):
    return jax.ShapeDtypeStruct((count, D), jnp.float32)


def spec_of(item):
    if item is None:
        return pl.BlockSpec(memory_space=pl.ANY)
    if isinstance(item, tuple):
        array, size, index = item
        shape, place = ((size,) + array.shape[1:], index)
    else:
        shape, place = (item.shape, 0)
    if len(shape) == 1 or shape == (1, 1):
        return pl.BlockSpec(memory_space=pltpu.SMEM)
    return pl.BlockSpec(shape, lambda i: (place,) + (0,) * (len(shape) - 1))


def run(kernel, outs, *operands, held=(), scratch=0, down=0, total=0, flops=0):
    arrays = [item[0] if isinstance(item, tuple) else item for item in operands]
    in_specs = [spec_of(item) for item in operands]
    shapes = [item[0] if isinstance(item, tuple) else item for item in outs]
    shapes = [jax.ShapeDtypeStruct(item.shape, item.dtype) for item in shapes]
    aliases = {}
    for array, place in held:
        aliases[len(arrays)] = place
        arrays.append(array)
        in_specs.append(spec_of(None))
    moved = sum(math.prod(x.shape) * x.dtype.itemsize for x in arrays + shapes)
    return pl.pallas_call(
        kernel,
        grid=(1,),
        out_shape=shapes,
        in_specs=in_specs,
        out_specs=[spec_of(item) for item in outs],
        input_output_aliases=aliases,
        scratch_shapes=[pltpu.VMEM((ROW, D), jnp.bfloat16)] * scratch
        + [pltpu.VMEM((4, D, D), jnp.bfloat16)] * down
        + [pltpu.VMEM((total, D), jnp.float32)] * (total > 0),
        compiler_params=pltpu.CompilerParams(vmem_limit_bytes=VMEM_BYTES),
        cost_estimate=pl.CostEstimate(flops=flops, bytes_accessed=moved, transcendentals=0),
    )(*arrays)


def spread(picks, kinds, ids, pieces, first_ids, bases):
    pieces = [piece.reshape(-1, D) for piece in pieces]
    return run(
        functools.partial(spread_kernel, picks, len(pieces)),
        [jax.ShapeDtypeStruct(base.shape, kind) for base, kind in zip(bases, kinds)],
        first_ids, ids[None], *pieces, *bases,
        flops=2 * len(picks) * ids.shape[0] * D * bases[0].shape[0],
    )


def pack_attn(project, output):
    width = output.shape[1]
    return jnp.stack([project[:, j * width : (j + 1) * width] for j in range(3)] + [output])


def pack_ffn(expand, reduce):
    rows, width = (expand.shape[0], reduce.shape[1])
    up = [expand[:, j * width : (j + 1) * width] for j in range(4)]
    return jnp.concatenate([jnp.stack(up), reduce.reshape(4, rows, width)])


def down_in_order(pack, count):
    parts = pack[4:8].reshape(4, count, -1, D).transpose(1, 0, 2, 3).reshape(4, D, D)
    return jnp.concatenate([pack[:4], parts])


def down_in_packs(grads, count):
    parts = grads[4:8].reshape(count, 4, -1, D).transpose(1, 0, 2, 3).reshape(4, D, D)
    return jnp.concatenate([grads[:4], parts])


def update_kernel(boosts, scalar_ref, dec_ref, enc_ref, *refs):
    factor = scalar_ref[0]
    packs = ((enc_ref, 8, 0), (dec_ref, 0, 8), (dec_ref, 4, None))
    rate = RATE_SCALE * math.sqrt(NPARAM / D) / CLIP

    def write(which, place, grad):
        weight, moment, average = (refs[3 * which + k][place] for k in range(3))
        outs = refs[12 + 4 * which : 16 + 4 * which]
        clipped = grad * factor
        moment = MOMENTUM * moment + clipped
        weight = weight - boosts[which] * rate * (clipped + MOMENTUM * moment)
        outs[0][place] = weight
        outs[1][place] = moment
        outs[2][place] = KEEP * average + (1.0 - KEEP) * weight
        outs[3][place] = low(weight)

    rows = enc_ref.shape[1]
    for layer, (pack_ref, attn, ffn) in enumerate(packs):
        for j in range(3):
            write(0, (layer, slice(None), slice(j * D, (j + 1) * D)), pack_ref[attn + j])
        write(1, (layer,), pack_ref[attn + 3])
        if ffn is None:
            continue
        for j in range(4):
            write(2, (layer, slice(None), slice(j * D, (j + 1) * D)), pack_ref[ffn + j])
            write(3, (layer, slice(j * rows, (j + 1) * rows)), pack_ref[ffn + 4 + j])


def shards(
    src_tokens,
    tgt_tokens,
    src_segments,
    tgt_lengths,
    mask_order,
    attn_project,
    attn_output,
    ffn_expand,
    ffn_reduce,
    norm_gains,
    length_table,
    embedding,
    momentum_attn_project,
    momentum_attn_output,
    momentum_ffn_expand,
    momentum_ffn_reduce,
    momentum_norm_gains,
    momentum_length_table,
    momentum_embedding,
    average_attn_project,
    average_attn_output,
    average_ffn_expand,
    average_ffn_reduce,
    average_norm_gains,
    average_length_table,
    average_embedding,
):
    masters = (
        attn_project,
        attn_output,
        ffn_expand,
        ffn_reduce,
        norm_gains,
        length_table,
        embedding,
    )
    moments = (
        momentum_attn_project,
        momentum_attn_output,
        momentum_ffn_expand,
        momentum_ffn_reduce,
        momentum_norm_gains,
        momentum_length_table,
        momentum_embedding,
    )
    averages = (
        average_attn_project,
        average_attn_output,
        average_ffn_expand,
        average_ffn_reduce,
        average_norm_gains,
        average_length_table,
        average_embedding,
    )
    count_z = lax.axis_size("z")
    here, side, core, half = (
        lax.axis_index("z"),
        lax.axis_index("y"),
        lax.axis_index("core"),
        lax.axis_index("vocab"),
    )
    rows_here = src_tokens.shape[0]
    count_dp = count_z * 4
    inverse = 1.0 / (SENTS * rows_here * count_dp)
    source, target, segments, lengths, order = (
        lax.dynamic_index_in_dim(array, half, 0, False)
        for array in (src_tokens, tgt_tokens, src_segments, tgt_lengths, mask_order)
    )
    shuffled = target[order]
    bounds = jnp.cumsum(lengths)
    tsegs = jnp.sum((order[:, None] >= bounds[None, :]).astype(jnp.int32), axis=1)
    position = sinusoid(ROW, D)
    dec_position = position[order]

    own_rows = low(embedding)
    shard = own_rows.shape[0]
    far_rows = swap(own_rows, "y")
    near = (own_rows, swap(own_rows, "core"))
    place = half * count_dp + here * 4
    firsts = [
        (place + at_side * 2 + at_core) * shard
        for at_side in (side, 1 - side)
        for at_core in (core, 1 - core)
    ]
    first_ids = jnp.stack(firsts).astype(jnp.int32)
    offsets = jnp.arange(shard, dtype=jnp.int32)

    few = ROW - MASKED + 16
    extra = jnp.where(jnp.arange(16) == 0, MASK_TOKEN, -1).astype(jnp.int32)
    group = count_z * 2
    numbers = jnp.concatenate([source, shuffled, extra])
    numbers = lax.all_to_all(
        jnp.broadcast_to(numbers[None], (group, 2 * ROW + 16)), ("z", "vocab"), 0, 0, tiled=True
    )
    numbers = turn(numbers.reshape(count_z, 2, -1)).reshape(group, -1)
    src_ids = numbers[:, :ROW].reshape(-1)
    goal_ids = numbers[:, ROW : ROW + MASKED].reshape(-1)
    dec_ids = numbers[:, ROW + MASKED :].reshape(-1)

    def look_up(tokens, blocks, starts):
        return sum(
            dot(low(tokens[:, None] == (offsets + start)[None, :]), rows)
            for rows, start in zip(blocks, starts)
        )

    near_src, near_dec = (look_up(ids, near, firsts[:2]) for ids in (src_ids, dec_ids))
    far_rows, near_src, near_dec = lax.optimization_barrier((far_rows, near_src, near_dec))
    away = (far_rows, swap(far_rows, "core"))
    src_rows, dec_rows = (
        low(found + look_up(ids, away, firsts[2:])).reshape(count_z, 2, -1, D)
        for ids, found in ((src_ids, near_src), (dec_ids, near_dec))
    )
    table_blocks = near + away

    blanks = jnp.zeros((1, length_table.shape[1], D - LCLS - 7), jnp.bfloat16)
    misc = jnp.concatenate([low(length_table).T[None], low(norm_gains).T[None], blanks], axis=2)
    enc_pack = gather_weight(
        jnp.concatenate(
            [
                low(pack_ffn(ffn_expand[0], ffn_reduce[0])),
                low(pack_attn(attn_project[0], attn_output[0])),
                misc,
            ]
        )
    )
    dec_pack = gather_weight(
        jnp.concatenate(
            [
                low(pack_attn(attn_project[1], attn_output[1])),
                low(pack_attn(attn_project[2], attn_output[2])),
                low(pack_ffn(ffn_expand[1], ffn_reduce[1])),
            ]
        )
    )
    plain = count_z != 4
    enc_ffn, dec_ffn = ((enc_pack, 8, 0), (dec_pack, 8, 1))
    if plain:
        enc_ffn = down_in_order(enc_pack, count_dp)
        dec_ffn = down_in_order(dec_pack[8:], count_dp)
    table = enc_pack[12, :, :LCLS].T
    gain = enc_pack[12, :, LCLS : LCLS + 7].T.astype(jnp.float32)
    scale_in = math.sqrt(D)
    class_ids = jnp.arange(LCLS, dtype=jnp.int32)
    sentence_ids = jnp.arange(SENTS, dtype=jnp.int32)

    src_part = add_vocab(src_rows)
    dec_part = scatter_line(dec_rows)
    src_part, dec_part = lax.optimization_barrier((src_part, dec_part))
    src_emb = scatter_line(src_part)
    dec_rows = add_vocab(dec_part)
    dec_emb = jnp.concatenate(
        [
            jnp.broadcast_to(dec_rows[ROW - MASKED][None], (MASKED, D)),
            dec_rows[: ROW - MASKED],
        ]
    )
    src_column, src_row = (segments[:, None], segments[None, :])
    tgt_column, tgt_row = (tsegs[:, None], tsegs[None, :])
    mega = 10**6
    x0 = scale_in * src_emb + position
    x1, x2, enc_top, *enc_attn_kept, enc_hidden = run(
        functools.partial(enc_fwd_kernel, plain), (FULL, FULL, FULL, HALF, HALF, HALF, HALF, HIDDEN),
        x0, gain, (enc_pack, 4, 2), enc_ffn, src_column, src_row, down=1, flops=1800 * mega,
    )
    y0 = scale_in * dec_emb + dec_position
    y1, *self_kept = run(
        dec_self_kernel, (FULL, HALF, HALF, HALF, HALF),
        y0, gain, (dec_pack, 4, 0), tgt_column, tgt_row, flops=700 * mega,
    )
    y2, y3, dec_top, *cross_kept, dec_hidden = run(
        functools.partial(dec_rest_kernel, plain), (FULL, FULL, FULL, HALF, HALF, HALF, HALF, HIDDEN),
        y1, enc_top, gain, (dec_pack, 4, 1), dec_ffn, tgt_column, src_row, down=1, flops=1800 * mega,
    )

    tops = gather_group(low(dec_top[:MASKED]))
    many = tops.shape[0]

    def rows_of(kind):
        return jax.ShapeDtypeStruct((shard, D), kind)

    column = jax.ShapeDtypeStruct((many, 1), jnp.float32)
    goal_column = goal_ids[:, None]
    peak, total, picked = run(
        head_fwd_kernel, (column, column, column),
        tops, goal_column, first_ids, *table_blocks, flops=8 * many * D * shard,
    )
    totals = jnp.stack([turn(part.reshape(count_z, 2, MASKED)) for part in (peak, total)])
    totals = butterfly(totals, join_totals, ("vocab", "z"))
    log_total = turn(totals[0] + jnp.log(totals[1])).reshape(-1)
    grad_rows, *grad_blocks = run(
        functools.partial(head_back_kernel, inverse),
        [jax.ShapeDtypeStruct((many, D), jnp.bfloat16)] + [rows_of(jnp.float32)] * 4,
        tops, goal_column, log_total[:, None], first_ids, *table_blocks,
        total=many, flops=24 * many * D * shard,
    )
    grad_rows = scatter_group(grad_rows.reshape(count_z, 2, MASKED, D))
    grad_top = jnp.concatenate([grad_rows, jnp.zeros((ROW - MASKED, D), jnp.float32)])

    member = (segments[None, :] == sentence_ids[:, None]).astype(jnp.float32)
    members = jnp.sum(member, axis=1, keepdims=True)
    pooled_low = low(jnp.dot(member, enc_top, precision=HIGHEST) / members)
    length_logits = jnp.einsum("sd,cd->sc", pooled_low, table, preferred_element_type=jnp.float32)
    length_total = jax.nn.logsumexp(length_logits, axis=1)
    class_hot = (lengths[:, None] - 1 == class_ids[None, :]).astype(jnp.float32)
    length_loss = length_total - jnp.sum(length_logits * class_hot, axis=1)
    loss_local = jnp.sum(log_total[:MASKED]) - jnp.sum(picked) + LENGTH_WEIGHT * jnp.sum(length_loss)
    grad_length = low(
        (jnp.exp(length_logits - length_total[:, None]) - class_hot) * (LENGTH_WEIGHT * inverse)
    )
    grad_table = jnp.einsum("sc,sd->dc", grad_length, pooled_low, preferred_element_type=jnp.float32)
    grad_pooled = jnp.einsum("sc,cd->sd", grad_length, table, preferred_element_type=jnp.float32)
    grad_enc = jnp.dot(member.T, grad_pooled / members, precision=HIGHEST)

    core_only = jnp.full((count_z,), core, jnp.int32)
    grad_stream, mine_dec, theirs_dec, dec_ffn_gain = run(
        functools.partial(ffn_back_kernel, 5, plain),
        (FULL, (halves_of(16), 8, 1), (halves_of(16), 8, 1), gains_of(2)),
        grad_top, y3, y2, dec_hidden, gain, dec_ffn, core_only, down=1, flops=2200 * mega,
    )
    grad_stream, memory_grad, mine_dec, theirs_dec, cross_gain = run(
        functools.partial(cross_back_kernel, 4),
        (FULL, FULL, (halves_of(16), 4, 1), (halves_of(16), 4, 1), gains_of(1)),
        grad_stream, y1, enc_top, *cross_kept, gain, (dec_pack, 4, 1), tgt_column, src_row,
        core_only, held=((mine_dec, 2), (theirs_dec, 3)), scratch=4, flops=1500 * mega,
    )
    dec_stream, mine_dec, theirs_dec, self_gain = run(
        functools.partial(self_back_kernel, 3),
        (FULL, (halves_of(16), 4, 0), (halves_of(16), 4, 0), gains_of(1)),
        grad_stream, y0, *self_kept, gain, (dec_pack, 4, 0), tgt_column, tgt_row,
        core_only, held=((mine_dec, 1), (theirs_dec, 2)), scratch=4, flops=1500 * mega,
    )
    sent = wide(low(scale_in * dec_stream))
    blank_sum = jnp.sum(sent[:MASKED], axis=0, keepdims=True)
    blank_high = low(blank_sum)
    blank_rest = low(blank_sum - wide(blank_high))
    sent = jnp.concatenate(
        [low(sent[MASKED:]), blank_high, blank_rest, jnp.zeros((14, D), jnp.bfloat16)]
    )
    again = jnp.where(jnp.arange(few) == ROW - MASKED + 1, MASK_TOKEN, 0).astype(jnp.int32)
    back_ids = jnp.where(again[None] > 0, again[None], dec_ids.reshape(-1, few)).reshape(-1)
    hold = lax.optimization_barrier
    if plain:
        whole = jnp.concatenate([mine_dec, theirs_dec], axis=1)
        whole = jnp.concatenate([whole[:8], down_in_packs(whole[8:], count_dp)])
        mine_dec, theirs_dec = jnp.split(whole, 2, axis=1)
    mine_dec, theirs_dec = swap_core(mine_dec, theirs_dec)
    dec_pair = pair_vocab(sent)
    grad_stream, mine_enc, theirs_enc, enc_ffn_gain = run(
        functools.partial(ffn_back_kernel, 1, plain),
        (FULL, (halves_of(13), 8, 0), (halves_of(13), 8, 0), gains_of(2)),
        grad_enc + memory_grad, x2, x1, enc_hidden, gain, enc_ffn, core_only,
        down=1, flops=2200 * mega,
    )
    grad_stream, dec_pair, mine_dec, theirs_dec = hold(
        (grad_stream, dec_pair, mine_dec, theirs_dec)
    )
    mine_dec, theirs_dec = add_vocab_parts(mine_dec, theirs_dec)
    dec_near = ring_first(dec_pair)
    enc_stream, mine_enc, theirs_enc, enc_attn_gain = run(
        functools.partial(self_back_kernel, 0),
        (FULL, (halves_of(13), 4, 2), (halves_of(13), 4, 2), gains_of(1)),
        grad_stream, x0, *enc_attn_kept, gain, (enc_pack, 4, 2), src_column, src_row,
        core_only, held=((mine_enc, 1), (theirs_enc, 2)), scratch=4, flops=1500 * mega,
    )
    grad_gain = jnp.concatenate(
        [enc_attn_gain, enc_ffn_gain, self_gain, cross_gain, dec_ffn_gain]
    ).T
    grad_misc = jnp.concatenate(
        [grad_table, grad_gain, jnp.zeros((D, D - LCLS - 7), jnp.float32)], axis=1
    )
    misc_parts = by_core(low(grad_misc)[None])
    if count_z != 4:
        misc_parts = jnp.split(low(grad_misc)[None], 2, axis=1)
    mine_enc, theirs_enc = (
        lax.dynamic_update_slice(part, misc_part, (12, 0, 0))
        for part, misc_part in zip((mine_enc, theirs_enc), misc_parts)
    )
    if plain:
        whole = jnp.concatenate([mine_enc, theirs_enc], axis=1)
        whole = jnp.concatenate([down_in_packs(whole[:8], count_dp), whole[8:]])
        mine_enc, theirs_enc = jnp.split(whole, 2, axis=1)
    mine_enc, theirs_enc = swap_core(mine_enc, theirs_enc)
    src_pair = pair_vocab(low(scale_in * enc_stream))
    dec_near, mine_enc, theirs_enc, src_pair, mine_dec, theirs_dec = hold(
        (dec_near, mine_enc, theirs_enc, src_pair, mine_dec, theirs_dec)
    )
    mine_enc, theirs_enc = add_side_parts(mine_enc, theirs_enc)
    dec_sent = ring_second(dec_pair, *dec_near)
    mine_enc, theirs_enc, dec_sent, src_pair, mine_dec, theirs_dec = hold(
        (mine_enc, theirs_enc, dec_sent, src_pair, mine_dec, theirs_dec)
    )
    theirs_dec = swap(theirs_dec, "vocab")
    theirs_enc = swap(theirs_enc, "y")
    src_near = ring_first(src_pair)
    grad_blocks = spread(
        (0, 1, 2, 3), [jnp.float32] * 4, back_ids, dec_sent, first_ids, grad_blocks
    )
    src_near, grad_blocks = hold((src_near, grad_blocks))
    src_sent = ring_second(src_pair, *src_near)
    mine_dec, theirs_dec, mine_enc, theirs_enc, src_sent, grad_blocks = hold(
        (mine_dec, theirs_dec, mine_enc, theirs_enc, src_sent, grad_blocks)
    )
    mine_dec, theirs_dec = add_side_parts(mine_dec, theirs_dec)
    theirs_dec = swap(theirs_dec, "y")
    enc_parts = line_parts(mine_enc, theirs_enc)
    enc_far = line_first(enc_parts)
    kinds = (jnp.float32, jnp.bfloat16)
    far_chip, far_sent = spread((2, 3), kinds, src_ids, src_sent, first_ids, grad_blocks[2:])
    far_back = swap(far_sent, "core")
    near_chip, near_sent = spread((0, 1), kinds, src_ids, src_sent, first_ids, grad_blocks[:2])
    near_back = swap(near_sent, "core")
    mine_dec, theirs_dec, far_back, near_back, enc_parts, enc_far = hold(
        (mine_dec, theirs_dec, far_back, near_back, enc_parts, enc_far)
    )
    far_chip = swap(low(far_chip + wide(far_back)), "y")
    dec_parts = line_parts(mine_dec, theirs_dec)
    dec_far = line_first(dec_parts)
    enc_line = line_second(enc_parts, enc_far)
    enc_line, dec_parts, dec_far, far_chip = hold((enc_line, dec_parts, dec_far, far_chip))
    dec_line = line_second(dec_parts, dec_far)
    sum_enc, enc_square = add_vocab_last(enc_line)
    dec_line, sum_enc, far_chip = hold((dec_line, sum_enc, far_chip))
    sum_dec, dec_square = join_vocab(dec_line)
    grad_embed = near_chip + wide(near_back) + wide(far_chip)
    layer_squares = dec_square + enc_square
    table_squares = jnp.sum(grad_embed * grad_embed)
    vocab_count = lax.axis_size("vocab")
    totals = butterfly(
        jnp.stack([layer_squares / vocab_count + table_squares, loss_local]),
        jnp.add,
        ("core", "vocab", "y", "z"),
    )
    squares, loss_sum = (totals[0], totals[1])
    grad_norm = jnp.sqrt(squares)
    factor = jnp.minimum(1.0, CLIP / grad_norm)
    rate = RATE_SCALE * math.sqrt(NPARAM / D) / CLIP
    layers = [
        item for k in range(4) for item in (masters[k], moments[k], averages[k])
    ]
    kinds = (jnp.float32, jnp.float32, jnp.float32, jnp.bfloat16)
    updated = run(
        functools.partial(update_kernel, RATE_FACTORS[:4]),
        [jax.ShapeDtypeStruct(masters[k].shape, kind) for k in range(4) for kind in kinds],
        factor[None], sum_dec, sum_enc, *layers,
    )
    results = [tuple(updated[4 * k : 4 * k + 4]) for k in range(4)]
    misc_sum = sum_enc[12]
    for k, grad in (
        (4, misc_sum[:, LCLS : LCLS + 7].T),
        (5, misc_sum[:, :LCLS].T),
        (6, grad_embed),
    ):
        clipped = grad * factor
        moment = MOMENTUM * moments[k] + clipped
        weight = masters[k] - RATE_FACTORS[k] * rate * (clipped + MOMENTUM * moment)
        average = KEEP * averages[k] + (1.0 - KEEP) * weight
        results.append((weight, moment, average, low(weight)))
    return (loss_sum, grad_norm) + tuple(result[k] for k in range(4) for result in results)


def solution(mesh):
    vocab = mesh.shape["vocab"]
    grid = Mesh(mesh.devices.reshape(-1, 2, 2, vocab), ("z", "y", "core", "vocab"))
    dp = ("z", "y", "core")
    return jax.shard_map(
        shards,
        mesh=grid,
        in_specs=(
            P(dp, None),
            P(dp, None),
            P(dp, None),
            P(dp, None),
            P(dp, None),
            P(None, dp, None),
            P(None, dp, None),
            P(None, dp, None),
            P(None, dp, None),
            P(None, dp),
            P(None, dp),
            P(("vocab",) + dp, None),
            P(None, dp, None),
            P(None, dp, None),
            P(None, dp, None),
            P(None, dp, None),
            P(None, dp),
            P(None, dp),
            P(("vocab",) + dp, None),
            P(None, dp, None),
            P(None, dp, None),
            P(None, dp, None),
            P(None, dp, None),
            P(None, dp),
            P(None, dp),
            P(("vocab",) + dp, None),
        ),
        out_specs=(
            P(),
            P(),
            P(None, dp, None),
            P(None, dp, None),
            P(None, dp, None),
            P(None, dp, None),
            P(None, dp),
            P(None, dp),
            P(("vocab",) + dp, None),
            P(None, dp, None),
            P(None, dp, None),
            P(None, dp, None),
            P(None, dp, None),
            P(None, dp),
            P(None, dp),
            P(("vocab",) + dp, None),
            P(None, dp, None),
            P(None, dp, None),
            P(None, dp, None),
            P(None, dp, None),
            P(None, dp),
            P(None, dp),
            P(("vocab",) + dp, None),
            P(None, dp, None),
            P(None, dp, None),
            P(None, dp, None),
            P(None, dp, None),
            P(None, dp),
            P(None, dp),
            P(("vocab",) + dp, None),
        ),
        check_vma=False,
    )
```

```python
import functools
import math

import jax
import jax.numpy as jnp
from jax import lax
from jax.experimental import pallas as pl
from jax.experimental.pallas import tpu as pltpu
from jax.sharding import Mesh
from jax.sharding import PartitionSpec as P

D = 512
HDIM = 64
LCLS = 256
ROW = 256
SENTS = 8
MASKED = 96
NPARAM = 23858688


HIGHEST = lax.Precision.HIGHEST
EPSILON = 1e-05
MASK_TOKEN = 3
MOMENTUM = 0.9
KEEP = 0.9
CLIP = 0.02
LENGTH_WEIGHT = 0.1
NEGATIVE = -1e30
RATE_SCALE = 0.25
RATE_FACTORS = (1.0, 1.0, 1.0, 1.0, 6.0, 24.0, 1.0)


def sinusoid(count, width):
    place = jnp.arange(count, dtype=jnp.float32)[:, None]
    index = jnp.arange(width // 2, dtype=jnp.float32)[None, :]
    angle = place * jnp.exp(-math.log(10000.0) * 2.0 * index / width)
    return jnp.concatenate([jnp.sin(angle), jnp.cos(angle)], axis=1)


SWAP = [(0, 1), (1, 0)]


def swap(value, axis):
    return lax.ppermute(value, axis, SWAP)


def shift(value, by):
    count = lax.axis_size("z")
    return lax.ppermute(value, "z", [(i, (i + by) % count) for i in range(count)])


def low(value):
    return value.astype(jnp.bfloat16)


def wide(value):
    return value.astype(jnp.float32)


def ring_first(value):
    if lax.axis_size("z") != 4:
        return value, value
    return shift(value, 1), shift(value, -1)


def ring_second(value, below, above):
    count = lax.axis_size("z")
    if count != 4:
        whole = lax.all_gather(value, "z", axis=0)
        here = lax.axis_index("z")
        return [lax.dynamic_index_in_dim(whole, (here - k) % count, 0, False) for k in range(count)]
    half = value.shape[0] // 2
    return [value, below, shift(below[:half], 1), shift(above[half:], -1), above]


def ring_gather(value):
    return ring_second(value, *ring_first(value))


def ring_scatter(blocks):
    count = lax.axis_size("z")
    if count != 4:
        here = lax.axis_index("z")
        order = (here - jnp.arange(count)) % count
        stacked = jnp.stack([low(block) for block in blocks])
        whole = jnp.zeros_like(stacked).at[order].set(stacked)
        return wide(lax.psum_scatter(whole, "z", scatter_dimension=0))
    half = blocks[0].shape[0] // 2
    from_above = shift(low(blocks[2][:half]), -1)
    from_below = shift(low(blocks[2][half:]), 1)
    down = jnp.concatenate([wide(blocks[1][:half]) + wide(from_above), wide(blocks[1][half:])])
    up = jnp.concatenate([wide(blocks[3][:half]), wide(blocks[3][half:]) + wide(from_below)])
    from_above = shift(low(down), -1)
    from_below = shift(low(up), 1)
    return wide(blocks[0]) + wide(from_above) + wide(from_below)


def gather_weight(value):
    size = value.shape[1] // lax.axis_size("vocab")
    part = lax.dynamic_slice_in_dim(value, lax.axis_index("vocab") * size, size, 1)
    return lax.all_gather(part, ("z", "y", "core", "vocab"), axis=1, tiled=True)


def take(value, index, axis):
    return lax.dynamic_index_in_dim(value, index, axis, False)


def add_swap(value):
    mine = low(value)
    return wide(mine) + wide(swap(mine, "vocab"))


def by_core(grads):
    core = lax.axis_index("core")
    count = lax.axis_size("z")
    parts = grads.reshape(grads.shape[0], count, 2, 2, -1, grads.shape[2])
    parts = parts.transpose(0, 3, 2, 1, 4, 5).reshape(grads.shape[0], 2, -1, grads.shape[2])
    return take(parts, core, 1), take(parts, 1 - core, 1)


def swap_core(mine, theirs):
    if lax.axis_size("z") != 4:
        mine, theirs = by_core(jnp.concatenate([mine, theirs], axis=1))
    return mine, swap(theirs, "core")


def low_sum(*refs):
    return low(sum(wide(ref[...]) for ref in refs))


def sums_kernel(at_ref, *refs):
    count = len(refs) // 3
    for k in range(count):
        refs[2 * count + k][...] = low_sum(refs[2 * k], refs[2 * k + 1])


def line_kernel(at_ref, *refs):
    own, down, far, up = (low_sum(refs[2 * k], refs[2 * k + 1]) for k in range(4))
    own_ref, down_ref, far_down_ref, far_up_ref, up_ref = refs[8:]
    own_ref[...] = own
    down_ref[...] = down
    up_ref[...] = up
    half = far.shape[2] // 2
    far_down_ref[...] = far[:, :, :half]
    far_up_ref[...] = far[:, :, half:]


def pass_kernel(down_ref, up_ref, above_ref, below_ref, down_out, up_out):
    half = above_ref.shape[2]
    down_out[:, :, :half] = low(wide(down_ref[:, :, :half]) + wide(above_ref[...]))
    down_out[:, :, half:] = down_ref[:, :, half:]
    up_out[:, :, :half] = up_ref[:, :, :half]
    up_out[:, :, half:] = low(wide(up_ref[:, :, half:]) + wide(below_ref[...]))


def three_kernel(one_ref, two_ref, three_ref, out_ref):
    out_ref[...] = low_sum(one_ref, two_ref, three_ref)


def two_kernel(one_ref, two_ref, out_ref, square_ref):
    total = wide(one_ref[...]) + wide(two_ref[...])
    out_ref[...] = total
    square_ref[0, 0] = jnp.sum(total * total)


def both_kernel(at_ref, mine_ref, theirs_ref, out_ref, square_ref):
    size = mine_ref.shape[0]
    mine, theirs = (wide(mine_ref[...]), wide(theirs_ref[...]))
    out_ref[pl.ds(at_ref[0] * size, size)] = mine
    out_ref[pl.ds((1 - at_ref[0]) * size, size)] = theirs
    square_ref[0, 0] = jnp.sum(mine * mine) + jnp.sum(theirs * theirs)


def staged(kernel, at, steps, block, mine, theirs, places, outs, out_place):
    def spec(place):
        return pl.BlockSpec(block, lambda i, at: place(i, at[0]))

    def out_spec(shape):
        return pl.BlockSpec(block[:2] + shape[2:], lambda i, at: out_place(i))

    return pl.pallas_call(
        kernel,
        grid_spec=pltpu.PrefetchScalarGridSpec(
            num_scalar_prefetch=1,
            grid=(steps,),
            in_specs=[spec(place) for place in places for _ in (0, 1)],
            out_specs=[out_spec(shape) for shape in outs],
        ),
        out_shape=[jax.ShapeDtypeStruct(shape, jnp.bfloat16) for shape in outs],
        compiler_params=pltpu.CompilerParams(vmem_limit_bytes=VMEM_BYTES),
    )(at[None].astype(jnp.int32), *([mine, theirs] * len(places)))


def add_vocab_parts(mine, theirs):
    blocks, rows, columns = mine.shape
    kept = (blocks // 2, rows, columns)
    steps = 2
    return staged(
        sums_kernel, lax.axis_index("vocab"), steps, (blocks // 2 // steps, rows, columns),
        mine, theirs,
        (lambda i, at: (at * steps + i, 0, 0), lambda i, at: ((1 - at) * steps + i, 0, 0)),
        (kept, kept), lambda i: (i, 0, 0),
    )


def add_side_parts(mine, theirs):
    blocks, rows, columns = mine.shape
    kept = (blocks, rows // 2, columns)
    steps = 2
    return staged(
        sums_kernel, lax.axis_index("y"), steps, (blocks, rows // 2 // steps, columns),
        mine, theirs,
        (lambda i, at: (0, at * steps + i, 0), lambda i, at: (0, (1 - at) * steps + i, 0)),
        (kept, kept), lambda i: (0, i, 0),
    )


def line_parts(mine, theirs):
    here, count = (lax.axis_index("z"), lax.axis_size("z"))
    blocks, rows, columns = mine.shape
    if count != 4:
        return low(wide(mine) + wide(theirs)).reshape(blocks, count, -1, columns)
    part = (blocks, rows // 4, columns)
    half = (blocks, rows // 4, columns // 2)
    places = [lambda i, at, k=k: (0, lax.rem(at - k + 4, 4), 0) for k in range(4)]
    return staged(
        line_kernel, here, 1, part, mine, theirs, places, (part, part, half, half, part),
        lambda i: (0, 0, 0),
    )


def line_first(parts):
    if lax.axis_size("z") != 4:
        return parts
    return shift(parts[2], -1), shift(parts[3], 1)


def line_second(parts, near):
    if lax.axis_size("z") != 4:
        return low(lax.psum_scatter(near, "z", scatter_dimension=1))
    own, down, _, _, up = parts
    down, up = run(pass_kernel, (down, up), down, up, *near)
    return run(three_kernel, (own,), own, shift(down, -1), shift(up, 1))[0]


SQUARE = jax.ShapeDtypeStruct((1, 1), jnp.float32)


def add_vocab_last(part):
    out = jax.ShapeDtypeStruct(part.shape, jnp.float32)
    total, square = run(two_kernel, (out, SQUARE), part, swap(part, "vocab"))
    return total, square[0, 0]


def join_vocab(part):
    out = jax.ShapeDtypeStruct((2 * part.shape[0],) + part.shape[1:], jnp.float32)
    half = lax.axis_index("vocab")[None].astype(jnp.int32)
    total, square = run(both_kernel, (out, SQUARE), half, part, swap(part, "vocab"))
    return total, square[0, 0]


def after(value, *others):
    return lax.optimization_barrier((value,) + others)[0]


def pair_vocab(value):
    return jnp.stack([value, swap(value, "vocab")])


def gather_group(value):
    pieces = ring_gather(pair_vocab(value))
    return jnp.concatenate([piece.reshape(-1, value.shape[-1]) for piece in pieces])


def gather_small(value):
    count = lax.axis_size("z")
    if count == 4:
        pieces = jnp.concatenate([value] + [shift(value, k) for k in range(1, count)])
    else:
        pieces = jnp.concatenate(ring_gather(value))
    return jnp.concatenate([pieces, swap(pieces, "vocab")])


def scatter_small(parts):
    held = wide(parts[0]) + wide(swap(parts[1], "vocab"))
    count = lax.axis_size("z")
    if count != 4:
        return scatter_line(low(held))
    return held[0] + sum(wide(shift(low(held[k]), -k)) for k in range(1, count))


def add_vocab(parts):
    return parts[..., 0, :, :] + swap(low(parts[..., 1, :, :]), "vocab")


def scatter_line(parts):
    return ring_scatter([parts[k] for k in range(parts.shape[0])])


def scatter_group(parts):
    return scatter_line(add_vocab(parts))


def butterfly(value, join, axes):
    for axis in axes:
        count = lax.axis_size(axis)
        step = 1
        while step < count:
            pairs = [(i, i ^ step) for i in range(count)]
            value = join(value, lax.ppermute(value, axis, pairs))
            step *= 2
    return value


def join_totals(left, right):
    peak = jnp.maximum(left[0], right[0])
    return jnp.stack(
        [peak, left[1] * jnp.exp(left[0] - peak) + right[1] * jnp.exp(right[0] - peak)]
    )


def join_line(totals):
    count = lax.axis_size("z")
    if count != 4:
        return butterfly(totals, join_totals, ("z",))
    joined = totals
    for k in range(1, count):
        joined = join_totals(joined, shift(totals, k))
    return joined


def turn(value):
    count = lax.axis_size("z")
    here, half = (lax.axis_index("z"), lax.axis_index("vocab"))
    value = jnp.where(half == 0, value, value[:, ::-1])
    backward = value[::-1]
    twice = jnp.concatenate([backward, backward])
    return lax.dynamic_slice_in_dim(twice, count - 1 - here, count, 0)


SCALE = HDIM ** (-0.5)
GELU_A = math.sqrt(2.0 / math.pi)
GELU_B = 0.044715


def dot(left, right):
    return jnp.dot(left, right, preferred_element_type=jnp.float32)


def dot_left(left, right):
    return lax.dot_general(left, right, (((0,), (0,)), ((), ())), preferred_element_type=jnp.float32)


def dot_right(left, right):
    return lax.dot_general(left, right, (((1,), (1,)), ((), ())), preferred_element_type=jnp.float32)


def norm_parts(stream):
    centred = stream - jnp.mean(stream, axis=-1, keepdims=True)
    inverse = lax.rsqrt(jnp.mean(centred * centred, axis=-1, keepdims=True) + EPSILON)
    return centred * inverse, inverse


def norm_back(grad, stream, gain):
    normed, inverse = norm_parts(stream)
    scaled = grad * gain
    through = scaled - jnp.mean(scaled, axis=-1, keepdims=True)
    through = through - normed * jnp.mean(scaled * normed, axis=-1, keepdims=True)
    return through * inverse, jnp.sum(grad * normed, axis=0, keepdims=True)


def gelu_parts(hidden):
    bend = jnp.tanh(GELU_A * (hidden + GELU_B * hidden * hidden * hidden))
    return bend, 0.5 * (1.0 + bend)


def lane_halves(kind):
    first = lax.broadcasted_iota(jnp.int32, (1, 2 * HDIM), 1) < HDIM
    ones = first.astype(jnp.float32)
    return first, (ones.astype(kind), (1.0 - ones).astype(kind))


def softmax_of(query, keys, allowed):
    scores = jnp.where(allowed, dot_right(query, keys) * SCALE, NEGATIVE)
    expo = jnp.exp(scores - jnp.max(scores, axis=-1, keepdims=True))
    return expo / jnp.sum(expo, axis=-1, keepdims=True)


def attend_inside(low_query, low_memory, w, allowed, q_ref, k_ref, v_ref, o_ref):
    q_ref[...] = low(dot(low_query, w[0]))
    k_ref[...] = low(dot(low_memory, w[1]))
    v_ref[...] = low(dot(low_memory, w[2]))
    first, keeps = lane_halves(jnp.bfloat16)
    for tile in range(0, D, 2 * HDIM):
        lanes = slice(tile, tile + 2 * HDIM)
        query, keys, values = (q_ref[:, lanes], k_ref[:, lanes], v_ref[:, lanes])
        outs = [
            dot(low(softmax_of(query * keep, keys, allowed)), values) for keep in keeps
        ]
        o_ref[:, lanes] = low(jnp.where(first, outs[0], outs[1]))
    return dot(o_ref[...], w[3])


def down_blocks(w, plain, wd_ref):
    if plain:
        return [w[4 + j] for j in range(4)]
    rows = D // 16
    for place in range(16):
        for j in range(4):
            start = (place % 4) * 4 * rows + j * rows
            wd_ref[place // 4, start : start + rows] = w[4 + j, place * rows : (place + 1) * rows]
    return [wd_ref[j] for j in range(4)]


def ffn_inside(normed, w, plain, h_ref, wd_ref):
    branch = None
    down = down_blocks(w, plain, wd_ref)
    for j in range(4):
        hidden = dot(normed, w[j])
        h_ref[j] = hidden
        part = dot(low(hidden * gelu_parts(hidden)[1]), down[j])
        branch = part if branch is None else branch + part
    return branch


def store_split(core_ref, mine_ref, theirs_ref, j, value):
    value = low(value)
    count = core_ref.shape[0]
    step = D // (4 * count)
    if count != 4:
        mine_ref[j] = value[: D // 2]
        theirs_ref[j] = value[D // 2 :]
        return
    upper, lower = (
        jnp.concatenate(
            [
                value[((z * 2 + y) * 2 + c) * step : ((z * 2 + y) * 2 + c + 1) * step]
                for y in (0, 1)
                for z in range(count)
            ]
        )
        for c in (0, 1)
    )
    first = core_ref[0] == 0
    mine_ref[j] = jnp.where(first, upper, lower)
    theirs_ref[j] = jnp.where(first, lower, upper)


def enc_fwd_kernel(plain, x_ref, gain_ref, wa_ref, wf_ref, sc_ref, sr_ref, x1_ref, x2_ref, top_ref, q_ref, k_ref, v_ref, o_ref, h_ref, *wd):
    allowed = sc_ref[...] == sr_ref[...]
    stream = x_ref[...]
    normed = low(norm_parts(stream)[0] * gain_ref[0:1])
    stream = stream + attend_inside(normed, normed, wa_ref, allowed, q_ref, k_ref, v_ref, o_ref)
    x1_ref[...] = stream
    normed = low(norm_parts(stream)[0] * gain_ref[1:2])
    stream = stream + ffn_inside(normed, wf_ref, plain, h_ref, *wd)
    x2_ref[...] = stream
    top_ref[...] = norm_parts(stream)[0] * gain_ref[2:3]


def dec_self_kernel(x_ref, gain_ref, w_ref, tc_ref, tr_ref, y1_ref, q_ref, k_ref, v_ref, o_ref):
    stream = x_ref[...]
    normed = low(norm_parts(stream)[0] * gain_ref[3:4])
    branch = attend_inside(
        normed, normed, w_ref, tc_ref[...] == tr_ref[...], q_ref, k_ref, v_ref, o_ref
    )
    y1_ref[...] = stream + branch


def dec_rest_kernel(plain, y1_ref, mem_ref, gain_ref, wa_ref, wf_ref, tc_ref, sr_ref, y2_ref, y3_ref, top_ref, q_ref, k_ref, v_ref, o_ref, h_ref, *wd):
    stream = y1_ref[...]
    normed = low(norm_parts(stream)[0] * gain_ref[4:5])
    memory = low(mem_ref[...])
    stream = stream + attend_inside(
        normed, memory, wa_ref, tc_ref[...] == sr_ref[...], q_ref, k_ref, v_ref, o_ref
    )
    y2_ref[...] = stream
    normed = low(norm_parts(stream)[0] * gain_ref[5:6])
    stream = stream + ffn_inside(normed, wf_ref, plain, h_ref, *wd)
    y3_ref[...] = stream
    top_ref[...] = norm_parts(stream)[0] * gain_ref[6:7]


def store_down(core_ref, mine_ref, theirs_ref, j, value):
    if core_ref.shape[0] != 4:
        store_split(core_ref, mine_ref, theirs_ref, 4 + j, value)
        return
    value = low(value)
    first = core_ref[0] == 0
    rows = D // 16
    for y in (0, 1):
        for part in range(4):
            upper, lower = (
                value[start : start + rows]
                for start in ((y * 2 + c) * 4 * rows + part * rows for c in (0, 1))
            )
            to = slice((y * 4 + j) * rows, (y * 4 + j + 1) * rows)
            mine_ref[4 + part, to] = jnp.where(first, upper, lower)
            theirs_ref[4 + part, to] = jnp.where(first, lower, upper)


def ffn_back_kernel(place, plain, grad_ref, end_ref, mid_ref, h_ref, gain_ref, w_ref, core_ref, out_ref, mine_ref, theirs_ref, dg_ref, *wd):
    grad_stream, end_gain = norm_back(grad_ref[...], end_ref[...], gain_ref[place + 1 : place + 2])
    grad_low = low(grad_stream)
    gain = gain_ref[place : place + 1]
    normed = low(norm_parts(mid_ref[...])[0] * gain)
    total = None
    down = down_blocks(w_ref, plain, *(wd or (None,)))
    for j in range(4):
        hidden = h_ref[j]
        bend, half = gelu_parts(hidden)
        store_down(core_ref, mine_ref, theirs_ref, j, dot_left(low(hidden * half), grad_low))
        slope = half + 0.5 * hidden * (1.0 - bend * bend) * GELU_A * (
            1.0 + 3.0 * GELU_B * hidden * hidden
        )
        grad_hidden = low(dot_right(grad_low, down[j]) * slope)
        store_split(core_ref, mine_ref, theirs_ref, j, dot_left(normed, grad_hidden))
        part = dot_right(grad_hidden, w_ref[j])
        total = part if total is None else total + part
    extra, mid_gain = norm_back(total, mid_ref[...], gain)
    out_ref[...] = grad_stream + extra
    dg_ref[...] = jnp.concatenate([mid_gain, end_gain], axis=0)


def attn_back_inside(grad_low, normed, memory, refs, w, allowed, dw_refs, scratch):
    q_ref, k_ref, v_ref, o_ref = refs
    do_ref, dq_ref, dk_ref, dv_ref = scratch
    store_split(*dw_refs, 3, dot_left(o_ref[...], grad_low))
    do_ref[...] = low(dot_right(grad_low, w[3]))
    first, keeps = lane_halves(jnp.bfloat16)
    for tile in range(0, D, 2 * HDIM):
        lanes = slice(tile, tile + 2 * HDIM)
        query, keys, values, grad_mixed = (
            ref[:, lanes] for ref in (q_ref, k_ref, v_ref, do_ref)
        )
        found = []
        for keep in keeps:
            probs = softmax_of(query * keep, keys, allowed)
            grad_probs = dot_right(grad_mixed * keep, values)
            inner = jnp.sum(probs * grad_probs, axis=-1, keepdims=True)
            grad_scores = low(probs * (grad_probs - inner))
            found.append(
                (
                    dot(grad_scores, keys),
                    dot_left(grad_scores, query),
                    dot_left(low(probs), grad_mixed),
                )
            )
        dq_ref[:, lanes] = low(jnp.where(first, found[0][0], found[1][0]) * SCALE)
        dk_ref[:, lanes] = low(jnp.where(first, found[0][1], found[1][1]) * SCALE)
        dv_ref[:, lanes] = low(jnp.where(first, found[0][2], found[1][2]))
    store_split(*dw_refs, 0, dot_left(normed, dq_ref[...]))
    store_split(*dw_refs, 1, dot_left(memory, dk_ref[...]))
    store_split(*dw_refs, 2, dot_left(memory, dv_ref[...]))
    grad_query = dot_right(dq_ref[...], w[0])
    grad_memory = dot_right(dk_ref[...], w[1]) + dot_right(dv_ref[...], w[2])
    return grad_query, grad_memory


def self_back_kernel(place, grad_ref, x_ref, q_ref, k_ref, v_ref, o_ref, gain_ref, w_ref, sc_ref, sr_ref, core_ref, held_ref, kept_ref, out_ref, mine_ref, theirs_ref, dg_ref, *scratch):
    gain = gain_ref[place : place + 1]
    normed = low(norm_parts(x_ref[...])[0] * gain)
    grad_query, grad_memory = attn_back_inside(
        low(grad_ref[...]), normed, normed, (q_ref, k_ref, v_ref, o_ref), w_ref,
        sc_ref[...] == sr_ref[...], (core_ref, mine_ref, theirs_ref), scratch,
    )
    extra, dg_ref[...] = norm_back(grad_query + grad_memory, x_ref[...], gain)
    out_ref[...] = grad_ref[...] + extra


def cross_back_kernel(place, grad_ref, x_ref, mem_ref, q_ref, k_ref, v_ref, o_ref, gain_ref, w_ref, sc_ref, sr_ref, core_ref, held_ref, kept_ref, out_ref, dmem_ref, mine_ref, theirs_ref, dg_ref, *scratch):
    gain = gain_ref[place : place + 1]
    normed = low(norm_parts(x_ref[...])[0] * gain)
    grad_query, dmem_ref[...] = attn_back_inside(
        low(grad_ref[...]), normed, low(mem_ref[...]), (q_ref, k_ref, v_ref, o_ref), w_ref,
        sc_ref[...] == sr_ref[...], (core_ref, mine_ref, theirs_ref), scratch,
    )
    extra, dg_ref[...] = norm_back(grad_query, x_ref[...], gain)
    out_ref[...] = grad_ref[...] + extra


def ids_along(first_ref, j, count, dim):
    shape = (1, count) if dim else (count, 1)
    return first_ref[j] + lax.broadcasted_iota(jnp.int32, shape, dim)


def head_fwd_kernel(top_ref, goal_ref, first_ref, *refs):
    blocks, (peak_ref, total_ref, pick_ref) = (refs[:4], refs[4:])
    peak_ref[...] = jnp.full(peak_ref.shape, NEGATIVE, jnp.float32)
    total_ref[...] = jnp.zeros(total_ref.shape, jnp.float32)
    pick_ref[...] = jnp.zeros(pick_ref.shape, jnp.float32)
    for j, block_ref in enumerate(blocks):
        logits = dot_right(top_ref[...], block_ref[...])
        hot = goal_ref[...] == ids_along(first_ref, j, block_ref.shape[0], 1)
        pick_ref[...] += jnp.sum(jnp.where(hot, logits, 0.0), axis=1, keepdims=True)
        peak = peak_ref[...]
        higher = jnp.maximum(peak, jnp.max(logits, axis=1, keepdims=True))
        total_ref[...] = total_ref[...] * jnp.exp(peak - higher) + jnp.sum(
            jnp.exp(logits - higher), axis=1, keepdims=True
        )
        peak_ref[...] = higher


def head_back_kernel(inverse, top_ref, goal_ref, log_ref, first_ref, *refs):
    blocks, (rows_ref, *grads_out, sum_ref) = (refs[:4], refs[4:])
    for j, block_ref in enumerate(blocks):
        logits = dot_right(top_ref[...], block_ref[...])
        hot = goal_ref[...] == ids_along(first_ref, j, block_ref.shape[0], 1)
        grads = low((jnp.exp(logits - log_ref[...]) - hot.astype(jnp.float32)) * inverse)
        rows = dot(grads, block_ref[...])
        sum_ref[...] = rows if j == 0 else sum_ref[...] + rows
        grads_out[j][...] = dot_left(grads, top_ref[...])
    rows_ref[...] = low(sum_ref[...])


def spread_kernel(picks, pieces, first_ref, ids_ref, *refs):
    count = len(picks)
    rows_refs, refs = (refs[:pieces], refs[pieces:])
    for j, base_ref, out_ref in zip(picks, refs[:count], refs[count:]):
        total = base_ref[...]
        start = 0
        for rows_ref in rows_refs:
            stop = start + rows_ref.shape[0]
            hot = ids_along(first_ref, j, base_ref.shape[0], 0) == ids_ref[:, start:stop]
            total = total + dot(hot.astype(jnp.bfloat16), rows_ref[...])
            start = stop
        out_ref[...] = total.astype(out_ref.dtype)


VMEM_BYTES = 38 * 2**20
FULL = jax.ShapeDtypeStruct((ROW, D), jnp.float32)
HALF = jax.ShapeDtypeStruct((ROW, D), jnp.bfloat16)
HIDDEN = jax.ShapeDtypeStruct((4, ROW, D), jnp.float32)


def halves_of(count):
    return jax.ShapeDtypeStruct((count, D // 2, D), jnp.bfloat16)


def gains_of(count):
    return jax.ShapeDtypeStruct((count, D), jnp.float32)


def spec_of(item):
    if item is None:
        return pl.BlockSpec(memory_space=pl.ANY)
    if isinstance(item, tuple):
        array, size, index = item
        shape, place = ((size,) + array.shape[1:], index)
    else:
        shape, place = (item.shape, 0)
    if len(shape) == 1 or shape == (1, 1):
        return pl.BlockSpec(memory_space=pltpu.SMEM)
    return pl.BlockSpec(shape, lambda i: (place,) + (0,) * (len(shape) - 1))


def run(kernel, outs, *operands, held=(), scratch=0, down=0, total=0, flops=0):
    arrays = [item[0] if isinstance(item, tuple) else item for item in operands]
    in_specs = [spec_of(item) for item in operands]
    shapes = [item[0] if isinstance(item, tuple) else item for item in outs]
    shapes = [jax.ShapeDtypeStruct(item.shape, item.dtype) for item in shapes]
    aliases = {}
    for array, place in held:
        aliases[len(arrays)] = place
        arrays.append(array)
        in_specs.append(spec_of(None))
    moved = sum(math.prod(x.shape) * x.dtype.itemsize for x in arrays + shapes)
    return pl.pallas_call(
        kernel,
        grid=(1,),
        out_shape=shapes,
        in_specs=in_specs,
        out_specs=[spec_of(item) for item in outs],
        input_output_aliases=aliases,
        scratch_shapes=[pltpu.VMEM((ROW, D), jnp.bfloat16)] * scratch
        + [pltpu.VMEM((4, D, D), jnp.bfloat16)] * down
        + [pltpu.VMEM((total, D), jnp.float32)] * (total > 0),
        compiler_params=pltpu.CompilerParams(vmem_limit_bytes=VMEM_BYTES),
        cost_estimate=pl.CostEstimate(flops=flops, bytes_accessed=moved, transcendentals=0),
    )(*arrays)


def spread(picks, kinds, ids, pieces, first_ids, bases):
    pieces = [piece.reshape(-1, D) for piece in pieces]
    return run(
        functools.partial(spread_kernel, picks, len(pieces)),
        [jax.ShapeDtypeStruct(base.shape, kind) for base, kind in zip(bases, kinds)],
        first_ids, ids[None], *pieces, *bases,
        flops=2 * len(picks) * ids.shape[0] * D * bases[0].shape[0],
    )


def pack_attn(project, output):
    width = output.shape[1]
    return jnp.stack([project[:, j * width : (j + 1) * width] for j in range(3)] + [output])


def pack_ffn(expand, reduce):
    rows, width = (expand.shape[0], reduce.shape[1])
    up = [expand[:, j * width : (j + 1) * width] for j in range(4)]
    return jnp.concatenate([jnp.stack(up), reduce.reshape(4, rows, width)])


def down_in_order(pack, count):
    parts = pack[4:8].reshape(4, count, -1, D).transpose(1, 0, 2, 3).reshape(4, D, D)
    return jnp.concatenate([pack[:4], parts])


def down_in_packs(grads, count):
    parts = grads[4:8].reshape(count, 4, -1, D).transpose(1, 0, 2, 3).reshape(4, D, D)
    return jnp.concatenate([grads[:4], parts])


def update_kernel(boosts, scalar_ref, dec_ref, enc_ref, *refs):
    factor = scalar_ref[0]
    packs = ((enc_ref, 8, 0), (dec_ref, 0, 8), (dec_ref, 4, None))
    rate = RATE_SCALE * math.sqrt(NPARAM / D) / CLIP

    def write(which, place, grad):
        weight, moment, average = (refs[3 * which + k][place] for k in range(3))
        outs = refs[12 + 4 * which : 16 + 4 * which]
        clipped = grad * factor
        moment = MOMENTUM * moment + clipped
        weight = weight - boosts[which] * rate * (clipped + MOMENTUM * moment)
        outs[0][place] = weight
        outs[1][place] = moment
        outs[2][place] = KEEP * average + (1.0 - KEEP) * weight
        outs[3][place] = low(weight)

    rows = enc_ref.shape[1]
    for layer, (pack_ref, attn, ffn) in enumerate(packs):
        for j in range(3):
            write(0, (layer, slice(None), slice(j * D, (j + 1) * D)), pack_ref[attn + j])
        write(1, (layer,), pack_ref[attn + 3])
        if ffn is None:
            continue
        for j in range(4):
            write(2, (layer, slice(None), slice(j * D, (j + 1) * D)), pack_ref[ffn + j])
            write(3, (layer, slice(j * rows, (j + 1) * rows)), pack_ref[ffn + 4 + j])


def shards(
    src_tokens,
    tgt_tokens,
    src_segments,
    tgt_lengths,
    mask_order,
    attn_project,
    attn_output,
    ffn_expand,
    ffn_reduce,
    norm_gains,
    length_table,
    embedding,
    momentum_attn_project,
    momentum_attn_output,
    momentum_ffn_expand,
    momentum_ffn_reduce,
    momentum_norm_gains,
    momentum_length_table,
    momentum_embedding,
    average_attn_project,
    average_attn_output,
    average_ffn_expand,
    average_ffn_reduce,
    average_norm_gains,
    average_length_table,
    average_embedding,
):
    masters = (
        attn_project,
        attn_output,
        ffn_expand,
        ffn_reduce,
        norm_gains,
        length_table,
        embedding,
    )
    moments = (
        momentum_attn_project,
        momentum_attn_output,
        momentum_ffn_expand,
        momentum_ffn_reduce,
        momentum_norm_gains,
        momentum_length_table,
        momentum_embedding,
    )
    averages = (
        average_attn_project,
        average_attn_output,
        average_ffn_expand,
        average_ffn_reduce,
        average_norm_gains,
        average_length_table,
        average_embedding,
    )
    count_z = lax.axis_size("z")
    here, side, core, half = (
        lax.axis_index("z"),
        lax.axis_index("y"),
        lax.axis_index("core"),
        lax.axis_index("vocab"),
    )
    rows_here = src_tokens.shape[0]
    count_dp = count_z * 4
    inverse = 1.0 / (SENTS * rows_here * count_dp)
    source, target, segments, lengths, order = (
        lax.dynamic_index_in_dim(array, half, 0, False)
        for array in (src_tokens, tgt_tokens, src_segments, tgt_lengths, mask_order)
    )
    shuffled = target[order]
    bounds = jnp.cumsum(lengths)
    tsegs = jnp.sum((order[:, None] >= bounds[None, :]).astype(jnp.int32), axis=1)
    position = sinusoid(ROW, D)
    dec_position = position[order]

    own_rows = low(embedding)
    shard = own_rows.shape[0]
    far_rows = swap(own_rows, "y")
    near = (own_rows, swap(own_rows, "core"))
    place = half * count_dp + here * 4
    firsts = [
        (place + at_side * 2 + at_core) * shard
        for at_side in (side, 1 - side)
        for at_core in (core, 1 - core)
    ]
    first_ids = jnp.stack(firsts).astype(jnp.int32)
    offsets = jnp.arange(shard, dtype=jnp.int32)

    few = ROW - MASKED + 16
    extra = jnp.where(jnp.arange(16) == 0, MASK_TOKEN, -1).astype(jnp.int32)
    group = count_z * 2
    numbers = jnp.concatenate([source, shuffled, extra])
    numbers = lax.all_to_all(
        jnp.broadcast_to(numbers[None], (group, 2 * ROW + 16)), ("z", "vocab"), 0, 0, tiled=True
    )
    numbers = turn(numbers.reshape(count_z, 2, -1)).reshape(group, -1)
    src_ids = numbers[:, :ROW].reshape(-1)
    goal_ids = numbers[:, ROW : ROW + MASKED].reshape(count_z, 2, MASKED)
    goal_ids = goal_ids.transpose(1, 0, 2).reshape(-1)
    dec_ids = numbers[:, ROW + MASKED :].reshape(-1)

    def look_up(tokens, blocks, starts):
        return sum(
            dot(low(tokens[:, None] == (offsets + start)[None, :]), rows)
            for rows, start in zip(blocks, starts)
        )

    near_src, near_dec = (look_up(ids, near, firsts[:2]) for ids in (src_ids, dec_ids))
    far_rows, near_src, near_dec = lax.optimization_barrier((far_rows, near_src, near_dec))
    away = (far_rows, swap(far_rows, "core"))
    src_rows, dec_rows = (
        low(found + look_up(ids, away, firsts[2:])).reshape(count_z, 2, -1, D)
        for ids, found in ((src_ids, near_src), (dec_ids, near_dec))
    )
    table_blocks = near + away

    blanks = jnp.zeros((1, length_table.shape[1], D - LCLS - 7), jnp.bfloat16)
    misc = jnp.concatenate([low(length_table).T[None], low(norm_gains).T[None], blanks], axis=2)
    pack = gather_weight(
        jnp.concatenate(
            [
                low(pack_ffn(ffn_expand[0], ffn_reduce[0])),
                low(pack_ffn(ffn_expand[1], ffn_reduce[1])),
                low(pack_attn(attn_project[0], attn_output[0])),
                low(pack_attn(attn_project[1], attn_output[1])),
                low(pack_attn(attn_project[2], attn_output[2])),
                misc,
            ]
        )
    )
    plain = count_z != 4
    enc_ffn, dec_ffn = ((pack, 8, 0), (pack, 8, 1))
    if plain:
        enc_ffn = down_in_order(pack[:8], count_dp)
        dec_ffn = down_in_order(pack[8:16], count_dp)
    table = pack[28, :, :LCLS].T
    gain = pack[28, :, LCLS : LCLS + 7].T.astype(jnp.float32)
    scale_in = math.sqrt(D)
    class_ids = jnp.arange(LCLS, dtype=jnp.int32)
    sentence_ids = jnp.arange(SENTS, dtype=jnp.int32)

    src_part = add_vocab(src_rows)
    dec_part = scatter_line(dec_rows)
    src_part, dec_part = lax.optimization_barrier((src_part, dec_part))
    src_emb = scatter_line(src_part)
    dec_rows = add_vocab(dec_part)
    dec_emb = jnp.concatenate(
        [
            jnp.broadcast_to(dec_rows[ROW - MASKED][None], (MASKED, D)),
            dec_rows[: ROW - MASKED],
        ]
    )
    src_column, src_row = (segments[:, None], segments[None, :])
    tgt_column, tgt_row = (tsegs[:, None], tsegs[None, :])
    mega = 10**6
    x0 = scale_in * src_emb + position
    x1, x2, enc_top, *enc_attn_kept, enc_hidden = run(
        functools.partial(enc_fwd_kernel, plain), (FULL, FULL, FULL, HALF, HALF, HALF, HALF, HIDDEN),
        x0, gain, (pack, 4, 4), enc_ffn, src_column, src_row, down=1, flops=1800 * mega,
    )
    y0 = scale_in * dec_emb + dec_position
    y1, *self_kept = run(
        dec_self_kernel, (FULL, HALF, HALF, HALF, HALF),
        y0, gain, (pack, 4, 5), tgt_column, tgt_row, flops=700 * mega,
    )
    y2, y3, dec_top, *cross_kept, dec_hidden = run(
        functools.partial(dec_rest_kernel, plain), (FULL, FULL, FULL, HALF, HALF, HALF, HALF, HIDDEN),
        y1, enc_top, gain, (pack, 4, 6), dec_ffn, tgt_column, src_row, down=1, flops=1800 * mega,
    )

    tops = gather_small(low(dec_top[:MASKED]))
    many = tops.shape[0]

    def rows_of(kind):
        return jax.ShapeDtypeStruct((shard, D), kind)

    column = jax.ShapeDtypeStruct((many, 1), jnp.float32)
    goal_column = goal_ids[:, None]
    peak, total, picked = run(
        head_fwd_kernel, (column, column, column),
        tops, goal_column, first_ids, *table_blocks, flops=8 * many * D * shard,
    )
    totals = jnp.stack([turn(part.reshape(2, count_z, MASKED).swapaxes(0, 1)) for part in (peak, total)])
    member = (segments[None, :] == sentence_ids[:, None]).astype(jnp.float32)
    members = jnp.sum(member, axis=1, keepdims=True)
    pooled_low = low(jnp.dot(member, enc_top, precision=HIGHEST) / members)
    length_logits = jnp.einsum("sd,cd->sc", pooled_low, table, preferred_element_type=jnp.float32)
    length_total = jax.nn.logsumexp(length_logits, axis=1)
    class_hot = (lengths[:, None] - 1 == class_ids[None, :]).astype(jnp.float32)
    length_loss = length_total - jnp.sum(length_logits * class_hot, axis=1)
    grad_length = low(
        (jnp.exp(length_logits - length_total[:, None]) - class_hot) * (LENGTH_WEIGHT * inverse)
    )
    grad_table = jnp.einsum("sc,sd->dc", grad_length, pooled_low, preferred_element_type=jnp.float32)
    grad_pooled = jnp.einsum("sc,cd->sd", grad_length, table, preferred_element_type=jnp.float32)
    grad_enc = jnp.dot(member.T, grad_pooled / members, precision=HIGHEST)

    totals, grad_enc, grad_table, length_loss = lax.optimization_barrier(
        (totals, grad_enc, grad_table, length_loss)
    )
    totals = join_line(butterfly(totals, join_totals, ("vocab",)))
    log_total = turn(totals[0] + jnp.log(totals[1])).swapaxes(0, 1).reshape(-1)
    grad_rows, *grad_blocks = run(
        functools.partial(head_back_kernel, inverse),
        [jax.ShapeDtypeStruct((many, D), jnp.bfloat16)] + [rows_of(jnp.float32)] * 4,
        tops, goal_column, log_total[:, None], first_ids, *table_blocks,
        total=many, flops=24 * many * D * shard,
    )
    grad_rows = scatter_small(grad_rows.reshape(2, count_z, MASKED, D))
    grad_top = jnp.concatenate([grad_rows, jnp.zeros((ROW - MASKED, D), jnp.float32)])

    loss_local = jnp.sum(log_total[:MASKED]) - jnp.sum(picked) + LENGTH_WEIGHT * jnp.sum(length_loss)
    core_only = jnp.full((count_z,), core, jnp.int32)
    grad_stream, mine_dec, theirs_dec, dec_ffn_gain = run(
        functools.partial(ffn_back_kernel, 5, plain),
        (FULL, (halves_of(16), 8, 1), (halves_of(16), 8, 1), gains_of(2)),
        grad_top, y3, y2, dec_hidden, gain, dec_ffn, core_only, down=1, flops=2200 * mega,
    )
    grad_stream, memory_grad, mine_dec, theirs_dec, cross_gain = run(
        functools.partial(cross_back_kernel, 4),
        (FULL, FULL, (halves_of(16), 4, 1), (halves_of(16), 4, 1), gains_of(1)),
        grad_stream, y1, enc_top, *cross_kept, gain, (pack, 4, 6), tgt_column, src_row,
        core_only, held=((mine_dec, 2), (theirs_dec, 3)), scratch=4, flops=1500 * mega,
    )
    dec_stream, mine_dec, theirs_dec, self_gain = run(
        functools.partial(self_back_kernel, 3),
        (FULL, (halves_of(16), 4, 0), (halves_of(16), 4, 0), gains_of(1)),
        grad_stream, y0, *self_kept, gain, (pack, 4, 5), tgt_column, tgt_row,
        core_only, held=((mine_dec, 1), (theirs_dec, 2)), scratch=4, flops=1500 * mega,
    )
    sent = wide(low(scale_in * dec_stream))
    blank_sum = jnp.sum(sent[:MASKED], axis=0, keepdims=True)
    blank_high = low(blank_sum)
    blank_rest = low(blank_sum - wide(blank_high))
    sent = jnp.concatenate(
        [low(sent[MASKED:]), blank_high, blank_rest, jnp.zeros((14, D), jnp.bfloat16)]
    )
    again = jnp.where(jnp.arange(few) == ROW - MASKED + 1, MASK_TOKEN, 0).astype(jnp.int32)
    back_ids = jnp.where(again[None] > 0, again[None], dec_ids.reshape(-1, few)).reshape(-1)
    hold = lax.optimization_barrier
    if plain:
        whole = jnp.concatenate([mine_dec, theirs_dec], axis=1)
        whole = jnp.concatenate([whole[:8], down_in_packs(whole[8:], count_dp)])
        mine_dec, theirs_dec = jnp.split(whole, 2, axis=1)
    mine_dec, theirs_dec = swap_core(mine_dec, theirs_dec)
    dec_pair = pair_vocab(sent)
    grad_stream, mine_enc, theirs_enc, enc_ffn_gain = run(
        functools.partial(ffn_back_kernel, 1, plain),
        (FULL, (halves_of(13), 8, 0), (halves_of(13), 8, 0), gains_of(2)),
        grad_enc + memory_grad, x2, x1, enc_hidden, gain, enc_ffn, core_only,
        down=1, flops=2200 * mega,
    )
    grad_stream, dec_pair, mine_dec, theirs_dec = hold(
        (grad_stream, dec_pair, mine_dec, theirs_dec)
    )
    mine_dec, theirs_dec = add_vocab_parts(mine_dec, theirs_dec)
    dec_near = ring_first(dec_pair)
    enc_stream, mine_enc, theirs_enc, enc_attn_gain = run(
        functools.partial(self_back_kernel, 0),
        (FULL, (halves_of(13), 4, 2), (halves_of(13), 4, 2), gains_of(1)),
        grad_stream, x0, *enc_attn_kept, gain, (pack, 4, 4), src_column, src_row,
        core_only, held=((mine_enc, 1), (theirs_enc, 2)), scratch=4, flops=1500 * mega,
    )
    grad_gain = jnp.concatenate(
        [enc_attn_gain, enc_ffn_gain, self_gain, cross_gain, dec_ffn_gain]
    ).T
    grad_misc = jnp.concatenate(
        [grad_table, grad_gain, jnp.zeros((D, D - LCLS - 7), jnp.float32)], axis=1
    )
    misc_parts = by_core(low(grad_misc)[None])
    if count_z != 4:
        misc_parts = jnp.split(low(grad_misc)[None], 2, axis=1)
    mine_enc, theirs_enc = (
        lax.dynamic_update_slice(part, misc_part, (12, 0, 0))
        for part, misc_part in zip((mine_enc, theirs_enc), misc_parts)
    )
    if plain:
        whole = jnp.concatenate([mine_enc, theirs_enc], axis=1)
        whole = jnp.concatenate([down_in_packs(whole[:8], count_dp), whole[8:]])
        mine_enc, theirs_enc = jnp.split(whole, 2, axis=1)
    mine_enc, theirs_enc = swap_core(mine_enc, theirs_enc)
    src_pair = pair_vocab(low(scale_in * enc_stream))
    dec_near, mine_enc, theirs_enc, src_pair, mine_dec, theirs_dec = hold(
        (dec_near, mine_enc, theirs_enc, src_pair, mine_dec, theirs_dec)
    )
    mine_enc, theirs_enc = add_side_parts(mine_enc, theirs_enc)
    dec_sent = ring_second(dec_pair, *dec_near)
    mine_enc, theirs_enc, dec_sent, src_pair, mine_dec, theirs_dec = hold(
        (mine_enc, theirs_enc, dec_sent, src_pair, mine_dec, theirs_dec)
    )
    theirs_dec = swap(theirs_dec, "vocab")
    theirs_enc = swap(theirs_enc, "y")
    src_near = ring_first(src_pair)
    grad_blocks = spread(
        (0, 1, 2, 3), [jnp.float32] * 4, back_ids, dec_sent, first_ids, grad_blocks
    )
    src_near, grad_blocks = hold((src_near, grad_blocks))
    src_sent = ring_second(src_pair, *src_near)
    mine_dec, theirs_dec, mine_enc, theirs_enc, src_sent, grad_blocks = hold(
        (mine_dec, theirs_dec, mine_enc, theirs_enc, src_sent, grad_blocks)
    )
    mine_dec, theirs_dec = add_side_parts(mine_dec, theirs_dec)
    theirs_dec = swap(theirs_dec, "y")
    enc_parts = line_parts(mine_enc, theirs_enc)
    enc_far = line_first(enc_parts)
    kinds = (jnp.float32, jnp.bfloat16)
    far_chip, far_sent = spread((2, 3), kinds, src_ids, src_sent, first_ids, grad_blocks[2:])
    far_back = swap(far_sent, "core")
    near_chip, near_sent = spread((0, 1), kinds, src_ids, src_sent, first_ids, grad_blocks[:2])
    near_back = swap(near_sent, "core")
    mine_dec, theirs_dec, far_back, near_back, enc_parts, enc_far = hold(
        (mine_dec, theirs_dec, far_back, near_back, enc_parts, enc_far)
    )
    far_chip = swap(low(far_chip + wide(far_back)), "y")
    dec_parts = line_parts(mine_dec, theirs_dec)
    dec_far = line_first(dec_parts)
    enc_line = line_second(enc_parts, enc_far)
    enc_line, dec_parts, dec_far, far_chip = hold((enc_line, dec_parts, dec_far, far_chip))
    dec_line = line_second(dec_parts, dec_far)
    sum_enc, enc_square = add_vocab_last(enc_line)
    dec_line, sum_enc, far_chip = hold((dec_line, sum_enc, far_chip))
    sum_dec, dec_square = join_vocab(dec_line)
    grad_embed = near_chip + wide(near_back) + wide(far_chip)
    layer_squares = dec_square + enc_square
    table_squares = jnp.sum(grad_embed * grad_embed)
    vocab_count = lax.axis_size("vocab")
    misc_sum = sum_enc[12]
    misc_sums = (misc_sum[:, LCLS : LCLS + 7].T, misc_sum[:, :LCLS].T)
    layer_squares, misc_sums = lax.optimization_barrier((layer_squares, misc_sums))
    totals = butterfly(
        jnp.stack([layer_squares / vocab_count + table_squares, loss_local]),
        jnp.add,
        ("core", "vocab", "y", "z"),
    )
    squares, loss_sum = (totals[0], totals[1])
    grad_norm = jnp.sqrt(squares)
    factor = jnp.minimum(1.0, CLIP / grad_norm)
    rate = RATE_SCALE * math.sqrt(NPARAM / D) / CLIP
    layers = [
        item for k in range(4) for item in (masters[k], moments[k], averages[k])
    ]
    kinds = (jnp.float32, jnp.float32, jnp.float32, jnp.bfloat16)
    updated = run(
        functools.partial(update_kernel, RATE_FACTORS[:4]),
        [jax.ShapeDtypeStruct(masters[k].shape, kind) for k in range(4) for kind in kinds],
        factor[None], sum_dec, sum_enc, *layers,
    )
    results = [tuple(updated[4 * k : 4 * k + 4]) for k in range(4)]
    for k, grad in (
        (4, misc_sums[0]),
        (5, misc_sums[1]),
        (6, grad_embed),
    ):
        clipped = grad * factor
        moment = MOMENTUM * moments[k] + clipped
        weight = masters[k] - RATE_FACTORS[k] * rate * (clipped + MOMENTUM * moment)
        average = KEEP * averages[k] + (1.0 - KEEP) * weight
        results.append((weight, moment, average, low(weight)))
    return (loss_sum, grad_norm) + tuple(result[k] for k in range(4) for result in results)


def solution(mesh):
    vocab = mesh.shape["vocab"]
    grid = Mesh(mesh.devices.reshape(-1, 2, 2, vocab), ("z", "y", "core", "vocab"))
    dp = ("z", "y", "core")
    return jax.shard_map(
        shards,
        mesh=grid,
        in_specs=(
            P(dp, None),
            P(dp, None),
            P(dp, None),
            P(dp, None),
            P(dp, None),
            P(None, dp, None),
            P(None, dp, None),
            P(None, dp, None),
            P(None, dp, None),
            P(None, dp),
            P(None, dp),
            P(("vocab",) + dp, None),
            P(None, dp, None),
            P(None, dp, None),
            P(None, dp, None),
            P(None, dp, None),
            P(None, dp),
            P(None, dp),
            P(("vocab",) + dp, None),
            P(None, dp, None),
            P(None, dp, None),
            P(None, dp, None),
            P(None, dp, None),
            P(None, dp),
            P(None, dp),
            P(("vocab",) + dp, None),
        ),
        out_specs=(
            P(),
            P(),
            P(None, dp, None),
            P(None, dp, None),
            P(None, dp, None),
            P(None, dp, None),
            P(None, dp),
            P(None, dp),
            P(("vocab",) + dp, None),
            P(None, dp, None),
            P(None, dp, None),
            P(None, dp, None),
            P(None, dp, None),
            P(None, dp),
            P(None, dp),
            P(("vocab",) + dp, None),
            P(None, dp, None),
            P(None, dp, None),
            P(None, dp, None),
            P(None, dp, None),
            P(None, dp),
            P(None, dp),
            P(("vocab",) + dp, None),
            P(None, dp, None),
            P(None, dp, None),
            P(None, dp, None),
            P(None, dp, None),
            P(None, dp),
            P(None, dp),
            P(("vocab",) + dp, None),
        ),
        check_vma=False,
    )
```

```python
import functools
import math

import jax
import jax.numpy as jnp
from jax import lax
from jax.experimental import pallas as pl
from jax.experimental.pallas import tpu as pltpu
from jax.sharding import Mesh
from jax.sharding import PartitionSpec as P

D = 512
HDIM = 64
LCLS = 256
ROW = 256
SENTS = 8
MASKED = 96
NPARAM = 23858688


HIGHEST = lax.Precision.HIGHEST
EPSILON = 1e-05
MASK_TOKEN = 3
MOMENTUM = 0.9
KEEP = 0.9
CLIP = 0.02
LENGTH_WEIGHT = 0.1
NEGATIVE = -1e30
RATE_SCALE = 0.25
RATE_FACTORS = (1.0, 1.0, 1.0, 1.0, 6.0, 24.0, 1.0)


def sinusoid(count, width):
    place = jnp.arange(count, dtype=jnp.float32)[:, None]
    index = jnp.arange(width // 2, dtype=jnp.float32)[None, :]
    angle = place * jnp.exp(-math.log(10000.0) * 2.0 * index / width)
    return jnp.concatenate([jnp.sin(angle), jnp.cos(angle)], axis=1)


SWAP = [(0, 1), (1, 0)]


def swap(value, axis):
    return lax.ppermute(value, axis, SWAP)


def shift(value, by):
    count = lax.axis_size("z")
    return lax.ppermute(value, "z", [(i, (i + by) % count) for i in range(count)])


def low(value):
    return value.astype(jnp.bfloat16)


def wide(value):
    return value.astype(jnp.float32)


def ring_first(value):
    if lax.axis_size("z") != 4:
        return value, value
    return shift(value, 1), shift(value, -1)


def ring_second(value, below, above):
    count = lax.axis_size("z")
    if count != 4:
        whole = lax.all_gather(value, "z", axis=0)
        here = lax.axis_index("z")
        return [lax.dynamic_index_in_dim(whole, (here - k) % count, 0, False) for k in range(count)]
    half = value.shape[0] // 2
    return [value, below, shift(below[:half], 1), shift(above[half:], -1), above]


def ring_gather(value):
    return ring_second(value, *ring_first(value))


def ring_scatter(blocks):
    count = lax.axis_size("z")
    if count != 4:
        here = lax.axis_index("z")
        order = (here - jnp.arange(count)) % count
        stacked = jnp.stack([low(block) for block in blocks])
        whole = jnp.zeros_like(stacked).at[order].set(stacked)
        return wide(lax.psum_scatter(whole, "z", scatter_dimension=0))
    half = blocks[0].shape[0] // 2
    from_above = shift(low(blocks[2][:half]), -1)
    from_below = shift(low(blocks[2][half:]), 1)
    down = jnp.concatenate([wide(blocks[1][:half]) + wide(from_above), wide(blocks[1][half:])])
    up = jnp.concatenate([wide(blocks[3][:half]), wide(blocks[3][half:]) + wide(from_below)])
    from_above = shift(low(down), -1)
    from_below = shift(low(up), 1)
    return wide(blocks[0]) + wide(from_above) + wide(from_below)


def gather_weight(value):
    size = value.shape[1] // lax.axis_size("vocab")
    part = lax.dynamic_slice_in_dim(value, lax.axis_index("vocab") * size, size, 1)
    return lax.all_gather(part, ("z", "y", "core", "vocab"), axis=1, tiled=True)


def take(value, index, axis):
    return lax.dynamic_index_in_dim(value, index, axis, False)


def add_swap(value):
    mine = low(value)
    return wide(mine) + wide(swap(mine, "vocab"))


def by_core(grads):
    core = lax.axis_index("core")
    count = lax.axis_size("z")
    parts = grads.reshape(grads.shape[0], count, 2, 2, -1, grads.shape[2])
    parts = parts.transpose(0, 3, 2, 1, 4, 5).reshape(grads.shape[0], 2, -1, grads.shape[2])
    return take(parts, core, 1), take(parts, 1 - core, 1)


def swap_core(mine, theirs):
    if lax.axis_size("z") != 4:
        mine, theirs = by_core(jnp.concatenate([mine, theirs], axis=1))
    return mine, swap(theirs, "core")


def low_sum(*refs):
    return low(sum(wide(ref[...]) for ref in refs))


def sums_kernel(at_ref, *refs):
    count = len(refs) // 3
    for k in range(count):
        refs[2 * count + k][...] = low_sum(refs[2 * k], refs[2 * k + 1])


def line_kernel(at_ref, *refs):
    own, down, far, up = (low_sum(refs[2 * k], refs[2 * k + 1]) for k in range(4))
    own_ref, down_ref, far_down_ref, far_up_ref, up_ref = refs[8:]
    own_ref[...] = own
    down_ref[...] = down
    up_ref[...] = up
    half = far.shape[2] // 2
    far_down_ref[...] = far[:, :, :half]
    far_up_ref[...] = far[:, :, half:]


def pass_kernel(down_ref, up_ref, above_ref, below_ref, down_out, up_out):
    half = above_ref.shape[2]
    down_out[:, :, :half] = low(wide(down_ref[:, :, :half]) + wide(above_ref[...]))
    down_out[:, :, half:] = down_ref[:, :, half:]
    up_out[:, :, :half] = up_ref[:, :, :half]
    up_out[:, :, half:] = low(wide(up_ref[:, :, half:]) + wide(below_ref[...]))


def three_kernel(one_ref, two_ref, three_ref, out_ref):
    out_ref[...] = low_sum(one_ref, two_ref, three_ref)


def two_kernel(one_ref, two_ref, out_ref, square_ref):
    total = wide(one_ref[...]) + wide(two_ref[...])
    out_ref[...] = total
    square_ref[0, 0] = jnp.sum(total * total)


def both_kernel(at_ref, mine_ref, theirs_ref, out_ref, square_ref):
    size = mine_ref.shape[0]
    mine, theirs = (wide(mine_ref[...]), wide(theirs_ref[...]))
    out_ref[pl.ds(at_ref[0] * size, size)] = mine
    out_ref[pl.ds((1 - at_ref[0]) * size, size)] = theirs
    square_ref[0, 0] = jnp.sum(mine * mine) + jnp.sum(theirs * theirs)


def embed_kernel(boost, scalar_ref, near_ref, back_ref, far_ref, weight_ref, moment_ref, average_ref, *outs):
    rate = RATE_SCALE * math.sqrt(NPARAM / D) / CLIP
    clipped = (near_ref[...] + wide(back_ref[...]) + wide(far_ref[...])) * scalar_ref[0]
    moment = MOMENTUM * moment_ref[...] + clipped
    weight = weight_ref[...] - boost * rate * (clipped + MOMENTUM * moment)
    outs[0][...] = weight
    outs[1][...] = moment
    outs[2][...] = KEEP * average_ref[...] + (1.0 - KEEP) * weight
    outs[3][...] = low(weight)


def update_rows(boost, factor, *arrays):
    rows = arrays[-1].shape[0]
    block = pl.BlockSpec((rows, 128), lambda i: (0, i))
    kinds = (jnp.float32, jnp.float32, jnp.float32, jnp.bfloat16)
    return pl.pallas_call(
        functools.partial(embed_kernel, boost),
        grid=(D // 128,),
        out_shape=[jax.ShapeDtypeStruct((rows, D), kind) for kind in kinds],
        in_specs=[pl.BlockSpec(memory_space=pltpu.SMEM)] + [block] * len(arrays),
        out_specs=[block] * 4,
        compiler_params=pltpu.CompilerParams(vmem_limit_bytes=VMEM_BYTES),
    )(factor[None], *arrays)


def staged(kernel, at, steps, block, mine, theirs, places, outs, out_place):
    def spec(place):
        return pl.BlockSpec(block, lambda i, at: place(i, at[0]))

    def out_spec(shape):
        return pl.BlockSpec(block[:2] + shape[2:], lambda i, at: out_place(i))

    return pl.pallas_call(
        kernel,
        grid_spec=pltpu.PrefetchScalarGridSpec(
            num_scalar_prefetch=1,
            grid=(steps,),
            in_specs=[spec(place) for place in places for _ in (0, 1)],
            out_specs=[out_spec(shape) for shape in outs],
        ),
        out_shape=[jax.ShapeDtypeStruct(shape, jnp.bfloat16) for shape in outs],
        compiler_params=pltpu.CompilerParams(vmem_limit_bytes=VMEM_BYTES),
    )(at[None].astype(jnp.int32), *([mine, theirs] * len(places)))


def add_vocab_parts(mine, theirs):
    blocks, rows, columns = mine.shape
    kept = (blocks // 2, rows, columns)
    steps = 2
    return staged(
        sums_kernel, lax.axis_index("vocab"), steps, (blocks // 2 // steps, rows, columns),
        mine, theirs,
        (lambda i, at: (at * steps + i, 0, 0), lambda i, at: ((1 - at) * steps + i, 0, 0)),
        (kept, kept), lambda i: (i, 0, 0),
    )


def add_side_parts(mine, theirs):
    blocks, rows, columns = mine.shape
    kept = (blocks, rows // 2, columns)
    steps = 2
    return staged(
        sums_kernel, lax.axis_index("y"), steps, (blocks, rows // 2 // steps, columns),
        mine, theirs,
        (lambda i, at: (0, at * steps + i, 0), lambda i, at: (0, (1 - at) * steps + i, 0)),
        (kept, kept), lambda i: (0, i, 0),
    )


def line_parts(mine, theirs):
    here, count = (lax.axis_index("z"), lax.axis_size("z"))
    blocks, rows, columns = mine.shape
    if count != 4:
        return low(wide(mine) + wide(theirs)).reshape(blocks, count, -1, columns)
    part = (blocks, rows // 4, columns)
    half = (blocks, rows // 4, columns // 2)
    places = [lambda i, at, k=k: (0, lax.rem(at - k + 4, 4), 0) for k in range(4)]
    return staged(
        line_kernel, here, 1, part, mine, theirs, places, (part, part, half, half, part),
        lambda i: (0, 0, 0),
    )


def line_first(parts):
    if lax.axis_size("z") != 4:
        return parts
    return shift(parts[2], -1), shift(parts[3], 1)


def line_second(parts, near):
    if lax.axis_size("z") != 4:
        return low(lax.psum_scatter(near, "z", scatter_dimension=1))
    own, down, _, _, up = parts
    down, up = run(pass_kernel, (down, up), down, up, *near)
    return run(three_kernel, (own,), own, shift(down, -1), shift(up, 1))[0]


SQUARE = jax.ShapeDtypeStruct((1, 1), jnp.float32)


def add_vocab_last(part):
    out = jax.ShapeDtypeStruct(part.shape, jnp.float32)
    total, square = run(two_kernel, (out, SQUARE), part, swap(part, "vocab"))
    return total, square[0, 0]


def join_vocab(part):
    out = jax.ShapeDtypeStruct((2 * part.shape[0],) + part.shape[1:], jnp.float32)
    half = lax.axis_index("vocab")[None].astype(jnp.int32)
    total, square = run(both_kernel, (out, SQUARE), half, part, swap(part, "vocab"))
    return total, square[0, 0]


def after(value, *others):
    return lax.optimization_barrier((value,) + others)[0]


def pair_vocab(value):
    return jnp.stack([value, swap(value, "vocab")])


def gather_group(value):
    pieces = ring_gather(pair_vocab(value))
    return jnp.concatenate([piece.reshape(-1, value.shape[-1]) for piece in pieces])


def gather_small(value):
    count = lax.axis_size("z")
    if count == 4:
        pieces = jnp.concatenate([value] + [shift(value, k) for k in range(1, count)])
    else:
        pieces = jnp.concatenate(ring_gather(value))
    return jnp.concatenate([pieces, swap(pieces, "vocab")])


def scatter_small(parts):
    held = wide(parts[0]) + wide(swap(parts[1], "vocab"))
    count = lax.axis_size("z")
    if count != 4:
        return scatter_line(low(held))
    return held[0] + sum(wide(shift(low(held[k]), -k)) for k in range(1, count))


def add_vocab(parts):
    return parts[..., 0, :, :] + swap(low(parts[..., 1, :, :]), "vocab")


def scatter_line(parts):
    return ring_scatter([parts[k] for k in range(parts.shape[0])])


def scatter_group(parts):
    return scatter_line(add_vocab(parts))


def butterfly(value, join, axes):
    for axis in axes:
        count = lax.axis_size(axis)
        step = 1
        while step < count:
            pairs = [(i, i ^ step) for i in range(count)]
            value = join(value, lax.ppermute(value, axis, pairs))
            step *= 2
    return value


def join_totals(left, right):
    peak = jnp.maximum(left[0], right[0])
    return jnp.stack(
        [peak, left[1] * jnp.exp(left[0] - peak) + right[1] * jnp.exp(right[0] - peak)]
    )


def join_line(totals):
    count = lax.axis_size("z")
    if count != 4:
        return butterfly(totals, join_totals, ("z",))
    joined = totals
    for k in range(1, count):
        joined = join_totals(joined, shift(totals, k))
    return joined


def turn(value):
    count = lax.axis_size("z")
    here, half = (lax.axis_index("z"), lax.axis_index("vocab"))
    value = jnp.where(half == 0, value, value[:, ::-1])
    backward = value[::-1]
    twice = jnp.concatenate([backward, backward])
    return lax.dynamic_slice_in_dim(twice, count - 1 - here, count, 0)


SCALE = HDIM ** (-0.5)
GELU_A = math.sqrt(2.0 / math.pi)
GELU_B = 0.044715


def dot(left, right):
    return jnp.dot(left, right, preferred_element_type=jnp.float32)


def dot_left(left, right):
    return lax.dot_general(left, right, (((0,), (0,)), ((), ())), preferred_element_type=jnp.float32)


def dot_right(left, right):
    return lax.dot_general(left, right, (((1,), (1,)), ((), ())), preferred_element_type=jnp.float32)


def norm_parts(stream):
    centred = stream - jnp.mean(stream, axis=-1, keepdims=True)
    inverse = lax.rsqrt(jnp.mean(centred * centred, axis=-1, keepdims=True) + EPSILON)
    return centred * inverse, inverse


def norm_back(grad, stream, gain):
    normed, inverse = norm_parts(stream)
    scaled = grad * gain
    through = scaled - jnp.mean(scaled, axis=-1, keepdims=True)
    through = through - normed * jnp.mean(scaled * normed, axis=-1, keepdims=True)
    return through * inverse, jnp.sum(grad * normed, axis=0, keepdims=True)


def gelu_parts(hidden):
    bend = jnp.tanh(GELU_A * (hidden + GELU_B * hidden * hidden * hidden))
    return bend, 0.5 * (1.0 + bend)


def lane_halves(kind):
    first = lax.broadcasted_iota(jnp.int32, (1, 2 * HDIM), 1) < HDIM
    ones = first.astype(jnp.float32)
    return first, (ones.astype(kind), (1.0 - ones).astype(kind))


def softmax_of(query, keys, allowed):
    scores = jnp.where(allowed, dot_right(query, keys) * SCALE, NEGATIVE)
    expo = jnp.exp(scores - jnp.max(scores, axis=-1, keepdims=True))
    return expo / jnp.sum(expo, axis=-1, keepdims=True)


def attend_inside(low_query, low_memory, w, allowed, q_ref, k_ref, v_ref, o_ref):
    q_ref[...] = low(dot(low_query, w[0]))
    k_ref[...] = low(dot(low_memory, w[1]))
    v_ref[...] = low(dot(low_memory, w[2]))
    first, keeps = lane_halves(jnp.bfloat16)
    for tile in range(0, D, 2 * HDIM):
        lanes = slice(tile, tile + 2 * HDIM)
        query, keys, values = (q_ref[:, lanes], k_ref[:, lanes], v_ref[:, lanes])
        outs = [
            dot(low(softmax_of(query * keep, keys, allowed)), values) for keep in keeps
        ]
        o_ref[:, lanes] = low(jnp.where(first, outs[0], outs[1]))
    return dot(o_ref[...], w[3])


def down_blocks(w, plain, wd_ref):
    if plain:
        return [w[4 + j] for j in range(4)]
    rows = D // 16
    for place in range(16):
        for j in range(4):
            start = (place % 4) * 4 * rows + j * rows
            wd_ref[place // 4, start : start + rows] = w[4 + j, place * rows : (place + 1) * rows]
    return [wd_ref[j] for j in range(4)]


def ffn_inside(normed, w, plain, h_ref, wd_ref):
    branch = None
    down = down_blocks(w, plain, wd_ref)
    for j in range(4):
        hidden = dot(normed, w[j])
        h_ref[j] = hidden
        part = dot(low(hidden * gelu_parts(hidden)[1]), down[j])
        branch = part if branch is None else branch + part
    return branch


def store_split(core_ref, mine_ref, theirs_ref, j, value):
    value = low(value)
    count = core_ref.shape[0]
    step = D // (4 * count)
    if count != 4:
        mine_ref[j] = value[: D // 2]
        theirs_ref[j] = value[D // 2 :]
        return
    upper, lower = (
        jnp.concatenate(
            [
                value[((z * 2 + y) * 2 + c) * step : ((z * 2 + y) * 2 + c + 1) * step]
                for y in (0, 1)
                for z in range(count)
            ]
        )
        for c in (0, 1)
    )
    first = core_ref[0] == 0
    mine_ref[j] = jnp.where(first, upper, lower)
    theirs_ref[j] = jnp.where(first, lower, upper)


def enc_fwd_kernel(plain, x_ref, gain_ref, wa_ref, wf_ref, sc_ref, sr_ref, x1_ref, x2_ref, top_ref, q_ref, k_ref, v_ref, o_ref, h_ref, *wd):
    allowed = sc_ref[...] == sr_ref[...]
    stream = x_ref[...]
    normed = low(norm_parts(stream)[0] * gain_ref[0:1])
    stream = stream + attend_inside(normed, normed, wa_ref, allowed, q_ref, k_ref, v_ref, o_ref)
    x1_ref[...] = stream
    normed = low(norm_parts(stream)[0] * gain_ref[1:2])
    stream = stream + ffn_inside(normed, wf_ref, plain, h_ref, *wd)
    x2_ref[...] = stream
    top_ref[...] = norm_parts(stream)[0] * gain_ref[2:3]


def dec_self_kernel(x_ref, gain_ref, w_ref, tc_ref, tr_ref, y1_ref, q_ref, k_ref, v_ref, o_ref):
    stream = x_ref[...]
    normed = low(norm_parts(stream)[0] * gain_ref[3:4])
    branch = attend_inside(
        normed, normed, w_ref, tc_ref[...] == tr_ref[...], q_ref, k_ref, v_ref, o_ref
    )
    y1_ref[...] = stream + branch


def dec_rest_kernel(plain, y1_ref, mem_ref, gain_ref, wa_ref, wf_ref, tc_ref, sr_ref, y2_ref, y3_ref, top_ref, q_ref, k_ref, v_ref, o_ref, h_ref, *wd):
    stream = y1_ref[...]
    normed = low(norm_parts(stream)[0] * gain_ref[4:5])
    memory = low(mem_ref[...])
    stream = stream + attend_inside(
        normed, memory, wa_ref, tc_ref[...] == sr_ref[...], q_ref, k_ref, v_ref, o_ref
    )
    y2_ref[...] = stream
    normed = low(norm_parts(stream)[0] * gain_ref[5:6])
    stream = stream + ffn_inside(normed, wf_ref, plain, h_ref, *wd)
    y3_ref[...] = stream
    top_ref[...] = norm_parts(stream)[0] * gain_ref[6:7]


def forward_kernel(plain, x_ref, y_ref, gain_ref, wa0, wf0, wa1, wa2, wf1, sc_ref, sr_ref, tc_ref, tr_ref, *refs):
    enc, self_part, rest, wd = (refs[:8], refs[8:13], refs[13:21], refs[21:])
    dec_self_kernel(y_ref, gain_ref, wa1, tc_ref, tr_ref, *self_part)
    enc_fwd_kernel(plain, x_ref, gain_ref, wa0, wf0, sc_ref, sr_ref, *enc, *wd)
    dec_rest_kernel(
        plain, self_part[0], enc[2], gain_ref, wa2, wf1, tc_ref, sr_ref, *rest, *wd
    )


def store_down(core_ref, mine_ref, theirs_ref, j, value):
    if core_ref.shape[0] != 4:
        store_split(core_ref, mine_ref, theirs_ref, 4 + j, value)
        return
    value = low(value)
    first = core_ref[0] == 0
    rows = D // 16
    for y in (0, 1):
        for part in range(4):
            upper, lower = (
                value[start : start + rows]
                for start in ((y * 2 + c) * 4 * rows + part * rows for c in (0, 1))
            )
            to = slice((y * 4 + j) * rows, (y * 4 + j + 1) * rows)
            mine_ref[4 + part, to] = jnp.where(first, upper, lower)
            theirs_ref[4 + part, to] = jnp.where(first, lower, upper)


def ffn_back_kernel(place, plain, grad_ref, end_ref, mid_ref, h_ref, gain_ref, w_ref, core_ref, out_ref, mine_ref, theirs_ref, dg_ref, *wd):
    grad_stream, end_gain = norm_back(grad_ref[...], end_ref[...], gain_ref[place + 1 : place + 2])
    grad_low = low(grad_stream)
    gain = gain_ref[place : place + 1]
    normed = low(norm_parts(mid_ref[...])[0] * gain)
    total = None
    down = down_blocks(w_ref, plain, *(wd or (None,)))
    for j in range(4):
        hidden = h_ref[j]
        bend, half = gelu_parts(hidden)
        store_down(core_ref, mine_ref, theirs_ref, j, dot_left(low(hidden * half), grad_low))
        slope = half + 0.5 * hidden * (1.0 - bend * bend) * GELU_A * (
            1.0 + 3.0 * GELU_B * hidden * hidden
        )
        grad_hidden = low(dot_right(grad_low, down[j]) * slope)
        store_split(core_ref, mine_ref, theirs_ref, j, dot_left(normed, grad_hidden))
        part = dot_right(grad_hidden, w_ref[j])
        total = part if total is None else total + part
    extra, mid_gain = norm_back(total, mid_ref[...], gain)
    out_ref[...] = grad_stream + extra
    dg_ref[...] = jnp.concatenate([mid_gain, end_gain], axis=0)


def attn_back_inside(grad_low, normed, memory, refs, w, allowed, dw_refs, scratch):
    q_ref, k_ref, v_ref, o_ref = refs
    do_ref, dq_ref, dk_ref, dv_ref = scratch
    store_split(*dw_refs, 3, dot_left(o_ref[...], grad_low))
    do_ref[...] = low(dot_right(grad_low, w[3]))
    first, keeps = lane_halves(jnp.bfloat16)
    for tile in range(0, D, 2 * HDIM):
        lanes = slice(tile, tile + 2 * HDIM)
        query, keys, values, grad_mixed = (
            ref[:, lanes] for ref in (q_ref, k_ref, v_ref, do_ref)
        )
        found = []
        for keep in keeps:
            probs = softmax_of(query * keep, keys, allowed)
            grad_probs = dot_right(grad_mixed * keep, values)
            inner = jnp.sum(probs * grad_probs, axis=-1, keepdims=True)
            grad_scores = low(probs * (grad_probs - inner))
            found.append(
                (
                    dot(grad_scores, keys),
                    dot_left(grad_scores, query),
                    dot_left(low(probs), grad_mixed),
                )
            )
        dq_ref[:, lanes] = low(jnp.where(first, found[0][0], found[1][0]) * SCALE)
        dk_ref[:, lanes] = low(jnp.where(first, found[0][1], found[1][1]) * SCALE)
        dv_ref[:, lanes] = low(jnp.where(first, found[0][2], found[1][2]))
    store_split(*dw_refs, 0, dot_left(normed, dq_ref[...]))
    store_split(*dw_refs, 1, dot_left(memory, dk_ref[...]))
    store_split(*dw_refs, 2, dot_left(memory, dv_ref[...]))
    grad_query = dot_right(dq_ref[...], w[0])
    grad_memory = dot_right(dk_ref[...], w[1]) + dot_right(dv_ref[...], w[2])
    return grad_query, grad_memory


def self_back_kernel(place, grad_ref, x_ref, q_ref, k_ref, v_ref, o_ref, gain_ref, w_ref, sc_ref, sr_ref, core_ref, held_ref, kept_ref, out_ref, mine_ref, theirs_ref, dg_ref, *scratch):
    gain = gain_ref[place : place + 1]
    normed = low(norm_parts(x_ref[...])[0] * gain)
    grad_query, grad_memory = attn_back_inside(
        low(grad_ref[...]), normed, normed, (q_ref, k_ref, v_ref, o_ref), w_ref,
        sc_ref[...] == sr_ref[...], (core_ref, mine_ref, theirs_ref), scratch,
    )
    extra, dg_ref[...] = norm_back(grad_query + grad_memory, x_ref[...], gain)
    out_ref[...] = grad_ref[...] + extra


def cross_back_kernel(place, grad_ref, x_ref, mem_ref, q_ref, k_ref, v_ref, o_ref, gain_ref, w_ref, sc_ref, sr_ref, core_ref, held_ref, kept_ref, out_ref, dmem_ref, mine_ref, theirs_ref, dg_ref, *scratch):
    gain = gain_ref[place : place + 1]
    normed = low(norm_parts(x_ref[...])[0] * gain)
    grad_query, dmem_ref[...] = attn_back_inside(
        low(grad_ref[...]), normed, low(mem_ref[...]), (q_ref, k_ref, v_ref, o_ref), w_ref,
        sc_ref[...] == sr_ref[...], (core_ref, mine_ref, theirs_ref), scratch,
    )
    extra, dg_ref[...] = norm_back(grad_query, x_ref[...], gain)
    out_ref[...] = grad_ref[...] + extra


def dec_back_kernel(plain, grad_ref, y0_ref, y1_ref, y2_ref, y3_ref, mem_ref, h_ref, *refs):
    cross, own, refs = (refs[:4], refs[4:8], refs[8:])
    gain_ref, wf, wa2, wa1, tc_ref, tr_ref, sr_ref, core_ref, *refs = refs
    out_ref, dmem_ref, mine_ref, theirs_ref, dg_self, dg_cross, dg_ffn, *scratch = refs
    first, second = (scratch[-1].at[pl.ds(k * ROW, ROW)] for k in (0, 1))
    parts = [
        (mine_ref.at[pl.ds(start, size)], theirs_ref.at[pl.ds(start, size)])
        for start, size in ((0, 4), (4, 4), (8, 8))
    ]
    ffn_back_kernel(
        5, plain, grad_ref, y3_ref, y2_ref, h_ref, gain_ref, wf, core_ref, first, *parts[2],
        dg_ffn, scratch[4],
    )
    cross_back_kernel(
        4, first, y1_ref, mem_ref, *cross, gain_ref, wa2, tc_ref, sr_ref, core_ref, None, None,
        second, dmem_ref, *parts[1], dg_cross, *scratch[:4],
    )
    self_back_kernel(
        3, second, y0_ref, *own, gain_ref, wa1, tc_ref, tr_ref, core_ref, None, None,
        out_ref, *parts[0], dg_self, *scratch[:4],
    )


def ids_along(first_ref, j, count, dim):
    shape = (1, count) if dim else (count, 1)
    return first_ref[j] + lax.broadcasted_iota(jnp.int32, shape, dim)


def head_fwd_kernel(top_ref, goal_ref, first_ref, *refs):
    blocks, (peak_ref, total_ref, pick_ref) = (refs[:4], refs[4:])
    peak_ref[...] = jnp.full(peak_ref.shape, NEGATIVE, jnp.float32)
    total_ref[...] = jnp.zeros(total_ref.shape, jnp.float32)
    pick_ref[...] = jnp.zeros(pick_ref.shape, jnp.float32)
    for j, block_ref in enumerate(blocks):
        logits = dot_right(top_ref[...], block_ref[...])
        hot = goal_ref[...] == ids_along(first_ref, j, block_ref.shape[0], 1)
        pick_ref[...] += jnp.sum(jnp.where(hot, logits, 0.0), axis=1, keepdims=True)
        peak = peak_ref[...]
        higher = jnp.maximum(peak, jnp.max(logits, axis=1, keepdims=True))
        total_ref[...] = total_ref[...] * jnp.exp(peak - higher) + jnp.sum(
            jnp.exp(logits - higher), axis=1, keepdims=True
        )
        peak_ref[...] = higher


def head_back_kernel(inverse, top_ref, goal_ref, log_ref, first_ref, *refs):
    blocks, (rows_ref, *grads_out, sum_ref) = (refs[:4], refs[4:])
    for j, block_ref in enumerate(blocks):
        logits = dot_right(top_ref[...], block_ref[...])
        hot = goal_ref[...] == ids_along(first_ref, j, block_ref.shape[0], 1)
        grads = low((jnp.exp(logits - log_ref[...]) - hot.astype(jnp.float32)) * inverse)
        rows = dot(grads, block_ref[...])
        sum_ref[...] = rows if j == 0 else sum_ref[...] + rows
        grads_out[j][...] = dot_left(grads, top_ref[...])
    rows_ref[...] = low(sum_ref[...])


def spread_kernel(picks, pieces, first_ref, ids_ref, *refs):
    count = len(picks)
    rows_refs, refs = (refs[:pieces], refs[pieces:])
    for j, base_ref, out_ref in zip(picks, refs[:count], refs[count:]):
        total = base_ref[...]
        start = 0
        for rows_ref in rows_refs:
            stop = start + rows_ref.shape[0]
            hot = ids_along(first_ref, j, base_ref.shape[0], 0) == ids_ref[:, start:stop]
            total = total + dot(hot.astype(jnp.bfloat16), rows_ref[...])
            start = stop
        out_ref[...] = total.astype(out_ref.dtype)


VMEM_BYTES = 38 * 2**20
FULL = jax.ShapeDtypeStruct((ROW, D), jnp.float32)
HALF = jax.ShapeDtypeStruct((ROW, D), jnp.bfloat16)
HIDDEN = jax.ShapeDtypeStruct((4, ROW, D), jnp.float32)


def halves_of(count):
    return jax.ShapeDtypeStruct((count, D // 2, D), jnp.bfloat16)


def gains_of(count):
    return jax.ShapeDtypeStruct((count, D), jnp.float32)


def spec_of(item):
    if item is None:
        return pl.BlockSpec(memory_space=pl.ANY)
    if isinstance(item, tuple):
        array, size, index = item
        shape, place = ((size,) + array.shape[1:], index)
    else:
        shape, place = (item.shape, 0)
    if len(shape) == 1 or shape == (1, 1):
        return pl.BlockSpec(memory_space=pltpu.SMEM)
    return pl.BlockSpec(
        shape, lambda i: (place,) + (0,) * (len(shape) - 1), pipeline_mode=pl.Buffered(1)
    )


def run(kernel, outs, *operands, held=(), scratch=0, down=0, total=0, flops=0, room=VMEM_BYTES):
    arrays = [item[0] if isinstance(item, tuple) else item for item in operands]
    in_specs = [spec_of(item) for item in operands]
    shapes = [item[0] if isinstance(item, tuple) else item for item in outs]
    shapes = [jax.ShapeDtypeStruct(item.shape, item.dtype) for item in shapes]
    aliases = {}
    for array, place in held:
        aliases[len(arrays)] = place
        arrays.append(array)
        in_specs.append(spec_of(None))
    moved = sum(math.prod(x.shape) * x.dtype.itemsize for x in arrays + shapes)
    return pl.pallas_call(
        kernel,
        grid=(1,),
        out_shape=shapes,
        in_specs=in_specs,
        out_specs=[spec_of(item) for item in outs],
        input_output_aliases=aliases,
        scratch_shapes=[pltpu.VMEM((ROW, D), jnp.bfloat16)] * scratch
        + [pltpu.VMEM((4, D, D), jnp.bfloat16)] * down
        + [pltpu.VMEM((total, D), jnp.float32)] * (total > 0),
        compiler_params=pltpu.CompilerParams(vmem_limit_bytes=room),
        cost_estimate=pl.CostEstimate(flops=flops, bytes_accessed=moved, transcendentals=0),
    )(*arrays)


def spread(picks, kinds, ids, pieces, first_ids, bases):
    pieces = [piece.reshape(-1, D) for piece in pieces]
    return run(
        functools.partial(spread_kernel, picks, len(pieces)),
        [jax.ShapeDtypeStruct(base.shape, kind) for base, kind in zip(bases, kinds)],
        first_ids, ids[None], *pieces, *bases,
        flops=2 * len(picks) * ids.shape[0] * D * bases[0].shape[0],
    )


def pack_attn(project, output):
    width = output.shape[1]
    return jnp.stack([project[:, j * width : (j + 1) * width] for j in range(3)] + [output])


def pack_ffn(expand, reduce):
    rows, width = (expand.shape[0], reduce.shape[1])
    up = [expand[:, j * width : (j + 1) * width] for j in range(4)]
    return jnp.concatenate([jnp.stack(up), reduce.reshape(4, rows, width)])


def down_in_order(pack, count):
    parts = pack[4:8].reshape(4, count, -1, D).transpose(1, 0, 2, 3).reshape(4, D, D)
    return jnp.concatenate([pack[:4], parts])


def down_in_packs(grads, count):
    parts = grads[4:8].reshape(count, 4, -1, D).transpose(1, 0, 2, 3).reshape(4, D, D)
    return jnp.concatenate([grads[:4], parts])


def update_kernel(boosts, scalar_ref, dec_ref, enc_ref, *refs):
    factor = scalar_ref[0]
    packs = ((enc_ref, 8, 0), (dec_ref, 0, 8), (dec_ref, 4, None))
    rate = RATE_SCALE * math.sqrt(NPARAM / D) / CLIP

    def write(which, place, grad):
        weight, moment, average = (refs[3 * which + k][place] for k in range(3))
        outs = refs[12 + 4 * which : 16 + 4 * which]
        clipped = grad * factor
        moment = MOMENTUM * moment + clipped
        weight = weight - boosts[which] * rate * (clipped + MOMENTUM * moment)
        outs[0][place] = weight
        outs[1][place] = moment
        outs[2][place] = KEEP * average + (1.0 - KEEP) * weight
        outs[3][place] = low(weight)

    rows = enc_ref.shape[1]
    for layer, (pack_ref, attn, ffn) in enumerate(packs):
        for j in range(3):
            write(0, (layer, slice(None), slice(j * D, (j + 1) * D)), pack_ref[attn + j])
        write(1, (layer,), pack_ref[attn + 3])
        if ffn is None:
            continue
        for j in range(4):
            write(2, (layer, slice(None), slice(j * D, (j + 1) * D)), pack_ref[ffn + j])
            write(3, (layer, slice(j * rows, (j + 1) * rows)), pack_ref[ffn + 4 + j])


def shards(
    src_tokens,
    tgt_tokens,
    src_segments,
    tgt_lengths,
    mask_order,
    attn_project,
    attn_output,
    ffn_expand,
    ffn_reduce,
    norm_gains,
    length_table,
    embedding,
    momentum_attn_project,
    momentum_attn_output,
    momentum_ffn_expand,
    momentum_ffn_reduce,
    momentum_norm_gains,
    momentum_length_table,
    momentum_embedding,
    average_attn_project,
    average_attn_output,
    average_ffn_expand,
    average_ffn_reduce,
    average_norm_gains,
    average_length_table,
    average_embedding,
):
    masters = (
        attn_project,
        attn_output,
        ffn_expand,
        ffn_reduce,
        norm_gains,
        length_table,
        embedding,
    )
    moments = (
        momentum_attn_project,
        momentum_attn_output,
        momentum_ffn_expand,
        momentum_ffn_reduce,
        momentum_norm_gains,
        momentum_length_table,
        momentum_embedding,
    )
    averages = (
        average_attn_project,
        average_attn_output,
        average_ffn_expand,
        average_ffn_reduce,
        average_norm_gains,
        average_length_table,
        average_embedding,
    )
    count_z = lax.axis_size("z")
    here, side, core, half = (
        lax.axis_index("z"),
        lax.axis_index("y"),
        lax.axis_index("core"),
        lax.axis_index("vocab"),
    )
    rows_here = src_tokens.shape[0]
    count_dp = count_z * 4
    inverse = 1.0 / (SENTS * rows_here * count_dp)
    source, target, segments, lengths, order = (
        lax.dynamic_index_in_dim(array, half, 0, False)
        for array in (src_tokens, tgt_tokens, src_segments, tgt_lengths, mask_order)
    )
    shuffled = target[order]
    bounds = jnp.cumsum(lengths)
    tsegs = jnp.sum((order[:, None] >= bounds[None, :]).astype(jnp.int32), axis=1)
    position = sinusoid(ROW, D)
    dec_position = position[order]

    own_rows = low(embedding)
    shard = own_rows.shape[0]
    far_rows = swap(own_rows, "y")
    near = (own_rows, swap(own_rows, "core"))
    place = half * count_dp + here * 4
    firsts = [
        (place + at_side * 2 + at_core) * shard
        for at_side in (side, 1 - side)
        for at_core in (core, 1 - core)
    ]
    first_ids = jnp.stack(firsts).astype(jnp.int32)
    offsets = jnp.arange(shard, dtype=jnp.int32)

    few = ROW - MASKED + 16
    extra = jnp.where(jnp.arange(16) == 0, MASK_TOKEN, -1).astype(jnp.int32)
    group = count_z * 2
    numbers = jnp.concatenate([source, shuffled, extra])
    numbers = lax.all_to_all(
        jnp.broadcast_to(numbers[None], (group, 2 * ROW + 16)), ("z", "vocab"), 0, 0, tiled=True
    )
    numbers = turn(numbers.reshape(count_z, 2, -1)).reshape(group, -1)
    src_ids = numbers[:, :ROW].reshape(-1)
    goal_ids = numbers[:, ROW : ROW + MASKED].reshape(count_z, 2, MASKED)
    goal_ids = goal_ids.transpose(1, 0, 2).reshape(-1)
    dec_ids = numbers[:, ROW + MASKED :].reshape(-1)

    def look_up(tokens, blocks, starts):
        return sum(
            dot(low(tokens[:, None] == (offsets + start)[None, :]), rows)
            for rows, start in zip(blocks, starts)
        )

    near_src, near_dec = (look_up(ids, near, firsts[:2]) for ids in (src_ids, dec_ids))
    far_rows, near_src, near_dec = lax.optimization_barrier((far_rows, near_src, near_dec))
    away = (far_rows, swap(far_rows, "core"))
    src_rows, dec_rows = (
        low(found + look_up(ids, away, firsts[2:])).reshape(count_z, 2, -1, D)
        for ids, found in ((src_ids, near_src), (dec_ids, near_dec))
    )
    table_blocks = near + away

    blanks = jnp.zeros((1, length_table.shape[1], D - LCLS - 7), jnp.bfloat16)
    misc = jnp.concatenate([low(length_table).T[None], low(norm_gains).T[None], blanks], axis=2)
    pack = gather_weight(
        jnp.concatenate(
            [
                low(pack_ffn(ffn_expand[0], ffn_reduce[0])),
                low(pack_ffn(ffn_expand[1], ffn_reduce[1])),
                low(pack_attn(attn_project[0], attn_output[0])),
                low(pack_attn(attn_project[1], attn_output[1])),
                low(pack_attn(attn_project[2], attn_output[2])),
                misc,
            ]
        )
    )
    plain = count_z != 4
    enc_ffn, dec_ffn = ((pack, 8, 0), (pack, 8, 1))
    if plain:
        enc_ffn = down_in_order(pack[:8], count_dp)
        dec_ffn = down_in_order(pack[8:16], count_dp)
    table = pack[28, :, :LCLS].T
    gain = pack[28, :, LCLS : LCLS + 7].T.astype(jnp.float32)
    scale_in = math.sqrt(D)
    class_ids = jnp.arange(LCLS, dtype=jnp.int32)
    sentence_ids = jnp.arange(SENTS, dtype=jnp.int32)

    src_part = add_vocab(src_rows)
    dec_part = scatter_line(dec_rows)
    src_part, dec_part = lax.optimization_barrier((src_part, dec_part))
    src_emb = scatter_line(src_part)
    dec_rows = add_vocab(dec_part)
    dec_emb = jnp.concatenate(
        [
            jnp.broadcast_to(dec_rows[ROW - MASKED][None], (MASKED, D)),
            dec_rows[: ROW - MASKED],
        ]
    )
    src_column, src_row = (segments[:, None], segments[None, :])
    tgt_column, tgt_row = (tsegs[:, None], tsegs[None, :])
    mega = 10**6
    x0 = scale_in * src_emb + position
    y0 = scale_in * dec_emb + dec_position
    kept = [HALF] * 4
    found = run(
        functools.partial(forward_kernel, plain),
        [FULL] * 3 + kept + [HIDDEN, FULL] + kept + [FULL] * 3 + kept + [HIDDEN],
        x0, y0, gain, (pack, 4, 4), enc_ffn, (pack, 4, 5), (pack, 4, 6), dec_ffn,
        src_column, src_row, tgt_column, tgt_row, down=1, flops=4300 * mega, room=52 * 2**20,
    )
    x1, x2, enc_top, *enc_attn_kept, enc_hidden = found[:8]
    y1, *self_kept = found[8:13]
    y2, y3, dec_top, *cross_kept, dec_hidden = found[13:]

    tops = gather_small(low(dec_top[:MASKED]))
    many = tops.shape[0]

    def rows_of(kind):
        return jax.ShapeDtypeStruct((shard, D), kind)

    column = jax.ShapeDtypeStruct((many, 1), jnp.float32)
    goal_column = goal_ids[:, None]
    peak, total, picked = run(
        head_fwd_kernel, (column, column, column),
        tops, goal_column, first_ids, *table_blocks, flops=8 * many * D * shard,
    )
    totals = jnp.stack([turn(part.reshape(2, count_z, MASKED).swapaxes(0, 1)) for part in (peak, total)])
    member = (segments[None, :] == sentence_ids[:, None]).astype(jnp.float32)
    members = jnp.sum(member, axis=1, keepdims=True)
    pooled_low = low(jnp.dot(member, enc_top, precision=HIGHEST) / members)
    length_logits = jnp.einsum("sd,cd->sc", pooled_low, table, preferred_element_type=jnp.float32)
    length_total = jax.nn.logsumexp(length_logits, axis=1)
    class_hot = (lengths[:, None] - 1 == class_ids[None, :]).astype(jnp.float32)
    length_loss = length_total - jnp.sum(length_logits * class_hot, axis=1)
    grad_length = low(
        (jnp.exp(length_logits - length_total[:, None]) - class_hot) * (LENGTH_WEIGHT * inverse)
    )
    grad_table = jnp.einsum("sc,sd->dc", grad_length, pooled_low, preferred_element_type=jnp.float32)
    grad_pooled = jnp.einsum("sc,cd->sd", grad_length, table, preferred_element_type=jnp.float32)
    grad_enc = jnp.dot(member.T, grad_pooled / members, precision=HIGHEST)

    totals, grad_enc, grad_table, length_loss = lax.optimization_barrier(
        (totals, grad_enc, grad_table, length_loss)
    )
    totals = join_line(butterfly(totals, join_totals, ("vocab",)))
    log_total = turn(totals[0] + jnp.log(totals[1])).swapaxes(0, 1).reshape(-1)
    grad_rows, *grad_blocks = run(
        functools.partial(head_back_kernel, inverse),
        [jax.ShapeDtypeStruct((many, D), jnp.bfloat16)] + [rows_of(jnp.float32)] * 4,
        tops, goal_column, log_total[:, None], first_ids, *table_blocks,
        total=many, flops=24 * many * D * shard,
    )
    grad_rows = scatter_small(grad_rows.reshape(2, count_z, MASKED, D))
    grad_top = jnp.concatenate([grad_rows, jnp.zeros((ROW - MASKED, D), jnp.float32)])

    loss_local = jnp.sum(log_total[:MASKED]) - jnp.sum(picked) + LENGTH_WEIGHT * jnp.sum(length_loss)
    core_only = jnp.full((count_z,), core, jnp.int32)
    dec_stream, memory_grad, mine_dec, theirs_dec, self_gain, cross_gain, dec_ffn_gain = run(
        functools.partial(dec_back_kernel, plain),
        (FULL, FULL, halves_of(16), halves_of(16), gains_of(1), gains_of(1), gains_of(2)),
        grad_top, y0, y1, y2, y3, enc_top, dec_hidden, *cross_kept, *self_kept, gain,
        dec_ffn, (pack, 4, 6), (pack, 4, 5), tgt_column, tgt_row, src_row, core_only,
        scratch=4, down=1, total=2 * ROW, flops=5200 * mega, room=48 * 2**20,
    )
    sent = wide(low(scale_in * dec_stream))
    blank_sum = jnp.sum(sent[:MASKED], axis=0, keepdims=True)
    blank_high = low(blank_sum)
    blank_rest = low(blank_sum - wide(blank_high))
    sent = jnp.concatenate(
        [low(sent[MASKED:]), blank_high, blank_rest, jnp.zeros((14, D), jnp.bfloat16)]
    )
    again = jnp.where(jnp.arange(few) == ROW - MASKED + 1, MASK_TOKEN, 0).astype(jnp.int32)
    back_ids = jnp.where(again[None] > 0, again[None], dec_ids.reshape(-1, few)).reshape(-1)
    hold = lax.optimization_barrier
    if plain:
        whole = jnp.concatenate([mine_dec, theirs_dec], axis=1)
        whole = jnp.concatenate([whole[:8], down_in_packs(whole[8:], count_dp)])
        mine_dec, theirs_dec = jnp.split(whole, 2, axis=1)
    mine_dec, theirs_dec = swap_core(mine_dec, theirs_dec)
    dec_pair = pair_vocab(sent)
    grad_stream, mine_enc, theirs_enc, enc_ffn_gain = run(
        functools.partial(ffn_back_kernel, 1, plain),
        (FULL, (halves_of(13), 8, 0), (halves_of(13), 8, 0), gains_of(2)),
        grad_enc + memory_grad, x2, x1, enc_hidden, gain, enc_ffn, core_only,
        down=1, flops=2200 * mega,
    )
    grad_stream, dec_pair, mine_dec, theirs_dec = hold(
        (grad_stream, dec_pair, mine_dec, theirs_dec)
    )
    mine_dec, theirs_dec = add_vocab_parts(mine_dec, theirs_dec)
    dec_near = ring_first(dec_pair)
    enc_stream, mine_enc, theirs_enc, enc_attn_gain = run(
        functools.partial(self_back_kernel, 0),
        (FULL, (halves_of(13), 4, 2), (halves_of(13), 4, 2), gains_of(1)),
        grad_stream, x0, *enc_attn_kept, gain, (pack, 4, 4), src_column, src_row,
        core_only, held=((mine_enc, 1), (theirs_enc, 2)), scratch=4, flops=1500 * mega,
    )
    grad_gain = jnp.concatenate(
        [enc_attn_gain, enc_ffn_gain, self_gain, cross_gain, dec_ffn_gain]
    ).T
    grad_misc = jnp.concatenate(
        [grad_table, grad_gain, jnp.zeros((D, D - LCLS - 7), jnp.float32)], axis=1
    )
    misc_parts = by_core(low(grad_misc)[None])
    if count_z != 4:
        misc_parts = jnp.split(low(grad_misc)[None], 2, axis=1)
    mine_enc, theirs_enc = (
        lax.dynamic_update_slice(part, misc_part, (12, 0, 0))
        for part, misc_part in zip((mine_enc, theirs_enc), misc_parts)
    )
    if plain:
        whole = jnp.concatenate([mine_enc, theirs_enc], axis=1)
        whole = jnp.concatenate([down_in_packs(whole[:8], count_dp), whole[8:]])
        mine_enc, theirs_enc = jnp.split(whole, 2, axis=1)
    mine_enc, theirs_enc = swap_core(mine_enc, theirs_enc)
    src_pair = pair_vocab(low(scale_in * enc_stream))
    dec_near, mine_enc, theirs_enc, src_pair, mine_dec, theirs_dec = hold(
        (dec_near, mine_enc, theirs_enc, src_pair, mine_dec, theirs_dec)
    )
    mine_enc, theirs_enc = add_side_parts(mine_enc, theirs_enc)
    dec_sent = ring_second(dec_pair, *dec_near)
    mine_enc, theirs_enc, dec_sent, src_pair, mine_dec, theirs_dec = hold(
        (mine_enc, theirs_enc, dec_sent, src_pair, mine_dec, theirs_dec)
    )
    theirs_dec = swap(theirs_dec, "vocab")
    theirs_enc = swap(theirs_enc, "y")
    src_near = ring_first(src_pair)
    grad_blocks = spread(
        (0, 1, 2, 3), [jnp.float32] * 4, back_ids, dec_sent, first_ids, grad_blocks
    )
    src_near, grad_blocks = hold((src_near, grad_blocks))
    src_sent = ring_second(src_pair, *src_near)
    mine_dec, theirs_dec, mine_enc, theirs_enc, src_sent, grad_blocks = hold(
        (mine_dec, theirs_dec, mine_enc, theirs_enc, src_sent, grad_blocks)
    )
    mine_dec, theirs_dec = add_side_parts(mine_dec, theirs_dec)
    mine_dec, theirs_dec, src_sent = hold((mine_dec, theirs_dec, src_sent))
    theirs_dec = swap(theirs_dec, "y")
    enc_parts = line_parts(mine_enc, theirs_enc)
    enc_far = line_first(enc_parts)
    kinds = (jnp.float32, jnp.bfloat16)
    far_chip, far_sent = spread((2, 3), kinds, src_ids, src_sent, first_ids, grad_blocks[2:])
    far_back = swap(far_sent, "core")
    near_chip, near_sent = spread((0, 1), kinds, src_ids, src_sent, first_ids, grad_blocks[:2])
    near_back = swap(near_sent, "core")
    mine_dec, theirs_dec, far_back, near_back, enc_parts, enc_far = hold(
        (mine_dec, theirs_dec, far_back, near_back, enc_parts, enc_far)
    )
    far_chip = swap(low(far_chip + wide(far_back)), "y")
    dec_parts = line_parts(mine_dec, theirs_dec)
    dec_far = line_first(dec_parts)
    enc_line = line_second(enc_parts, enc_far)
    enc_line, dec_parts, dec_far, far_chip = hold((enc_line, dec_parts, dec_far, far_chip))
    dec_line = line_second(dec_parts, dec_far)
    sum_enc, enc_square = add_vocab_last(enc_line)
    dec_line, sum_enc, far_chip = hold((dec_line, sum_enc, far_chip))
    sum_dec, dec_square = join_vocab(dec_line)
    grad_embed = near_chip + wide(near_back) + wide(far_chip)
    layer_squares = dec_square + enc_square
    table_squares = jnp.sum(grad_embed * grad_embed)
    vocab_count = lax.axis_size("vocab")
    misc_sum = sum_enc[12]
    misc_sums = (misc_sum[:, LCLS : LCLS + 7], misc_sum[:, :LCLS])
    layer_squares, misc_sums = lax.optimization_barrier((layer_squares, misc_sums))
    totals = butterfly(
        jnp.stack([layer_squares / vocab_count + table_squares, loss_local]),
        jnp.add,
        ("core", "vocab", "y", "z"),
    )
    squares, loss_sum = (totals[0], totals[1])
    grad_norm = jnp.sqrt(squares)
    factor = jnp.minimum(1.0, CLIP / grad_norm)
    rate = RATE_SCALE * math.sqrt(NPARAM / D) / CLIP
    layers = [
        item for k in range(4) for item in (masters[k], moments[k], averages[k])
    ]
    kinds = (jnp.float32, jnp.float32, jnp.float32, jnp.bfloat16)
    updated = run(
        functools.partial(update_kernel, RATE_FACTORS[:4]),
        [jax.ShapeDtypeStruct(masters[k].shape, kind) for k in range(4) for kind in kinds],
        factor[None], sum_dec, sum_enc, *layers,
    )
    results = [tuple(updated[4 * k : 4 * k + 4]) for k in range(4)]
    for k, grad in ((4, misc_sums[0]), (5, misc_sums[1])):
        clipped = grad * factor
        moment = MOMENTUM * moments[k].T + clipped
        weight = masters[k].T - RATE_FACTORS[k] * rate * (clipped + MOMENTUM * moment)
        average = KEEP * averages[k].T + (1.0 - KEEP) * weight
        results.append((weight.T, moment.T, average.T, low(weight).T))
    results.append(
        update_rows(
            RATE_FACTORS[6], factor, near_chip, near_back, far_chip, masters[6], moments[6],
            averages[6],
        )
    )
    return (loss_sum, grad_norm) + tuple(result[k] for k in range(4) for result in results)


def solution(mesh):
    vocab = mesh.shape["vocab"]
    grid = Mesh(mesh.devices.reshape(-1, 2, 2, vocab), ("z", "y", "core", "vocab"))
    dp = ("z", "y", "core")
    return jax.shard_map(
        shards,
        mesh=grid,
        in_specs=(
            P(dp, None),
            P(dp, None),
            P(dp, None),
            P(dp, None),
            P(dp, None),
            P(None, dp, None),
            P(None, dp, None),
            P(None, dp, None),
            P(None, dp, None),
            P(None, dp),
            P(None, dp),
            P(("vocab",) + dp, None),
            P(None, dp, None),
            P(None, dp, None),
            P(None, dp, None),
            P(None, dp, None),
            P(None, dp),
            P(None, dp),
            P(("vocab",) + dp, None),
            P(None, dp, None),
            P(None, dp, None),
            P(None, dp, None),
            P(None, dp, None),
            P(None, dp),
            P(None, dp),
            P(("vocab",) + dp, None),
        ),
        out_specs=(
            P(),
            P(),
            P(None, dp, None),
            P(None, dp, None),
            P(None, dp, None),
            P(None, dp, None),
            P(None, dp),
            P(None, dp),
            P(("vocab",) + dp, None),
            P(None, dp, None),
            P(None, dp, None),
            P(None, dp, None),
            P(None, dp, None),
            P(None, dp),
            P(None, dp),
            P(("vocab",) + dp, None),
            P(None, dp, None),
            P(None, dp, None),
            P(None, dp, None),
            P(None, dp, None),
            P(None, dp),
            P(None, dp),
            P(("vocab",) + dp, None),
            P(None, dp, None),
            P(None, dp, None),
            P(None, dp, None),
            P(None, dp, None),
            P(None, dp),
            P(None, dp),
            P(("vocab",) + dp, None),
        ),
        check_vma=False,
    )
```

```python
import functools
import math

import jax
import jax.numpy as jnp
from jax import lax
from jax.experimental import pallas as pl
from jax.experimental.pallas import tpu as pltpu
from jax.sharding import Mesh
from jax.sharding import PartitionSpec as P

D = 512
HDIM = 64
LCLS = 256
ROW = 256
SENTS = 8
MASKED = 96
NPARAM = 23858688


HIGHEST = lax.Precision.HIGHEST
EPSILON = 1e-05
MASK_TOKEN = 3
MOMENTUM = 0.9
KEEP = 0.9
CLIP = 0.02
LENGTH_WEIGHT = 0.1
NEGATIVE = -1e30
RATE_SCALE = 0.25
RATE_FACTORS = (1.0, 1.0, 1.0, 1.0, 6.0, 24.0, 1.0)


def sinusoid(count, width):
    place = jnp.arange(count, dtype=jnp.float32)[:, None]
    index = jnp.arange(width // 2, dtype=jnp.float32)[None, :]
    angle = place * jnp.exp(-math.log(10000.0) * 2.0 * index / width)
    return jnp.concatenate([jnp.sin(angle), jnp.cos(angle)], axis=1)


SWAP = [(0, 1), (1, 0)]


def swap(value, axis):
    return lax.ppermute(value, axis, SWAP)


def shift(value, by):
    count = lax.axis_size("z")
    return lax.ppermute(value, "z", [(i, (i + by) % count) for i in range(count)])


def low(value):
    return value.astype(jnp.bfloat16)


def wide(value):
    return value.astype(jnp.float32)


def ring_first(value):
    if lax.axis_size("z") != 4:
        return value, value
    return shift(value, 1), shift(value, -1)


def ring_second(value, below, above):
    count = lax.axis_size("z")
    if count != 4:
        whole = lax.all_gather(value, "z", axis=0)
        here = lax.axis_index("z")
        return [lax.dynamic_index_in_dim(whole, (here - k) % count, 0, False) for k in range(count)]
    half = value.shape[0] // 2
    return [value, below, shift(below[:half], 1), shift(above[half:], -1), above]


def ring_gather(value):
    return ring_second(value, *ring_first(value))


def ring_scatter(blocks):
    count = lax.axis_size("z")
    if count != 4:
        here = lax.axis_index("z")
        order = (here - jnp.arange(count)) % count
        stacked = jnp.stack([low(block) for block in blocks])
        whole = jnp.zeros_like(stacked).at[order].set(stacked)
        return wide(lax.psum_scatter(whole, "z", scatter_dimension=0))
    half = blocks[0].shape[0] // 2
    from_above = shift(low(blocks[2][:half]), -1)
    from_below = shift(low(blocks[2][half:]), 1)
    down = jnp.concatenate([wide(blocks[1][:half]) + wide(from_above), wide(blocks[1][half:])])
    up = jnp.concatenate([wide(blocks[3][:half]), wide(blocks[3][half:]) + wide(from_below)])
    from_above = shift(low(down), -1)
    from_below = shift(low(up), 1)
    return wide(blocks[0]) + wide(from_above) + wide(from_below)


def gather_weight(value):
    size = value.shape[1] // lax.axis_size("vocab")
    part = lax.dynamic_slice_in_dim(value, lax.axis_index("vocab") * size, size, 1)
    return lax.all_gather(part, ("z", "y", "core", "vocab"), axis=1, tiled=True)


def take(value, index, axis):
    return lax.dynamic_index_in_dim(value, index, axis, False)


def add_swap(value):
    mine = low(value)
    return wide(mine) + wide(swap(mine, "vocab"))


def by_core(grads):
    core = lax.axis_index("core")
    count = lax.axis_size("z")
    parts = grads.reshape(grads.shape[0], count, 2, 2, -1, grads.shape[2])
    parts = parts.transpose(0, 3, 2, 1, 4, 5).reshape(grads.shape[0], 2, -1, grads.shape[2])
    return take(parts, core, 1), take(parts, 1 - core, 1)


def swap_core(mine, theirs):
    if lax.axis_size("z") != 4:
        mine, theirs = by_core(jnp.concatenate([mine, theirs], axis=1))
    return mine, swap(theirs, "core")


def low_sum(*refs):
    return low(sum(wide(ref[...]) for ref in refs))


def sums_kernel(at_ref, *refs):
    count = len(refs) // 3
    for k in range(count):
        refs[2 * count + k][...] = low_sum(refs[2 * k], refs[2 * k + 1])


def line_kernel(at_ref, *refs):
    own, down, far, up = (low_sum(refs[2 * k], refs[2 * k + 1]) for k in range(4))
    own_ref, down_ref, far_down_ref, far_up_ref, up_ref = refs[8:]
    own_ref[...] = own
    down_ref[...] = down
    up_ref[...] = up
    half = far.shape[2] // 2
    far_down_ref[...] = far[:, :, :half]
    far_up_ref[...] = far[:, :, half:]


def pass_kernel(down_ref, up_ref, above_ref, below_ref, down_out, up_out):
    half = above_ref.shape[2]
    down_out[:, :, :half] = low(wide(down_ref[:, :, :half]) + wide(above_ref[...]))
    down_out[:, :, half:] = down_ref[:, :, half:]
    up_out[:, :, :half] = up_ref[:, :, :half]
    up_out[:, :, half:] = low(wide(up_ref[:, :, half:]) + wide(below_ref[...]))


def three_kernel(one_ref, two_ref, three_ref, out_ref):
    out_ref[...] = low_sum(one_ref, two_ref, three_ref)


def two_kernel(one_ref, two_ref, out_ref, square_ref):
    total = wide(one_ref[...]) + wide(two_ref[...])
    out_ref[...] = total
    square_ref[0, 0] = jnp.sum(total * total)


def both_kernel(at_ref, mine_ref, theirs_ref, out_ref, square_ref):
    size = mine_ref.shape[0]
    mine, theirs = (wide(mine_ref[...]), wide(theirs_ref[...]))
    out_ref[pl.ds(at_ref[0] * size, size)] = mine
    out_ref[pl.ds((1 - at_ref[0]) * size, size)] = theirs
    square_ref[0, 0] = jnp.sum(mine * mine) + jnp.sum(theirs * theirs)


def embed_kernel(boost, scalar_ref, near_ref, back_ref, far_ref, weight_ref, moment_ref, average_ref, *outs):
    rate = RATE_SCALE * math.sqrt(NPARAM / D) / CLIP
    clipped = (near_ref[...] + wide(back_ref[...]) + wide(far_ref[...])) * scalar_ref[0]
    moment = MOMENTUM * moment_ref[...] + clipped
    weight = weight_ref[...] - boost * rate * (clipped + MOMENTUM * moment)
    outs[0][...] = weight
    outs[1][...] = moment
    outs[2][...] = KEEP * average_ref[...] + (1.0 - KEEP) * weight
    outs[3][...] = low(weight)


def update_rows(boost, factor, *arrays):
    rows = arrays[-1].shape[0]
    block = pl.BlockSpec((rows, 128), lambda i: (0, i))
    kinds = (jnp.float32, jnp.float32, jnp.float32, jnp.bfloat16)
    return pl.pallas_call(
        functools.partial(embed_kernel, boost),
        grid=(D // 128,),
        out_shape=[jax.ShapeDtypeStruct((rows, D), kind) for kind in kinds],
        in_specs=[pl.BlockSpec(memory_space=pltpu.SMEM)] + [block] * len(arrays),
        out_specs=[block] * 4,
        compiler_params=pltpu.CompilerParams(vmem_limit_bytes=VMEM_BYTES),
    )(factor[None], *arrays)


def staged(kernel, at, steps, block, mine, theirs, places, outs, out_place):
    def spec(place):
        return pl.BlockSpec(block, lambda i, at: place(i, at[0]))

    def out_spec(shape):
        return pl.BlockSpec(block[:2] + shape[2:], lambda i, at: out_place(i))

    return pl.pallas_call(
        kernel,
        grid_spec=pltpu.PrefetchScalarGridSpec(
            num_scalar_prefetch=1,
            grid=(steps,),
            in_specs=[spec(place) for place in places for _ in (0, 1)],
            out_specs=[out_spec(shape) for shape in outs],
        ),
        out_shape=[jax.ShapeDtypeStruct(shape, jnp.bfloat16) for shape in outs],
        compiler_params=pltpu.CompilerParams(vmem_limit_bytes=VMEM_BYTES),
    )(at[None].astype(jnp.int32), *([mine, theirs] * len(places)))


def add_vocab_parts(mine, theirs):
    blocks, rows, columns = mine.shape
    kept = (blocks // 2, rows, columns)
    steps = 2
    return staged(
        sums_kernel, lax.axis_index("vocab"), steps, (blocks // 2 // steps, rows, columns),
        mine, theirs,
        (lambda i, at: (at * steps + i, 0, 0), lambda i, at: ((1 - at) * steps + i, 0, 0)),
        (kept, kept), lambda i: (i, 0, 0),
    )


def add_side_parts(mine, theirs):
    blocks, rows, columns = mine.shape
    kept = (blocks, rows // 2, columns)
    steps = 2
    return staged(
        sums_kernel, lax.axis_index("y"), steps, (blocks, rows // 2 // steps, columns),
        mine, theirs,
        (lambda i, at: (0, at * steps + i, 0), lambda i, at: (0, (1 - at) * steps + i, 0)),
        (kept, kept), lambda i: (0, i, 0),
    )


def line_parts(mine, theirs):
    here, count = (lax.axis_index("z"), lax.axis_size("z"))
    blocks, rows, columns = mine.shape
    if count != 4:
        return low(wide(mine) + wide(theirs)).reshape(blocks, count, -1, columns)
    part = (blocks, rows // 4, columns)
    half = (blocks, rows // 4, columns // 2)
    places = [lambda i, at, k=k: (0, lax.rem(at - k + 4, 4), 0) for k in range(4)]
    return staged(
        line_kernel, here, 1, part, mine, theirs, places, (part, part, half, half, part),
        lambda i: (0, 0, 0),
    )


def line_first(parts):
    if lax.axis_size("z") != 4:
        return parts
    return shift(parts[2], -1), shift(parts[3], 1)


def line_second(parts, near):
    if lax.axis_size("z") != 4:
        return low(lax.psum_scatter(near, "z", scatter_dimension=1))
    own, down, _, _, up = parts
    down, up = run(pass_kernel, (down, up), down, up, *near)
    return run(three_kernel, (own,), own, shift(down, -1), shift(up, 1))[0]


SQUARE = jax.ShapeDtypeStruct((1, 1), jnp.float32)


def add_vocab_last(part):
    out = jax.ShapeDtypeStruct(part.shape, jnp.float32)
    total, square = run(two_kernel, (out, SQUARE), part, swap(part, "vocab"))
    return total, square[0, 0]


def join_vocab(part):
    out = jax.ShapeDtypeStruct((2 * part.shape[0],) + part.shape[1:], jnp.float32)
    half = lax.axis_index("vocab")[None].astype(jnp.int32)
    total, square = run(both_kernel, (out, SQUARE), half, part, swap(part, "vocab"))
    return total, square[0, 0]


def after(value, *others):
    return lax.optimization_barrier((value,) + others)[0]


def pair_vocab(value):
    return jnp.stack([value, swap(value, "vocab")])


def gather_group(value):
    pieces = ring_gather(pair_vocab(value))
    return jnp.concatenate([piece.reshape(-1, value.shape[-1]) for piece in pieces])


def gather_small(value):
    count = lax.axis_size("z")
    if count == 4:
        pieces = jnp.concatenate([value] + [shift(value, k) for k in range(1, count)])
    else:
        pieces = jnp.concatenate(ring_gather(value))
    return jnp.concatenate([pieces, swap(pieces, "vocab")])


def scatter_small(parts):
    held = wide(parts[0]) + wide(swap(parts[1], "vocab"))
    count = lax.axis_size("z")
    if count != 4:
        return scatter_line(low(held))
    return held[0] + sum(wide(shift(low(held[k]), -k)) for k in range(1, count))


def add_vocab(parts):
    return parts[..., 0, :, :] + swap(low(parts[..., 1, :, :]), "vocab")


def scatter_line(parts):
    return ring_scatter([parts[k] for k in range(parts.shape[0])])


def scatter_group(parts):
    return scatter_line(add_vocab(parts))


def butterfly(value, join, axes):
    for axis in axes:
        count = lax.axis_size(axis)
        step = 1
        while step < count:
            pairs = [(i, i ^ step) for i in range(count)]
            value = join(value, lax.ppermute(value, axis, pairs))
            step *= 2
    return value


def add_four(value, axes):
    near, far, both = (
        lax.ppermute(value, axes, [(i, i ^ step) for i in range(4)]) for step in (1, 2, 3)
    )
    return (value + near) + (far + both)


def join_totals(left, right):
    peak = jnp.maximum(left[0], right[0])
    return jnp.stack(
        [peak, left[1] * jnp.exp(left[0] - peak) + right[1] * jnp.exp(right[0] - peak)]
    )


def join_line(totals):
    count = lax.axis_size("z")
    if count != 4:
        return butterfly(totals, join_totals, ("z",))
    joined = totals
    for k in range(1, count):
        joined = join_totals(joined, shift(totals, k))
    return joined


def turn(value):
    count = lax.axis_size("z")
    here, half = (lax.axis_index("z"), lax.axis_index("vocab"))
    value = jnp.where(half == 0, value, value[:, ::-1])
    backward = value[::-1]
    twice = jnp.concatenate([backward, backward])
    return lax.dynamic_slice_in_dim(twice, count - 1 - here, count, 0)


SCALE = HDIM ** (-0.5)
GELU_A = math.sqrt(2.0 / math.pi)
GELU_B = 0.044715


def dot(left, right):
    return jnp.dot(left, right, preferred_element_type=jnp.float32)


def dot_left(left, right):
    return lax.dot_general(left, right, (((0,), (0,)), ((), ())), preferred_element_type=jnp.float32)


def dot_right(left, right):
    return lax.dot_general(left, right, (((1,), (1,)), ((), ())), preferred_element_type=jnp.float32)


def norm_parts(stream):
    centred = stream - jnp.mean(stream, axis=-1, keepdims=True)
    inverse = lax.rsqrt(jnp.mean(centred * centred, axis=-1, keepdims=True) + EPSILON)
    return centred * inverse, inverse


def norm_back(grad, stream, gain):
    normed, inverse = norm_parts(stream)
    scaled = grad * gain
    through = scaled - jnp.mean(scaled, axis=-1, keepdims=True)
    through = through - normed * jnp.mean(scaled * normed, axis=-1, keepdims=True)
    return through * inverse, jnp.sum(grad * normed, axis=0, keepdims=True)


def gelu_parts(hidden):
    bend = jnp.tanh(GELU_A * (hidden + GELU_B * hidden * hidden * hidden))
    return bend, 0.5 * (1.0 + bend)


def lane_halves(kind):
    first = lax.broadcasted_iota(jnp.int32, (1, 2 * HDIM), 1) < HDIM
    ones = first.astype(jnp.float32)
    return first, (ones.astype(kind), (1.0 - ones).astype(kind))


def softmax_of(query, keys, allowed):
    scores = jnp.where(allowed, dot_right(query, keys) * SCALE, NEGATIVE)
    expo = jnp.exp(scores - jnp.max(scores, axis=-1, keepdims=True))
    return expo / jnp.sum(expo, axis=-1, keepdims=True)


def attend_inside(low_query, low_memory, w, allowed, q_ref, k_ref, v_ref, o_ref):
    q_ref[...] = low(dot(low_query, w[0]))
    k_ref[...] = low(dot(low_memory, w[1]))
    v_ref[...] = low(dot(low_memory, w[2]))
    first, keeps = lane_halves(jnp.bfloat16)
    for tile in range(0, D, 2 * HDIM):
        lanes = slice(tile, tile + 2 * HDIM)
        query, keys, values = (q_ref[:, lanes], k_ref[:, lanes], v_ref[:, lanes])
        outs = [
            dot(low(softmax_of(query * keep, keys, allowed)), values) for keep in keeps
        ]
        o_ref[:, lanes] = low(jnp.where(first, outs[0], outs[1]))
    return dot(o_ref[...], w[3])


def down_blocks(w, plain, wd_ref):
    if plain:
        return [w[4 + j] for j in range(4)]
    rows = D // 16
    for place in range(16):
        for j in range(4):
            start = (place % 4) * 4 * rows + j * rows
            wd_ref[place // 4, start : start + rows] = w[4 + j, place * rows : (place + 1) * rows]
    return [wd_ref[j] for j in range(4)]


def ffn_inside(normed, w, plain, h_ref, wd_ref):
    branch = None
    down = down_blocks(w, plain, wd_ref)
    for j in range(4):
        hidden = dot(normed, w[j])
        h_ref[j] = hidden
        part = dot(low(hidden * gelu_parts(hidden)[1]), down[j])
        branch = part if branch is None else branch + part
    return branch


def store_split(core_ref, mine_ref, theirs_ref, j, value):
    value = low(value)
    count = core_ref.shape[0]
    step = D // (4 * count)
    if count != 4:
        mine_ref[j] = value[: D // 2]
        theirs_ref[j] = value[D // 2 :]
        return
    upper, lower = (
        jnp.concatenate(
            [
                value[((z * 2 + y) * 2 + c) * step : ((z * 2 + y) * 2 + c + 1) * step]
                for y in (0, 1)
                for z in range(count)
            ]
        )
        for c in (0, 1)
    )
    first = core_ref[0] == 0
    mine_ref[j] = jnp.where(first, upper, lower)
    theirs_ref[j] = jnp.where(first, lower, upper)


def enc_fwd_kernel(plain, x_ref, gain_ref, wa_ref, wf_ref, sc_ref, sr_ref, x1_ref, x2_ref, top_ref, q_ref, k_ref, v_ref, o_ref, h_ref, *wd):
    allowed = sc_ref[...] == sr_ref[...]
    stream = x_ref[...]
    normed = low(norm_parts(stream)[0] * gain_ref[0:1])
    stream = stream + attend_inside(normed, normed, wa_ref, allowed, q_ref, k_ref, v_ref, o_ref)
    x1_ref[...] = stream
    normed = low(norm_parts(stream)[0] * gain_ref[1:2])
    stream = stream + ffn_inside(normed, wf_ref, plain, h_ref, *wd)
    x2_ref[...] = stream
    top_ref[...] = norm_parts(stream)[0] * gain_ref[2:3]


def dec_self_kernel(x_ref, gain_ref, w_ref, tc_ref, tr_ref, y1_ref, q_ref, k_ref, v_ref, o_ref):
    stream = x_ref[...]
    normed = low(norm_parts(stream)[0] * gain_ref[3:4])
    branch = attend_inside(
        normed, normed, w_ref, tc_ref[...] == tr_ref[...], q_ref, k_ref, v_ref, o_ref
    )
    y1_ref[...] = stream + branch


def dec_rest_kernel(plain, y1_ref, mem_ref, gain_ref, wa_ref, wf_ref, tc_ref, sr_ref, y2_ref, y3_ref, top_ref, q_ref, k_ref, v_ref, o_ref, h_ref, *wd):
    stream = y1_ref[...]
    normed = low(norm_parts(stream)[0] * gain_ref[4:5])
    memory = low(mem_ref[...])
    stream = stream + attend_inside(
        normed, memory, wa_ref, tc_ref[...] == sr_ref[...], q_ref, k_ref, v_ref, o_ref
    )
    y2_ref[...] = stream
    normed = low(norm_parts(stream)[0] * gain_ref[5:6])
    stream = stream + ffn_inside(normed, wf_ref, plain, h_ref, *wd)
    y3_ref[...] = stream
    top_ref[...] = norm_parts(stream)[0] * gain_ref[6:7]


def forward_kernel(plain, x_ref, y_ref, gain_ref, wa0, wf0, wa1, wa2, wf1, sc_ref, sr_ref, tc_ref, tr_ref, *refs):
    enc, self_part, rest, wd = (refs[:8], refs[8:13], refs[13:21], refs[21:])
    dec_self_kernel(y_ref, gain_ref, wa1, tc_ref, tr_ref, *self_part)
    enc_fwd_kernel(plain, x_ref, gain_ref, wa0, wf0, sc_ref, sr_ref, *enc, *wd)
    dec_rest_kernel(
        plain, self_part[0], enc[2], gain_ref, wa2, wf1, tc_ref, sr_ref, *rest, *wd
    )


def store_down(core_ref, mine_ref, theirs_ref, j, value):
    if core_ref.shape[0] != 4:
        store_split(core_ref, mine_ref, theirs_ref, 4 + j, value)
        return
    value = low(value)
    first = core_ref[0] == 0
    rows = D // 16
    for y in (0, 1):
        for part in range(4):
            upper, lower = (
                value[start : start + rows]
                for start in ((y * 2 + c) * 4 * rows + part * rows for c in (0, 1))
            )
            to = slice((y * 4 + j) * rows, (y * 4 + j + 1) * rows)
            mine_ref[4 + part, to] = jnp.where(first, upper, lower)
            theirs_ref[4 + part, to] = jnp.where(first, lower, upper)


def ffn_back_kernel(place, plain, grad_ref, end_ref, mid_ref, h_ref, gain_ref, w_ref, core_ref, out_ref, mine_ref, theirs_ref, dg_ref, *wd):
    grad_stream, end_gain = norm_back(grad_ref[...], end_ref[...], gain_ref[place + 1 : place + 2])
    grad_low = low(grad_stream)
    gain = gain_ref[place : place + 1]
    normed = low(norm_parts(mid_ref[...])[0] * gain)
    total = None
    down = down_blocks(w_ref, plain, *(wd or (None,)))
    for j in range(4):
        hidden = h_ref[j]
        bend, half = gelu_parts(hidden)
        store_down(core_ref, mine_ref, theirs_ref, j, dot_left(low(hidden * half), grad_low))
        slope = half + 0.5 * hidden * (1.0 - bend * bend) * GELU_A * (
            1.0 + 3.0 * GELU_B * hidden * hidden
        )
        grad_hidden = low(dot_right(grad_low, down[j]) * slope)
        store_split(core_ref, mine_ref, theirs_ref, j, dot_left(normed, grad_hidden))
        part = dot_right(grad_hidden, w_ref[j])
        total = part if total is None else total + part
    extra, mid_gain = norm_back(total, mid_ref[...], gain)
    out_ref[...] = grad_stream + extra
    dg_ref[...] = jnp.concatenate([mid_gain, end_gain], axis=0)


def attn_back_inside(grad_low, normed, memory, refs, w, allowed, dw_refs, scratch):
    q_ref, k_ref, v_ref, o_ref = refs
    do_ref, dq_ref, dk_ref, dv_ref = scratch
    store_split(*dw_refs, 3, dot_left(o_ref[...], grad_low))
    do_ref[...] = low(dot_right(grad_low, w[3]))
    first, keeps = lane_halves(jnp.bfloat16)
    for tile in range(0, D, 2 * HDIM):
        lanes = slice(tile, tile + 2 * HDIM)
        query, keys, values, grad_mixed = (
            ref[:, lanes] for ref in (q_ref, k_ref, v_ref, do_ref)
        )
        found = []
        for keep in keeps:
            probs = softmax_of(query * keep, keys, allowed)
            grad_probs = dot_right(grad_mixed * keep, values)
            inner = jnp.sum(probs * grad_probs, axis=-1, keepdims=True)
            grad_scores = low(probs * (grad_probs - inner))
            found.append(
                (
                    dot(grad_scores, keys),
                    dot_left(grad_scores, query),
                    dot_left(low(probs), grad_mixed),
                )
            )
        dq_ref[:, lanes] = low(jnp.where(first, found[0][0], found[1][0]) * SCALE)
        dk_ref[:, lanes] = low(jnp.where(first, found[0][1], found[1][1]) * SCALE)
        dv_ref[:, lanes] = low(jnp.where(first, found[0][2], found[1][2]))
    store_split(*dw_refs, 0, dot_left(normed, dq_ref[...]))
    store_split(*dw_refs, 1, dot_left(memory, dk_ref[...]))
    store_split(*dw_refs, 2, dot_left(memory, dv_ref[...]))
    grad_query = dot_right(dq_ref[...], w[0])
    grad_memory = dot_right(dk_ref[...], w[1]) + dot_right(dv_ref[...], w[2])
    return grad_query, grad_memory


def self_back_kernel(place, grad_ref, x_ref, q_ref, k_ref, v_ref, o_ref, gain_ref, w_ref, sc_ref, sr_ref, core_ref, held_ref, kept_ref, out_ref, mine_ref, theirs_ref, dg_ref, *scratch):
    gain = gain_ref[place : place + 1]
    normed = low(norm_parts(x_ref[...])[0] * gain)
    grad_query, grad_memory = attn_back_inside(
        low(grad_ref[...]), normed, normed, (q_ref, k_ref, v_ref, o_ref), w_ref,
        sc_ref[...] == sr_ref[...], (core_ref, mine_ref, theirs_ref), scratch,
    )
    extra, dg_ref[...] = norm_back(grad_query + grad_memory, x_ref[...], gain)
    out_ref[...] = grad_ref[...] + extra


def cross_back_kernel(place, grad_ref, x_ref, mem_ref, q_ref, k_ref, v_ref, o_ref, gain_ref, w_ref, sc_ref, sr_ref, core_ref, held_ref, kept_ref, out_ref, dmem_ref, mine_ref, theirs_ref, dg_ref, *scratch):
    gain = gain_ref[place : place + 1]
    normed = low(norm_parts(x_ref[...])[0] * gain)
    grad_query, dmem_ref[...] = attn_back_inside(
        low(grad_ref[...]), normed, low(mem_ref[...]), (q_ref, k_ref, v_ref, o_ref), w_ref,
        sc_ref[...] == sr_ref[...], (core_ref, mine_ref, theirs_ref), scratch,
    )
    extra, dg_ref[...] = norm_back(grad_query, x_ref[...], gain)
    out_ref[...] = grad_ref[...] + extra


def dec_back_kernel(plain, grad_ref, y0_ref, y1_ref, y2_ref, y3_ref, mem_ref, h_ref, *refs):
    cross, own, refs = (refs[:4], refs[4:8], refs[8:])
    gain_ref, wf, wa2, wa1, tc_ref, tr_ref, sr_ref, core_ref, *refs = refs
    out_ref, dmem_ref, mine_ref, theirs_ref, dg_self, dg_cross, dg_ffn, *scratch = refs
    first, second = (scratch[-1].at[pl.ds(k * ROW, ROW)] for k in (0, 1))
    parts = [
        (mine_ref.at[pl.ds(start, size)], theirs_ref.at[pl.ds(start, size)])
        for start, size in ((0, 4), (4, 4), (8, 8))
    ]
    ffn_back_kernel(
        5, plain, grad_ref, y3_ref, y2_ref, h_ref, gain_ref, wf, core_ref, first, *parts[2],
        dg_ffn, scratch[4],
    )
    cross_back_kernel(
        4, first, y1_ref, mem_ref, *cross, gain_ref, wa2, tc_ref, sr_ref, core_ref, None, None,
        second, dmem_ref, *parts[1], dg_cross, *scratch[:4],
    )
    self_back_kernel(
        3, second, y0_ref, *own, gain_ref, wa1, tc_ref, tr_ref, core_ref, None, None,
        out_ref, *parts[0], dg_self, *scratch[:4],
    )


def ids_along(first_ref, j, count, dim):
    shape = (1, count) if dim else (count, 1)
    return first_ref[j] + lax.broadcasted_iota(jnp.int32, shape, dim)


def head_fwd_kernel(top_ref, goal_ref, first_ref, *refs):
    blocks, (peak_ref, total_ref, pick_ref) = (refs[:4], refs[4:])
    peak_ref[...] = jnp.full(peak_ref.shape, NEGATIVE, jnp.float32)
    total_ref[...] = jnp.zeros(total_ref.shape, jnp.float32)
    pick_ref[...] = jnp.zeros(pick_ref.shape, jnp.float32)
    for j, block_ref in enumerate(blocks):
        logits = dot_right(top_ref[...], block_ref[...])
        hot = goal_ref[...] == ids_along(first_ref, j, block_ref.shape[0], 1)
        pick_ref[...] += jnp.sum(jnp.where(hot, logits, 0.0), axis=1, keepdims=True)
        peak = peak_ref[...]
        higher = jnp.maximum(peak, jnp.max(logits, axis=1, keepdims=True))
        total_ref[...] = total_ref[...] * jnp.exp(peak - higher) + jnp.sum(
            jnp.exp(logits - higher), axis=1, keepdims=True
        )
        peak_ref[...] = higher


def head_back_kernel(inverse, top_ref, goal_ref, log_ref, first_ref, *refs):
    blocks, (rows_ref, *grads_out, sum_ref) = (refs[:4], refs[4:])
    for j, block_ref in enumerate(blocks):
        logits = dot_right(top_ref[...], block_ref[...])
        hot = goal_ref[...] == ids_along(first_ref, j, block_ref.shape[0], 1)
        grads = low((jnp.exp(logits - log_ref[...]) - hot.astype(jnp.float32)) * inverse)
        rows = dot(grads, block_ref[...])
        sum_ref[...] = rows if j == 0 else sum_ref[...] + rows
        grads_out[j][...] = dot_left(grads, top_ref[...])
    rows_ref[...] = low(sum_ref[...])


def spread_kernel(picks, pieces, first_ref, ids_ref, *refs):
    count = len(picks)
    rows_refs, refs = (refs[:pieces], refs[pieces:])
    for j, base_ref, out_ref in zip(picks, refs[:count], refs[count:]):
        total = base_ref[...]
        start = 0
        for rows_ref in rows_refs:
            stop = start + rows_ref.shape[0]
            hot = ids_along(first_ref, j, base_ref.shape[0], 0) == ids_ref[:, start:stop]
            total = total + dot(hot.astype(jnp.bfloat16), rows_ref[...])
            start = stop
        out_ref[...] = total.astype(out_ref.dtype)


VMEM_BYTES = 38 * 2**20
FULL = jax.ShapeDtypeStruct((ROW, D), jnp.float32)
HALF = jax.ShapeDtypeStruct((ROW, D), jnp.bfloat16)
HIDDEN = jax.ShapeDtypeStruct((4, ROW, D), jnp.float32)


def halves_of(count):
    return jax.ShapeDtypeStruct((count, D // 2, D), jnp.bfloat16)


def gains_of(count):
    return jax.ShapeDtypeStruct((count, D), jnp.float32)


def spec_of(item):
    if item is None:
        return pl.BlockSpec(memory_space=pl.ANY)
    if isinstance(item, tuple):
        array, size, index = item
        shape, place = ((size,) + array.shape[1:], index)
    else:
        shape, place = (item.shape, 0)
    if len(shape) == 1 or shape == (1, 1):
        return pl.BlockSpec(memory_space=pltpu.SMEM)
    return pl.BlockSpec(
        shape, lambda i: (place,) + (0,) * (len(shape) - 1), pipeline_mode=pl.Buffered(1)
    )


def run(kernel, outs, *operands, held=(), scratch=0, down=0, total=0, flops=0, room=VMEM_BYTES):
    arrays = [item[0] if isinstance(item, tuple) else item for item in operands]
    in_specs = [spec_of(item) for item in operands]
    shapes = [item[0] if isinstance(item, tuple) else item for item in outs]
    shapes = [jax.ShapeDtypeStruct(item.shape, item.dtype) for item in shapes]
    aliases = {}
    for array, place in held:
        aliases[len(arrays)] = place
        arrays.append(array)
        in_specs.append(spec_of(None))
    moved = sum(math.prod(x.shape) * x.dtype.itemsize for x in arrays + shapes)
    return pl.pallas_call(
        kernel,
        grid=(1,),
        out_shape=shapes,
        in_specs=in_specs,
        out_specs=[spec_of(item) for item in outs],
        input_output_aliases=aliases,
        scratch_shapes=[pltpu.VMEM((ROW, D), jnp.bfloat16)] * scratch
        + [pltpu.VMEM((4, D, D), jnp.bfloat16)] * down
        + [pltpu.VMEM((total, D), jnp.float32)] * (total > 0),
        compiler_params=pltpu.CompilerParams(vmem_limit_bytes=room),
        cost_estimate=pl.CostEstimate(flops=flops, bytes_accessed=moved, transcendentals=0),
    )(*arrays)


def spread(picks, kinds, ids, pieces, first_ids, bases):
    pieces = [piece.reshape(-1, D) for piece in pieces]
    return run(
        functools.partial(spread_kernel, picks, len(pieces)),
        [jax.ShapeDtypeStruct(base.shape, kind) for base, kind in zip(bases, kinds)],
        first_ids, ids[None], *pieces, *bases,
        flops=2 * len(picks) * ids.shape[0] * D * bases[0].shape[0],
    )


def pack_attn(project, output):
    width = output.shape[1]
    return jnp.stack([project[:, j * width : (j + 1) * width] for j in range(3)] + [output])


def pack_ffn(expand, reduce):
    rows, width = (expand.shape[0], reduce.shape[1])
    up = [expand[:, j * width : (j + 1) * width] for j in range(4)]
    return jnp.concatenate([jnp.stack(up), reduce.reshape(4, rows, width)])


def down_in_order(pack, count):
    parts = pack[4:8].reshape(4, count, -1, D).transpose(1, 0, 2, 3).reshape(4, D, D)
    return jnp.concatenate([pack[:4], parts])


def down_in_packs(grads, count):
    parts = grads[4:8].reshape(count, 4, -1, D).transpose(1, 0, 2, 3).reshape(4, D, D)
    return jnp.concatenate([grads[:4], parts])


def update_kernel(boosts, scalar_ref, dec_ref, enc_ref, *refs):
    factor = scalar_ref[0]
    packs = ((enc_ref, 8, 0), (dec_ref, 0, 8), (dec_ref, 4, None))
    rate = RATE_SCALE * math.sqrt(NPARAM / D) / CLIP

    def write(which, place, grad):
        weight, moment, average = (refs[3 * which + k][place] for k in range(3))
        outs = refs[12 + 4 * which : 16 + 4 * which]
        clipped = grad * factor
        moment = MOMENTUM * moment + clipped
        weight = weight - boosts[which] * rate * (clipped + MOMENTUM * moment)
        outs[0][place] = weight
        outs[1][place] = moment
        outs[2][place] = KEEP * average + (1.0 - KEEP) * weight
        outs[3][place] = low(weight)

    rows = enc_ref.shape[1]
    for layer, (pack_ref, attn, ffn) in enumerate(packs):
        for j in range(3):
            write(0, (layer, slice(None), slice(j * D, (j + 1) * D)), pack_ref[attn + j])
        write(1, (layer,), pack_ref[attn + 3])
        if ffn is None:
            continue
        for j in range(4):
            write(2, (layer, slice(None), slice(j * D, (j + 1) * D)), pack_ref[ffn + j])
            write(3, (layer, slice(j * rows, (j + 1) * rows)), pack_ref[ffn + 4 + j])


def shards(
    src_tokens,
    tgt_tokens,
    src_segments,
    tgt_lengths,
    mask_order,
    attn_project,
    attn_output,
    ffn_expand,
    ffn_reduce,
    norm_gains,
    length_table,
    embedding,
    momentum_attn_project,
    momentum_attn_output,
    momentum_ffn_expand,
    momentum_ffn_reduce,
    momentum_norm_gains,
    momentum_length_table,
    momentum_embedding,
    average_attn_project,
    average_attn_output,
    average_ffn_expand,
    average_ffn_reduce,
    average_norm_gains,
    average_length_table,
    average_embedding,
):
    masters = (
        attn_project,
        attn_output,
        ffn_expand,
        ffn_reduce,
        norm_gains,
        length_table,
        embedding,
    )
    moments = (
        momentum_attn_project,
        momentum_attn_output,
        momentum_ffn_expand,
        momentum_ffn_reduce,
        momentum_norm_gains,
        momentum_length_table,
        momentum_embedding,
    )
    averages = (
        average_attn_project,
        average_attn_output,
        average_ffn_expand,
        average_ffn_reduce,
        average_norm_gains,
        average_length_table,
        average_embedding,
    )
    count_z = lax.axis_size("z")
    here, side, core, half = (
        lax.axis_index("z"),
        lax.axis_index("y"),
        lax.axis_index("core"),
        lax.axis_index("vocab"),
    )
    rows_here = src_tokens.shape[0]
    count_dp = count_z * 4
    inverse = 1.0 / (SENTS * rows_here * count_dp)
    source, target, segments, lengths, order = (
        lax.dynamic_index_in_dim(array, half, 0, False)
        for array in (src_tokens, tgt_tokens, src_segments, tgt_lengths, mask_order)
    )
    shuffled = target[order]
    bounds = jnp.cumsum(lengths)
    tsegs = jnp.sum((order[:, None] >= bounds[None, :]).astype(jnp.int32), axis=1)
    position = sinusoid(ROW, D)
    dec_position = position[order]

    own_rows = low(embedding)
    shard = own_rows.shape[0]
    far_rows = swap(own_rows, "y")
    near = (own_rows, swap(own_rows, "core"))
    place = half * count_dp + here * 4
    firsts = [
        (place + at_side * 2 + at_core) * shard
        for at_side in (side, 1 - side)
        for at_core in (core, 1 - core)
    ]
    first_ids = jnp.stack(firsts).astype(jnp.int32)
    offsets = jnp.arange(shard, dtype=jnp.int32)

    few = ROW - MASKED + 16
    extra = jnp.where(jnp.arange(16) == 0, MASK_TOKEN, -1).astype(jnp.int32)
    group = count_z * 2
    numbers = jnp.concatenate([source, shuffled, extra])
    numbers = lax.all_to_all(
        jnp.broadcast_to(numbers[None], (group, 2 * ROW + 16)), ("z", "vocab"), 0, 0, tiled=True
    )
    numbers = turn(numbers.reshape(count_z, 2, -1)).reshape(group, -1)
    src_ids = numbers[:, :ROW].reshape(-1)
    goal_ids = numbers[:, ROW : ROW + MASKED].reshape(count_z, 2, MASKED)
    goal_ids = goal_ids.transpose(1, 0, 2).reshape(-1)
    dec_ids = numbers[:, ROW + MASKED :].reshape(-1)

    def look_up(tokens, blocks, starts):
        return sum(
            dot(low(tokens[:, None] == (offsets + start)[None, :]), rows)
            for rows, start in zip(blocks, starts)
        )

    near_src, near_dec = (look_up(ids, near, firsts[:2]) for ids in (src_ids, dec_ids))
    far_rows, near_src, near_dec = lax.optimization_barrier((far_rows, near_src, near_dec))
    away = (far_rows, swap(far_rows, "core"))
    src_rows, dec_rows = (
        low(found + look_up(ids, away, firsts[2:])).reshape(count_z, 2, -1, D)
        for ids, found in ((src_ids, near_src), (dec_ids, near_dec))
    )
    table_blocks = near + away

    blanks = jnp.zeros((1, length_table.shape[1], D - LCLS - 7), jnp.bfloat16)
    misc = jnp.concatenate([low(length_table).T[None], low(norm_gains).T[None], blanks], axis=2)
    pack = gather_weight(
        jnp.concatenate(
            [
                low(pack_ffn(ffn_expand[0], ffn_reduce[0])),
                low(pack_ffn(ffn_expand[1], ffn_reduce[1])),
                low(pack_attn(attn_project[0], attn_output[0])),
                low(pack_attn(attn_project[1], attn_output[1])),
                low(pack_attn(attn_project[2], attn_output[2])),
                misc,
            ]
        )
    )
    plain = count_z != 4
    enc_ffn, dec_ffn = ((pack, 8, 0), (pack, 8, 1))
    if plain:
        enc_ffn = down_in_order(pack[:8], count_dp)
        dec_ffn = down_in_order(pack[8:16], count_dp)
    table = pack[28, :, :LCLS].T
    gain = pack[28, :, LCLS : LCLS + 7].T.astype(jnp.float32)
    scale_in = math.sqrt(D)
    class_ids = jnp.arange(LCLS, dtype=jnp.int32)
    sentence_ids = jnp.arange(SENTS, dtype=jnp.int32)

    src_part = add_vocab(src_rows)
    dec_part = scatter_line(dec_rows)
    src_part, dec_part = lax.optimization_barrier((src_part, dec_part))
    src_emb = scatter_line(src_part)
    dec_rows = add_vocab(dec_part)
    dec_emb = jnp.concatenate(
        [
            jnp.broadcast_to(dec_rows[ROW - MASKED][None], (MASKED, D)),
            dec_rows[: ROW - MASKED],
        ]
    )
    src_column, src_row = (segments[:, None], segments[None, :])
    tgt_column, tgt_row = (tsegs[:, None], tsegs[None, :])
    mega = 10**6
    x0 = scale_in * src_emb + position
    y0 = scale_in * dec_emb + dec_position
    kept = [HALF] * 4
    found = run(
        functools.partial(forward_kernel, plain),
        [FULL] * 3 + kept + [HIDDEN, FULL] + kept + [FULL] * 3 + kept + [HIDDEN],
        x0, y0, gain, (pack, 4, 4), enc_ffn, (pack, 4, 5), (pack, 4, 6), dec_ffn,
        src_column, src_row, tgt_column, tgt_row, down=1, flops=4300 * mega, room=52 * 2**20,
    )
    x1, x2, enc_top, *enc_attn_kept, enc_hidden = found[:8]
    y1, *self_kept = found[8:13]
    y2, y3, dec_top, *cross_kept, dec_hidden = found[13:]

    tops = gather_small(low(dec_top[:MASKED]))
    many = tops.shape[0]

    def rows_of(kind):
        return jax.ShapeDtypeStruct((shard, D), kind)

    column = jax.ShapeDtypeStruct((many, 1), jnp.float32)
    goal_column = goal_ids[:, None]
    peak, total, picked = run(
        head_fwd_kernel, (column, column, column),
        tops, goal_column, first_ids, *table_blocks, flops=8 * many * D * shard,
    )
    totals = jnp.stack([turn(part.reshape(2, count_z, MASKED).swapaxes(0, 1)) for part in (peak, total)])
    member = (segments[None, :] == sentence_ids[:, None]).astype(jnp.float32)
    members = jnp.sum(member, axis=1, keepdims=True)
    pooled_low = low(jnp.dot(member, enc_top, precision=HIGHEST) / members)
    length_logits = jnp.einsum("sd,cd->sc", pooled_low, table, preferred_element_type=jnp.float32)
    length_total = jax.nn.logsumexp(length_logits, axis=1)
    class_hot = (lengths[:, None] - 1 == class_ids[None, :]).astype(jnp.float32)
    length_loss = length_total - jnp.sum(length_logits * class_hot, axis=1)
    grad_length = low(
        (jnp.exp(length_logits - length_total[:, None]) - class_hot) * (LENGTH_WEIGHT * inverse)
    )
    grad_table = jnp.einsum("sc,sd->dc", grad_length, pooled_low, preferred_element_type=jnp.float32)
    grad_pooled = jnp.einsum("sc,cd->sd", grad_length, table, preferred_element_type=jnp.float32)
    grad_enc = jnp.dot(member.T, grad_pooled / members, precision=HIGHEST)

    totals, grad_enc, grad_table, length_loss = lax.optimization_barrier(
        (totals, grad_enc, grad_table, length_loss)
    )
    totals = join_line(butterfly(totals, join_totals, ("vocab",)))
    log_total = turn(totals[0] + jnp.log(totals[1])).swapaxes(0, 1).reshape(-1)
    grad_rows, *grad_blocks = run(
        functools.partial(head_back_kernel, inverse),
        [jax.ShapeDtypeStruct((many, D), jnp.bfloat16)] + [rows_of(jnp.float32)] * 4,
        tops, goal_column, log_total[:, None], first_ids, *table_blocks,
        total=many, flops=24 * many * D * shard,
    )
    grad_rows = scatter_small(grad_rows.reshape(2, count_z, MASKED, D))
    grad_top = jnp.concatenate([grad_rows, jnp.zeros((ROW - MASKED, D), jnp.float32)])

    loss_local = jnp.sum(log_total[:MASKED]) - jnp.sum(picked) + LENGTH_WEIGHT * jnp.sum(length_loss)
    core_only = jnp.full((count_z,), core, jnp.int32)
    dec_stream, memory_grad, mine_dec, theirs_dec, self_gain, cross_gain, dec_ffn_gain = run(
        functools.partial(dec_back_kernel, plain),
        (FULL, FULL, halves_of(16), halves_of(16), gains_of(1), gains_of(1), gains_of(2)),
        grad_top, y0, y1, y2, y3, enc_top, dec_hidden, *cross_kept, *self_kept, gain,
        dec_ffn, (pack, 4, 6), (pack, 4, 5), tgt_column, tgt_row, src_row, core_only,
        scratch=4, down=1, total=2 * ROW, flops=5200 * mega, room=48 * 2**20,
    )
    sent = wide(low(scale_in * dec_stream))
    blank_sum = jnp.sum(sent[:MASKED], axis=0, keepdims=True)
    blank_high = low(blank_sum)
    blank_rest = low(blank_sum - wide(blank_high))
    sent = jnp.concatenate(
        [low(sent[MASKED:]), blank_high, blank_rest, jnp.zeros((14, D), jnp.bfloat16)]
    )
    again = jnp.where(jnp.arange(few) == ROW - MASKED + 1, MASK_TOKEN, 0).astype(jnp.int32)
    back_ids = jnp.where(again[None] > 0, again[None], dec_ids.reshape(-1, few)).reshape(-1)
    hold = lax.optimization_barrier
    if plain:
        whole = jnp.concatenate([mine_dec, theirs_dec], axis=1)
        whole = jnp.concatenate([whole[:8], down_in_packs(whole[8:], count_dp)])
        mine_dec, theirs_dec = jnp.split(whole, 2, axis=1)
    mine_dec, theirs_dec = swap_core(mine_dec, theirs_dec)
    dec_pair = pair_vocab(sent)
    grad_stream, mine_enc, theirs_enc, enc_ffn_gain = run(
        functools.partial(ffn_back_kernel, 1, plain),
        (FULL, (halves_of(13), 8, 0), (halves_of(13), 8, 0), gains_of(2)),
        grad_enc + memory_grad, x2, x1, enc_hidden, gain, enc_ffn, core_only,
        down=1, flops=2200 * mega,
    )
    grad_stream, dec_pair, mine_dec, theirs_dec = hold(
        (grad_stream, dec_pair, mine_dec, theirs_dec)
    )
    mine_dec, theirs_dec = add_vocab_parts(mine_dec, theirs_dec)
    dec_near = ring_first(dec_pair)
    enc_stream, mine_enc, theirs_enc, enc_attn_gain = run(
        functools.partial(self_back_kernel, 0),
        (FULL, (halves_of(13), 4, 2), (halves_of(13), 4, 2), gains_of(1)),
        grad_stream, x0, *enc_attn_kept, gain, (pack, 4, 4), src_column, src_row,
        core_only, held=((mine_enc, 1), (theirs_enc, 2)), scratch=4, flops=1500 * mega,
    )
    grad_gain = jnp.concatenate(
        [enc_attn_gain, enc_ffn_gain, self_gain, cross_gain, dec_ffn_gain]
    ).T
    grad_misc = jnp.concatenate(
        [grad_table, grad_gain, jnp.zeros((D, D - LCLS - 7), jnp.float32)], axis=1
    )
    misc_parts = by_core(low(grad_misc)[None])
    if count_z != 4:
        misc_parts = jnp.split(low(grad_misc)[None], 2, axis=1)
    mine_enc, theirs_enc = (
        lax.dynamic_update_slice(part, misc_part, (12, 0, 0))
        for part, misc_part in zip((mine_enc, theirs_enc), misc_parts)
    )
    if plain:
        whole = jnp.concatenate([mine_enc, theirs_enc], axis=1)
        whole = jnp.concatenate([down_in_packs(whole[:8], count_dp), whole[8:]])
        mine_enc, theirs_enc = jnp.split(whole, 2, axis=1)
    mine_enc, theirs_enc = swap_core(mine_enc, theirs_enc)
    src_pair = pair_vocab(low(scale_in * enc_stream))
    dec_near, mine_enc, theirs_enc, src_pair, mine_dec, theirs_dec = hold(
        (dec_near, mine_enc, theirs_enc, src_pair, mine_dec, theirs_dec)
    )
    mine_enc, theirs_enc = add_side_parts(mine_enc, theirs_enc)
    dec_sent = ring_second(dec_pair, *dec_near)
    mine_enc, theirs_enc, dec_sent, src_pair, mine_dec, theirs_dec = hold(
        (mine_enc, theirs_enc, dec_sent, src_pair, mine_dec, theirs_dec)
    )
    theirs_dec = swap(theirs_dec, "vocab")
    theirs_enc = swap(theirs_enc, "y")
    src_near = ring_first(src_pair)
    grad_blocks = spread(
        (0, 1, 2, 3), [jnp.float32] * 4, back_ids, dec_sent, first_ids, grad_blocks
    )
    src_near, grad_blocks = hold((src_near, grad_blocks))
    src_sent = ring_second(src_pair, *src_near)
    mine_dec, theirs_dec, mine_enc, theirs_enc, src_sent, grad_blocks = hold(
        (mine_dec, theirs_dec, mine_enc, theirs_enc, src_sent, grad_blocks)
    )
    mine_dec, theirs_dec = add_side_parts(mine_dec, theirs_dec)
    mine_dec, theirs_dec, src_sent = hold((mine_dec, theirs_dec, src_sent))
    theirs_dec = swap(theirs_dec, "y")
    enc_parts = line_parts(mine_enc, theirs_enc)
    enc_far = line_first(enc_parts)
    kinds = (jnp.float32, jnp.bfloat16)
    far_chip, far_sent = spread((2, 3), kinds, src_ids, src_sent, first_ids, grad_blocks[2:])
    far_back = swap(far_sent, "core")
    near_chip, near_sent = spread((0, 1), kinds, src_ids, src_sent, first_ids, grad_blocks[:2])
    near_back = swap(near_sent, "core")
    mine_dec, theirs_dec, far_back, near_back, enc_parts, enc_far = hold(
        (mine_dec, theirs_dec, far_back, near_back, enc_parts, enc_far)
    )
    far_chip = swap(low(far_chip + wide(far_back)), "y")
    dec_parts = line_parts(mine_dec, theirs_dec)
    dec_far = line_first(dec_parts)
    enc_line = line_second(enc_parts, enc_far)
    enc_line, dec_parts, dec_far, far_chip = hold((enc_line, dec_parts, dec_far, far_chip))
    dec_line = line_second(dec_parts, dec_far)
    sum_enc, enc_square = add_vocab_last(enc_line)
    dec_line, sum_enc, far_chip = hold((dec_line, sum_enc, far_chip))
    sum_dec, dec_square = join_vocab(dec_line)
    grad_embed = near_chip + wide(near_back) + wide(far_chip)
    layer_squares = dec_square + enc_square
    table_squares = jnp.sum(grad_embed * grad_embed)
    vocab_count = lax.axis_size("vocab")
    misc_sum = sum_enc[12]
    misc_sums = (misc_sum[:, LCLS : LCLS + 7], misc_sum[:, :LCLS])
    layer_squares, misc_sums = lax.optimization_barrier((layer_squares, misc_sums))
    totals = jnp.stack([layer_squares / vocab_count + table_squares, loss_local])
    totals = butterfly(add_four(totals, ("y", "core")), jnp.add, ("vocab",))
    totals = butterfly(totals, jnp.add, ("z",)) if plain else add_four(totals, "z")
    squares, loss_sum = (totals[0], totals[1])
    grad_norm = jnp.sqrt(squares)
    factor = jnp.minimum(1.0, CLIP / grad_norm)
    rate = RATE_SCALE * math.sqrt(NPARAM / D) / CLIP
    layers = [
        item for k in range(4) for item in (masters[k], moments[k], averages[k])
    ]
    kinds = (jnp.float32, jnp.float32, jnp.float32, jnp.bfloat16)
    updated = run(
        functools.partial(update_kernel, RATE_FACTORS[:4]),
        [jax.ShapeDtypeStruct(masters[k].shape, kind) for k in range(4) for kind in kinds],
        factor[None], sum_dec, sum_enc, *layers,
    )
    results = [tuple(updated[4 * k : 4 * k + 4]) for k in range(4)]
    for k, grad in ((4, misc_sums[0]), (5, misc_sums[1])):
        clipped = grad * factor
        moment = MOMENTUM * moments[k].T + clipped
        weight = masters[k].T - RATE_FACTORS[k] * rate * (clipped + MOMENTUM * moment)
        average = KEEP * averages[k].T + (1.0 - KEEP) * weight
        results.append((weight.T, moment.T, average.T, low(weight).T))
    results.append(
        update_rows(
            RATE_FACTORS[6], factor, near_chip, near_back, far_chip, masters[6], moments[6],
            averages[6],
        )
    )
    return (loss_sum, grad_norm) + tuple(result[k] for k in range(4) for result in results)


def solution(mesh):
    vocab = mesh.shape["vocab"]
    grid = Mesh(mesh.devices.reshape(-1, 2, 2, vocab), ("z", "y", "core", "vocab"))
    dp = ("z", "y", "core")
    return jax.shard_map(
        shards,
        mesh=grid,
        in_specs=(
            P(dp, None),
            P(dp, None),
            P(dp, None),
            P(dp, None),
            P(dp, None),
            P(None, dp, None),
            P(None, dp, None),
            P(None, dp, None),
            P(None, dp, None),
            P(None, dp),
            P(None, dp),
            P(("vocab",) + dp, None),
            P(None, dp, None),
            P(None, dp, None),
            P(None, dp, None),
            P(None, dp, None),
            P(None, dp),
            P(None, dp),
            P(("vocab",) + dp, None),
            P(None, dp, None),
            P(None, dp, None),
            P(None, dp, None),
            P(None, dp, None),
            P(None, dp),
            P(None, dp),
            P(("vocab",) + dp, None),
        ),
        out_specs=(
            P(),
            P(),
            P(None, dp, None),
            P(None, dp, None),
            P(None, dp, None),
            P(None, dp, None),
            P(None, dp),
            P(None, dp),
            P(("vocab",) + dp, None),
            P(None, dp, None),
            P(None, dp, None),
            P(None, dp, None),
            P(None, dp, None),
            P(None, dp),
            P(None, dp),
            P(("vocab",) + dp, None),
            P(None, dp, None),
            P(None, dp, None),
            P(None, dp, None),
            P(None, dp, None),
            P(None, dp),
            P(None, dp),
            P(("vocab",) + dp, None),
            P(None, dp, None),
            P(None, dp, None),
            P(None, dp, None),
            P(None, dp, None),
            P(None, dp),
            P(None, dp),
            P(("vocab",) + dp, None),
        ),
        check_vma=False,
    )
```
